256 devices in a mesh: seq: 32 (over z, x), outer: 8 (over y, core).
Axes of the slice: x: 4, y: 4, z: 8, core: 2. Of those that a mesh axis runs over, the one named last changes fastest.
Arguments:
- queries: bfloat16 [65536, 1024], P(('outer', 'seq')), may hold values from -48 to 48
- keys: bfloat16 [65536, 1024], P(('outer', 'seq')), may hold values from -6 to 6
- values: bfloat16 [65536, 1024], P(('outer', 'seq')), may hold values from -6 to 6
- out_grad: bfloat16 [65536, 1024], P(('outer', 'seq')), may hold values from -6 to 6
- near_offsets: int32 [16], replicated, may hold values from 0 to 63
- far_offsets: int32 [16], replicated, may hold values from 0 to 255
Outputs:
- attn_out: bfloat16 [65536, 1024], P(('outer', 'seq'))
- query_grad: bfloat16 [65536, 1024], P(('outer', 'seq'))
- key_grad: bfloat16 [65536, 1024], P(('outer', 'seq'))
- value_grad: bfloat16 [65536, 1024], P(('outer', 'seq'))
The draws below stay inside these ranges and needn't reach their ends.
All inputs are finite; a program needn't handle non-finite values.
Results may differ from the reference program's by a relative error of at most 0.0065.
Values may be sent and summed in bfloat16 or wider, within the bound.
No kernel may reach another device: no remote copies, remote signals or barrier semaphores. Data moves between devices by JAX's collectives and lax.ppermute only.
A program may use at most 64 MiB of HBM per device.

```python
import jax
import jax.numpy as jnp
from jax import lax

HEADS = 16
HEAD_FEATURES = 64
WIDTH = 1024
TOK_DEV = 256
NEAR_RATE = 64
FAR_RATE = 256
NEAR_SEGMENT = 8192
TOKENS = 65536


def draw_queries(key, part):
    key = jax.random.fold_in(key, 11)
    base = jnp.clip(jax.random.normal(jax.random.fold_in(key, 1), (TOKENS, HEADS, HEAD_FEATURES), jnp.float32), -4.0, 4.0)
    return base.reshape(TOKENS, HEADS * HEAD_FEATURES).astype(jnp.bfloat16)


def draw_keys(key, part):
    key = jax.random.fold_in(key, 13)
    base = jnp.clip(jax.random.normal(jax.random.fold_in(key, 1), (TOKENS, HEADS, HEAD_FEATURES), jnp.float32), -5.0, 5.0)
    return base.reshape(TOKENS, HEADS * HEAD_FEATURES).astype(jnp.bfloat16)


def touch_ends(entries, key, least, top_value):
    longest = entries.shape.index(max(entries.shape))
    spots = []
    for shift in (0, 1):
        where = [jax.random.randint(jax.random.fold_in(key, axis), (), 0, length) for axis, length in enumerate(entries.shape)]
        where[longest] = (where[longest] + shift) % entries.shape[longest]
        spots.append(tuple(where))
    return entries.at[spots[0]].set(least).at[spots[1]].set(top_value)


def shard_levels(own_key, dims, cuts, smallest, top_value):
    loudness, own = 1.0, jax.random.fold_in(own_key, 6)
    for axis_at, blocks in cuts:
        steps = jnp.exp(jax.random.uniform(jax.random.fold_in(own, axis_at), (blocks,), jnp.float32, smallest / len(cuts), top_value / len(cuts)))
        loudness = loudness * jnp.repeat(steps, dims[axis_at] // blocks).reshape([-1 if axis == axis_at else 1 for axis in range(len(dims))])
    return loudness


def noise(own_key, shape, scale, bound, shards=(), kind=jnp.bfloat16):
    array = jax.random.normal(own_key, shape, jnp.float32) * scale
    if len(shards) > 0:
        array = shard_levels(own_key, shape, shards, -0.22, 0.18) * array
    return jnp.clip(array, min=-bound, max=bound).astype(kind)


def setup_inputs(seed: int = 0) -> dict:
    splits = jax.random.split(jax.random.key(seed), 7)
    return {
        "queries": draw_queries(jax.random.fold_in(splits[6], 71), 0),
        "keys": draw_keys(jax.random.fold_in(splits[6], 71), 0),
        "values": noise(splits[2], (TOKENS, WIDTH), 1.0, 6.0, ((0, 256),)),
        "out_grad": noise(splits[3], (TOKENS, WIDTH), 1.0, 6.0, ((0, 256),)),
        "near_offsets": touch_ends(jax.random.randint(splits[4], (HEADS,), 0, NEAR_RATE), jax.random.fold_in(splits[4], 1), 0, NEAR_RATE - 1).astype(jnp.int32),
        "far_offsets": touch_ends(jax.random.randint(splits[5], (HEADS,), 0, FAR_RATE), jax.random.fold_in(splits[5], 1), 0, FAR_RATE - 1).astype(jnp.int32),
    }


HIGH_PRECISION = lax.Precision.HIGHEST


def split_heads(matrix):
    return matrix.reshape(matrix.shape[0], HEADS, HEAD_FEATURES)


def select_rows(source, dilation, offsets):
    shaped = source.reshape((source.shape[0] // dilation, dilation) + source.shape[1:])
    choose_index = jnp.broadcast_to(offsets.astype(jnp.int32)[None, None, :, None], (shaped.shape[0], 1, shaped.shape[2], shaped.shape[3]))
    return jnp.take_along_axis(shaped, choose_index, axis=1)[:, 0]


def spread_rows(source, dilation, offsets, filler):
    chosen = jnp.arange(dilation, dtype=jnp.int32)[None, :, None, None] == offsets.astype(jnp.int32)[None, None, :, None]
    spread = jnp.where(chosen, source[:, None], filler)
    return spread.reshape((source.shape[0] * dilation,) + source.shape[1:])


def widen_precision(tensor):
    return tensor.astype(jnp.float32)


def rounded_values(tensor):
    narrow = lax.optimization_barrier(tensor.astype(jnp.bfloat16))
    return narrow.astype(jnp.float32)


def level_scores(query_piece, key_piece, query_pos, key_pos):
    score_matrix = jnp.einsum('ywf,zwf->wyz', widen_precision(query_piece), widen_precision(key_piece), precision=HIGH_PRECISION) * (HEAD_FEATURES ** -0.5)
    allowed = key_pos[None, None, :] <= query_pos[None, :, None]
    return score_matrix, allowed


def attend_level(query_piece, key_piece, value_piece, query_pos, key_pos):
    score_matrix, allowed = level_scores(query_piece, key_piece, query_pos, key_pos)
    level_top = jnp.max(jnp.where(allowed, score_matrix, -jnp.inf), axis=2)
    attention_weight = jnp.where(allowed, jnp.exp(score_matrix - level_top[:, :, None]), 0.0)
    level_total = jnp.sum(attention_weight, axis=2)
    level_running_sum = jnp.einsum('cue,eco->uco', rounded_values(attention_weight), widen_precision(value_piece), precision=HIGH_PRECISION)
    return level_top.T, level_total.T, level_running_sum


def pair_grads(query_piece, key_piece, value_piece, gradient_piece, lse_part, delta_part, query_pos, key_pos):
    logit_scale_factor = HEAD_FEATURES ** -0.5
    score_matrix, allowed = level_scores(query_piece, key_piece, query_pos, key_pos)
    attention_weight = jnp.where(allowed, jnp.exp(score_matrix - lse_part.T[:, :, None]), 0.0)
    weight_gradient = jnp.einsum('ywf,zwf->wyz', widen_precision(gradient_piece), widen_precision(value_piece), precision=HIGH_PRECISION)
    dscores = attention_weight * (weight_gradient - delta_part.T[:, :, None])
    weight_lowered = rounded_values(attention_weight)
    score_gradient_lowered = rounded_values(dscores)
    query_addend = jnp.einsum('cue,eco->uco', score_gradient_lowered, widen_precision(key_piece), precision=HIGH_PRECISION) * logit_scale_factor
    key_addend = jnp.einsum('lap,alv->plv', score_gradient_lowered, widen_precision(query_piece), precision=HIGH_PRECISION) * logit_scale_factor
    value_addend = jnp.einsum('lap,alv->plv', weight_lowered, widen_precision(gradient_piece), precision=HIGH_PRECISION)
    return query_addend, key_addend, value_addend


def spread_level(pieces, dilation, offsets):
    level_top = spread_rows(pieces[0][:, :, None], dilation, offsets, -jnp.inf)[:, :, 0]
    level_total = spread_rows(pieces[1][:, :, None], dilation, offsets, 0.0)[:, :, 0]
    level_running_sum = spread_rows(pieces[2], dilation, offsets, 0.0)
    return level_top, level_total, level_running_sum


def merge_levels(levels):
    overall = jnp.maximum(jnp.maximum(levels[0][0], levels[1][0]), levels[2][0])
    denom = jnp.exp(levels[0][0] - overall) * levels[0][1]
    denom = denom + jnp.exp(levels[1][0] - overall) * levels[1][1]
    denom = denom + jnp.exp(levels[2][0] - overall) * levels[2][1]
    lse = overall + jnp.log(denom)
    out_full = jnp.exp(levels[0][0] - lse)[:, :, None] * levels[0][2]
    out_full = out_full + jnp.exp(levels[1][0] - lse)[:, :, None] * levels[1][2]
    out_full = out_full + jnp.exp(levels[2][0] - lse)[:, :, None] * levels[2][2]
    return lse, out_full


def reference(queries, keys, values, out_grad, near_offsets, far_offsets):
    query_h = split_heads(queries)
    key_h = split_heads(keys)
    value_h = split_heads(values)
    grad_h = split_heads(out_grad)
    blocks = TOKENS // TOK_DEV
    positions = jnp.arange(TOK_DEV, dtype=jnp.int32)
    segments = TOKENS // NEAR_SEGMENT
    near_count = NEAR_SEGMENT // NEAR_RATE
    near_pos = jnp.arange(near_count, dtype=jnp.int32)
    far_pos = jnp.arange(TOKENS // FAR_RATE, dtype=jnp.int32)

    def by_blocks(tensor):
        return tensor.reshape((blocks, TOK_DEV) + tensor.shape[1:])

    def by_segments(tensor):
        return tensor.reshape((segments, near_count) + tensor.shape[1:])

    def flatten(tensor):
        return tensor.reshape((tensor.shape[0] * tensor.shape[1],) + tensor.shape[2:])

    def local_forward(pieces):
        return attend_level(pieces[0], pieces[1], pieces[2], positions, positions)

    def near_forward(pieces):
        return attend_level(pieces[0], pieces[1], pieces[2], near_pos, near_pos)

    local_parts = lax.map(local_forward, (by_blocks(query_h), by_blocks(key_h), by_blocks(value_h)))
    local_parts = tuple(flatten(tensor) for tensor in local_parts)
    near_inputs = tuple(by_segments(select_rows(tensor, NEAR_RATE, near_offsets)) for tensor in (query_h, key_h, value_h))
    near_parts = lax.map(near_forward, near_inputs)
    near_parts = spread_level(tuple(flatten(tensor) for tensor in near_parts), NEAR_RATE, near_offsets)
    far_inputs = tuple(select_rows(tensor, FAR_RATE, far_offsets) for tensor in (query_h, key_h, value_h))
    far_parts = attend_level(far_inputs[0], far_inputs[1], far_inputs[2], far_pos, far_pos)
    far_parts = spread_level(far_parts, FAR_RATE, far_offsets)
    lse, out_full = merge_levels((local_parts, near_parts, far_parts))
    attn_out = out_full.reshape(TOKENS, WIDTH).astype(jnp.bfloat16)
    delta = jnp.sum(widen_precision(grad_h) * out_full, axis=2)

    def local_backward(pieces):
        return pair_grads(pieces[0], pieces[1], pieces[2], pieces[3], pieces[4], pieces[5], positions, positions)

    def near_backward(pieces):
        return pair_grads(pieces[0], pieces[1], pieces[2], pieces[3], pieces[4], pieces[5], near_pos, near_pos)

    local_grads = lax.map(local_backward, tuple(by_blocks(tensor) for tensor in (query_h, key_h, value_h, grad_h, lse, delta)))
    local_grads = tuple(flatten(tensor) for tensor in local_grads)

    def select_all(dilation, offsets):
        picked = [select_rows(tensor, dilation, offsets) for tensor in (query_h, key_h, value_h, grad_h)]
        picked.append(select_rows(lse[:, :, None], dilation, offsets)[:, :, 0])
        picked.append(select_rows(delta[:, :, None], dilation, offsets)[:, :, 0])
        return tuple(picked)

    near_grads = lax.map(near_backward, tuple(by_segments(tensor) for tensor in select_all(NEAR_RATE, near_offsets)))
    near_grads = tuple(spread_rows(flatten(tensor), NEAR_RATE, near_offsets, 0.0) for tensor in near_grads)
    far_sel = select_all(FAR_RATE, far_offsets)
    far_grads = pair_grads(far_sel[0], far_sel[1], far_sel[2], far_sel[3], far_sel[4], far_sel[5], far_pos, far_pos)
    far_grads = tuple(spread_rows(tensor, FAR_RATE, far_offsets, 0.0) for tensor in far_grads)
    results = []
    for which in range(3):
        total_grad = local_grads[which] + near_grads[which] + far_grads[which]
        results.append(total_grad.reshape(TOKENS, WIDTH).astype(jnp.bfloat16))
    return attn_out, results[0], results[1], results[2]
```

```python
import functools

import jax
import jax.numpy as jnp
from jax import lax
from jax.experimental import pallas as pl
from jax.experimental.pallas import tpu as pltpu
from jax.sharding import PartitionSpec as P

HEADS = 16
FEAT = 64
ROWS = 256
WIDTH = 1024
NEAR_RATE = 64
FAR_RATE = 256
SEQ = 32
OUTER = 8
SLOTS = 8
FAR_SLOT = 4
STAT_SLOT = 5
GROUP = 4
GROUPS = HEADS // GROUP
GLANES = GROUP * FEAT
GSLOTS = GROUP * SLOTS
SCALE = FEAT**-0.5
LOW = -1e30
F32 = jnp.float32
BF16 = jnp.bfloat16
VMEM_BYTES = 60 * 1024 * 1024


def iota(shape, axis):
    return lax.broadcasted_iota(jnp.int32, shape, axis)


def dot_nn(a, b):
    return lax.dot_general(a, b, (((1,), (0,)), ((), ())), preferred_element_type=F32)


def dot_nt(a, b):
    return lax.dot_general(a, b, (((1,), (1,)), ((), ())), preferred_element_type=F32)


def dot_tn(a, b):
    return lax.dot_general(a, b, (((0,), (0,)), ((), ())), preferred_element_type=F32)


def parts_of(value):
    high = value.astype(BF16).astype(F32)
    rest = value - high
    middle = rest.astype(BF16).astype(F32)
    return high, middle, rest - middle


def part_lanes(lse, d, at):
    out = jnp.zeros((lse.shape[0], at.shape[1]), F32)
    for index, part in enumerate(parts_of(lse) + parts_of(d)):
        out = jnp.where(at == index, part, out)
    return out


def read_parts(lanes, at):
    lse = jnp.sum(jnp.where((at >= 0) & (at < 3), lanes, 0.0), axis=1, keepdims=True)
    d = jnp.sum(jnp.where((at >= 3) & (at < 6), lanes, 0.0), axis=1, keepdims=True)
    return lse, d


def pack_stats(lse, d):
    rows = lse.shape[0]
    row, lane = iota((rows, 128), 0), iota((rows, 128), 1)
    at = jnp.where(lane // 8 == row % SLOTS, lane % 8, -1)
    spread = part_lanes(lse, d, at).reshape(rows // SLOTS, SLOTS, 128)
    total = jnp.sum(spread, axis=1, keepdims=True)
    return jnp.broadcast_to(total, spread.shape).reshape(rows, 128)


def unpack_stats(block):
    groups = block.shape[0]
    lanes = jnp.broadcast_to(block[:, STAT_SLOT : STAT_SLOT + 1, :], (groups, SLOTS, 128))
    lanes = lanes.reshape(groups * SLOTS, 128)
    row, lane = iota(lanes.shape, 0), iota(lanes.shape, 1)
    return read_parts(lanes, jnp.where(lane // 8 == row % SLOTS, lane % 8, -1))


def swap_halves(x):
    return pltpu.roll(x, FEAT, 1)


def slot_rows(near_ref, far_ref, first):
    index = iota((GSLOTS, 1), 0)
    slot = index % SLOTS
    near = jnp.zeros((GSLOTS, 1), jnp.int32)
    far = jnp.zeros((GSLOTS, 1), jnp.int32)
    for h in range(GROUP):
        here = index // SLOTS == h
        near = jnp.where(here, near_ref[first + h], near)
        far = jnp.where(here, far_ref[first + h], far)
    row = jnp.where(slot < FAR_SLOT, near + NEAR_RATE * slot, jnp.where(slot == FAR_SLOT, far, -1))
    repeat = (slot == FAR_SLOT) & (far % NEAR_RATE == near)
    return row, repeat, slot


def head_mask():
    return iota((GSLOTS, GLANES), 1) // FEAT == iota((GSLOTS, GLANES), 0) // SLOTS


def softmax_terms(scores, allowed, weight_grads):
    masked = jnp.where(allowed, scores, LOW)
    top = jnp.max(masked, axis=1, keepdims=True)
    weights = jnp.where(allowed, jnp.exp(masked - top), 0.0)
    total = jnp.sum(weights, axis=1, keepdims=True)
    return top, total, jnp.sum(weights * weight_grads, axis=1, keepdims=True)


def merge_terms(lse, d, top, total, grad_total):
    overall = jnp.maximum(lse, top)
    old, new = jnp.exp(lse - overall), jnp.exp(top - overall)
    mass = old + new * total
    return overall + jnp.log(mass), (old * d + new * grad_total) / mass


def select_kernel(near_ref, far_ref, q_ref, k_ref, v_ref, g_ref, pay_ref, qs_ref, gs_ref, s_ref, gv_ref):
    row, _, slot = slot_rows(near_ref, far_ref, pl.program_id(0) * GROUP)
    pick = jnp.where(iota((GSLOTS, ROWS), 1) == row, 1.0, 0.0).astype(BF16)
    mask = head_mask()

    def selected(ref):
        return jnp.where(mask, dot_nn(pick, ref[...]), 0.0)

    def folded(x):
        x = x[:, :128] + x[:, 128:]
        return x + swap_halves(x)

    qs, ks, vs, gs = selected(q_ref), selected(k_ref), selected(v_ref), selected(g_ref)
    qb, gb = qs.astype(BF16), gs.astype(BF16)
    qs_ref[0] = qb
    gs_ref[0] = gb
    allowed = iota((GSLOTS, ROWS), 1) <= row
    scores = jnp.where(allowed, dot_nt(qb, k_ref[...]) * SCALE, LOW)
    grads = dot_nt(gb, v_ref[...])
    s_ref[0] = scores
    gv_ref[0] = grads
    top, total, grad_total = softmax_terms(scores, allowed, grads)
    used = slot <= FAR_SLOT
    total = jnp.where(used, total, 1.0)
    lse = jnp.where(used, top + jnp.log(total), 0.0)
    stats = pack_stats(lse, jnp.where(used, grad_total / total, 0.0))
    low_half = iota((GSLOTS, 128), 1) < FEAT
    qk = jnp.where(low_half, folded(qs), folded(ks))
    vg = jnp.where(low_half, folded(vs), folded(gs))
    qk = jnp.where(slot == STAT_SLOT, stats, qk)
    block = jnp.concatenate(
        [qk.reshape(GROUP, SLOTS, 128), vg.reshape(GROUP, SLOTS, 128)], axis=1
    ).astype(BF16)
    pay_ref[0] = block
    pay_ref[1] = block


def select_call(near, far, q, k, v, g):
    smem = pl.BlockSpec(memory_space=pltpu.SMEM)
    cols = pl.BlockSpec((ROWS, GLANES), lambda b: (0, b))
    group = lambda: pl.BlockSpec((1, GSLOTS, ROWS), lambda b: (b, 0, 0))
    return pl.pallas_call(
        select_kernel,
        grid=(GROUPS,),
        in_specs=[smem, smem, cols, cols, cols, cols],
        out_specs=[pl.BlockSpec((2, GROUP, 2 * SLOTS, 128), lambda b: (0, b, 0, 0))] + [group()] * 4,
        out_shape=[
            jax.ShapeDtypeStruct((2, HEADS, 2 * SLOTS, 128), BF16),
            jax.ShapeDtypeStruct((GROUPS, GSLOTS, GLANES), BF16),
            jax.ShapeDtypeStruct((GROUPS, GSLOTS, GLANES), BF16),
            jax.ShapeDtypeStruct((GROUPS, GSLOTS, ROWS), F32),
            jax.ShapeDtypeStruct((GROUPS, GSLOTS, ROWS), F32),
        ],
        compiler_params=pltpu.CompilerParams(vmem_limit_bytes=VMEM_BYTES),
        name="select_rows",
    )(near, far, q, k, v, g)


def local_group(near_ref, far_ref, first, q_ref, k_ref, v_ref, g_ref):
    lane = iota((1, GLANES), 1)
    query = iota((1, ROWS), 1)
    allowed = iota((ROWS, ROWS), 0) <= iota((ROWS, ROWS), 1)
    q, k, v, g = q_ref[...], k_ref[...], v_ref[...], g_ref[...]
    q = (q.astype(F32) * SCALE).astype(BF16)
    row_of = iota((GLANES, 1), 0)
    kt, vt = jnp.transpose(k), jnp.transpose(v)
    zero = jnp.zeros((), BF16)
    out_t = jnp.zeros((GLANES, ROWS), F32)
    dq_t = jnp.zeros((GLANES, ROWS), F32)
    dk = jnp.zeros((ROWS, GLANES), F32)
    dv = jnp.zeros((ROWS, GLANES), F32)
    for h in range(GROUP):
        near, far = near_ref[first + h], far_ref[first + h]
        special = (query % NEAR_RATE == near) | (query == far)
        here = lane // FEAT == h
        here_t = row_of // FEAT == h
        scores = jnp.where(allowed, dot_nt(jnp.where(here, k, zero), q), LOW)
        grads = dot_nt(jnp.where(here, v, zero), g)
        weights = jnp.exp(scores - jnp.max(scores, axis=0, keepdims=True))
        total = jnp.sum(weights, axis=0, keepdims=True)
        weights = weights * jnp.where(special, 0.0, 1.0 / total)
        delta = jnp.sum(weights * grads, axis=0, keepdims=True)
        dscores = (weights * (grads - delta)).astype(BF16)
        weights = weights.astype(BF16)
        out_t += dot_nn(jnp.where(here_t, vt, zero), weights)
        dq_t += dot_nn(jnp.where(here_t, kt, zero), dscores)
        dk += dot_nn(dscores, jnp.where(here, q, zero))
        dv += dot_nn(weights, jnp.where(here, g, zero))
    return jnp.transpose(out_t), jnp.transpose(dq_t) * SCALE, dk, dv


def local_kernel(base, near_ref, far_ref, q_ref, k_ref, v_ref, g_ref, *refs):
    out_ref, dq_ref, dk_ref, dv_ref = refs[-4:]
    first = (pl.program_id(0) + base) * GROUP
    out, dq, dk, dv = local_group(near_ref, far_ref, first, q_ref, k_ref, v_ref, g_ref)
    out_ref[...] = out.astype(BF16)
    dq_ref[...] = dq.astype(BF16)
    dk_ref[...] = dk
    dv_ref[...] = dv


def local_call(base, count, near, far, q, k, v, g, done):
    smem = pl.BlockSpec(memory_space=pltpu.SMEM)
    cols = lambda: pl.BlockSpec((ROWS, GLANES), lambda b: (0, b + base))
    types = (BF16, BF16, F32, F32)
    return pl.pallas_call(
        functools.partial(local_kernel, base),
        grid=(count,),
        in_specs=[smem, smem] + [cols()] * 4 + [pl.BlockSpec(memory_space=pl.ANY)] * len(done),
        out_specs=[cols()] * 4,
        out_shape=[jax.ShapeDtypeStruct((ROWS, WIDTH), kind) for kind in types],
        input_output_aliases={6 + i: i for i in range(len(done))},
        compiler_params=pltpu.CompilerParams(vmem_limit_bytes=VMEM_BYTES),
        cost_estimate=pl.CostEstimate(
            flops=count * GROUP * 14 * ROWS * ROWS * FEAT,
            bytes_accessed=count * 7 * ROWS * GLANES * 2,
            transcendentals=count * GROUP * ROWS * ROWS,
        ),
        name="local_level",
    )(near, far, q, k, v, g, *done)


def slot_positions(near, far):
    col = iota((SEQ * SLOTS, 1), 0)
    line = iota((1, SEQ * SLOTS), 1)

    def position(index):
        slot = index % SLOTS
        return index // SLOTS * ROWS + jnp.where(slot < FAR_SLOT, near + NEAR_RATE * slot, far)

    return col, line, position(col), position(line)


def pair_halves(qk, vg):
    low = iota(qk.shape, 1) < FEAT
    q0 = jnp.where(low, qk, 0.0)
    k0 = jnp.where(low, swap_halves(qk), 0.0)
    g0 = jnp.where(low, swap_halves(vg), 0.0)
    v0 = jnp.where(low, vg, 0.0)
    k1 = jnp.where(low, 0.0, qk)
    g1 = jnp.where(low, 0.0, vg)
    return tuple(x.astype(BF16) for x in (q0, k0, v0, g0, k1, g1))


def near_kernel(near_ref, far_ref, got_ref, send_ref, stat_ref):
    head = lax.axis_index("seq") % HEADS
    near, far = near_ref[head], far_ref[head]
    got = got_ref[...].astype(F32)
    qk, vg = got[:, :SLOTS].reshape(SEQ * SLOTS, 128), got[:, SLOTS:].reshape(SEQ * SLOTS, 128)
    lse, d = unpack_stats(got)
    q0, k0, v0, g0, _, _ = pair_halves(qk, vg)
    col, line, col_at, line_at = slot_positions(near, far)
    asks = (col % SLOTS < FAR_SLOT) | ((col % SLOTS == FAR_SLOT) & (far % NEAR_RATE == near))
    allowed = asks & (line % SLOTS < FAR_SLOT) & (line_at <= col_at)
    terms = softmax_terms(dot_nt(q0, k0) * SCALE, allowed, dot_nt(g0, v0))
    lse, d = merge_terms(lse, d, *terms)
    lane = iota((SEQ * SLOTS, 128), 1)
    stats = part_lanes(lse, d, lane)
    stat_ref[...] = stats
    rows = SEQ * SLOTS
    pick = iota((SEQ, rows), 1) == iota((SEQ, rows), 0) * SLOTS + FAR_SLOT
    pick = jnp.where(pick, 1.0, 0.0).astype(BF16)
    block = jnp.concatenate([dot_nn(pick, x.astype(BF16)) for x in (qk, vg, stats)], axis=0)
    block = block.astype(BF16)
    for o in range(OUTER):
        send_ref[o] = block


def near_call(near, far, got):
    smem = pl.BlockSpec(memory_space=pltpu.SMEM)
    return pl.pallas_call(
        near_kernel,
        in_specs=[smem, smem, pl.BlockSpec(memory_space=pltpu.VMEM)],
        out_specs=[pl.BlockSpec(memory_space=pltpu.VMEM)] * 2,
        out_shape=[
            jax.ShapeDtypeStruct((OUTER, 3 * SEQ, 128), BF16),
            jax.ShapeDtypeStruct((SEQ * SLOTS, 128), F32),
        ],
        compiler_params=pltpu.CompilerParams(vmem_limit_bytes=VMEM_BYTES),
        name="near_forward",
    )(near, far, got)


def level_grads(halves, scores, allowed, grads, lse, delta):
    q0, k0, v0, g0, k1, g1 = halves
    weights = jnp.where(allowed, jnp.exp(jnp.where(allowed, scores - lse, 0.0)), 0.0)
    dscores = (weights * (grads - delta)).astype(BF16)
    weights = weights.astype(BF16)
    query_side = dot_nn(weights, v0) + dot_nn(dscores, k1)
    key_side = dot_tn(dscores, q0) + dot_tn(weights, g1)
    low = iota((1, 128), 1) < FEAT
    return query_side * jnp.where(low, 1.0, SCALE), key_side * jnp.where(low, SCALE, 1.0)


def owner_kernel(near_ref, far_ref, got_ref, stat_ref, far_got_ref, send_ref):
    head = lax.axis_index("seq") % HEADS
    segment = lax.axis_index("outer")
    near, far = near_ref[head], far_ref[head]
    rows = SEQ * SLOTS
    lane = iota((rows, 128), 1)

    far_qk = far_got_ref[:, :SEQ].reshape(rows, 128).astype(F32)
    far_vg = far_got_ref[:, SEQ : 2 * SEQ].reshape(rows, 128).astype(F32)
    far_stats = far_got_ref[:, 2 * SEQ :].reshape(rows, 128).astype(F32)
    far_halves = pair_halves(far_qk, far_vg)
    scores = dot_nt(far_halves[0], far_halves[1]) * SCALE
    grads = dot_nt(far_halves[3], far_halves[2])
    allowed = iota((rows, rows), 1) <= iota((rows, rows), 0)
    top, total, grad_total = softmax_terms(scores, allowed, grads)
    lse, delta = merge_terms(*read_parts(far_stats, lane), top, total, grad_total)
    query_side, key_side = level_grads(far_halves, scores, allowed, grads, lse, delta)
    own_stats = part_lanes(top + jnp.log(total), grad_total / total, lane).astype(BF16)

    row, column = iota((rows, rows), 0), iota((rows, rows), 1)
    own = column == segment * SEQ + row // SLOTS
    to_far = jnp.where(own & (row % SLOTS == FAR_SLOT), 1.0, 0.0).astype(BF16)
    to_all = jnp.where(own, 1.0, 0.0).astype(BF16)
    first = dot_nn(to_far, query_side.astype(BF16))
    second = dot_nn(to_far, key_side.astype(BF16))
    far_lse, far_d = read_parts(dot_nn(to_all, own_stats), lane)

    col, line, col_at, line_at = slot_positions(near, far)
    slot = col % SLOTS
    active = (slot == FAR_SLOT) | ((slot < FAR_SLOT) & (near + NEAR_RATE * slot == far))
    lse, d = read_parts(stat_ref[...], lane)
    merged_lse, merged_d = merge_terms(lse, d, far_lse, 1.0, far_d)
    lse, delta = jnp.where(active, merged_lse, lse), jnp.where(active, merged_d, d)

    got = got_ref[...].astype(F32)
    halves = pair_halves(got[:, :SLOTS].reshape(rows, 128), got[:, SLOTS:].reshape(rows, 128))
    allowed = (slot < FAR_SLOT) & (line % SLOTS < FAR_SLOT) & (line_at <= col_at)
    query_side, key_side = level_grads(
        halves, dot_nt(halves[0], halves[1]) * SCALE, allowed, dot_nt(halves[3], halves[2]), lse, delta
    )
    first += query_side
    second += key_side
    used = slot <= FAR_SLOT
    stats = pack_stats(jnp.where(used, lse, 0.0), jnp.where(used, delta, 0.0))
    first = jnp.where(slot == STAT_SLOT, stats, first)
    send_ref[...] = jnp.concatenate(
        [first.reshape(SEQ, SLOTS, 128), second.reshape(SEQ, SLOTS, 128)], axis=1
    ).astype(BF16)


def owner_call(near, far, got, stats, far_got):
    smem = pl.BlockSpec(memory_space=pltpu.SMEM)
    vmem = pl.BlockSpec(memory_space=pltpu.VMEM)
    return pl.pallas_call(
        owner_kernel,
        in_specs=[smem, smem, vmem, vmem, vmem],
        out_specs=vmem,
        out_shape=jax.ShapeDtypeStruct((SEQ, 2 * SLOTS, 128), BF16),
        compiler_params=pltpu.CompilerParams(vmem_limit_bytes=VMEM_BYTES),
        name="owner_level",
    )(near, far, got, stats, far_got)


def finish_kernel(
    near_ref, far_ref, got_ref, qs_ref, gs_ref, s_ref, gv_ref, k_ref, v_ref,
    out_in, dq_in, dk_in, dv_in, out_ref, dq_ref, dk_ref, dv_ref,
):
    row, repeat, slot = slot_rows(near_ref, far_ref, pl.program_id(0) * GROUP)
    pick = jnp.where(iota((GSLOTS, ROWS), 1) == row, 1.0, 0.0).astype(BF16)
    mask = head_mask()
    got = got_ref[...].astype(F32)
    lse, delta = unpack_stats(got)
    used = slot <= FAR_SLOT
    low = iota((GSLOTS, 128), 1) < FEAT

    def spread(x, keep_low):
        x = jnp.where(used & (low if keep_low else ~low), x, 0.0)
        x = x + swap_halves(x)
        return jnp.where(mask, jnp.concatenate([x, x], axis=1), 0.0)

    first = got[:, :SLOTS].reshape(GSLOTS, 128)
    second = got[:, SLOTS:].reshape(GSLOTS, 128)
    weights = jnp.where(repeat, 0.0, jnp.exp(s_ref[0] - lse))
    dscores = (weights * (gv_ref[0] - delta)).astype(BF16)
    weights = weights.astype(BF16)
    out = jnp.where(mask, dot_nn(weights, v_ref[...]), 0.0) + spread(first, True)
    dq = jnp.where(mask, dot_nn(dscores, k_ref[...]), 0.0) * SCALE + spread(first, False)
    out_ref[...] = (out_in[...].astype(F32) + dot_tn(pick, out.astype(BF16))).astype(BF16)
    dq_ref[...] = (dq_in[...].astype(F32) + dot_tn(pick, dq.astype(BF16))).astype(BF16)
    qs = (qs_ref[0].astype(F32) * SCALE).astype(BF16)
    dk = dot_tn(dscores, qs) + dot_tn(pick, spread(second, True).astype(BF16))
    dv = dot_tn(weights, gs_ref[0]) + dot_tn(pick, spread(second, False).astype(BF16))
    dk_ref[...] = (dk_in[...] + dk).astype(BF16)
    dv_ref[...] = (dv_in[...] + dv).astype(BF16)


def finish_call(near, far, got, qs, gs, s, gv, k, v, parts):
    smem = pl.BlockSpec(memory_space=pltpu.SMEM)
    cols = lambda: pl.BlockSpec((ROWS, GLANES), lambda b: (0, b))
    group = lambda: pl.BlockSpec((1, GSLOTS, ROWS), lambda b: (b, 0, 0))
    chunk = pl.BlockSpec((GROUP, 2 * SLOTS, 128), lambda b: (b, 0, 0))
    return pl.pallas_call(
        finish_kernel,
        grid=(GROUPS,),
        in_specs=[smem, smem, chunk] + [group()] * 4 + [cols()] * 6,
        out_specs=[cols()] * 4,
        out_shape=[jax.ShapeDtypeStruct((ROWS, WIDTH), BF16)] * 4,
        compiler_params=pltpu.CompilerParams(vmem_limit_bytes=VMEM_BYTES),
        name="finish_rows",
    )(near, far, got, qs, gs, s, gv, k, v, *parts)


def exchange(x, axis):
    return lax.all_to_all(x, axis, split_axis=0, concat_axis=0, tiled=True)


def on_device(queries, keys, values, out_grad, near_offsets, far_offsets):
    arrays = (queries, keys, values, out_grad)
    half = GROUPS // 2
    pay, qs, gs, s, gv = select_call(near_offsets, far_offsets, *arrays)
    got = exchange(pay.reshape(SEQ, 2 * SLOTS, 128), "seq")
    (near_1, far_1), _ = lax.optimization_barrier(((near_offsets, far_offsets), pay))
    parts = local_call(0, half, near_1, far_1, *arrays, ())
    got, parts = lax.optimization_barrier((got, parts))
    far_pay, stats = near_call(near_offsets, far_offsets, got)
    far_got = exchange(far_pay, "outer")
    back = owner_call(near_offsets, far_offsets, got, stats, far_got)
    (near_2, far_2), back = lax.optimization_barrier(((near_offsets, far_offsets), back))
    back_got = exchange(back, "seq")
    parts = local_call(half, GROUPS - half, near_2, far_2, *arrays, parts)
    return finish_call(
        near_offsets, far_offsets, back_got, qs, gs, s, gv, keys, values, parts
    )


def solution(mesh):
    split = P(("outer", "seq"), None)
    return jax.shard_map(
        on_device,
        mesh=mesh,
        in_specs=(split, split, split, split, P(), P()),
        out_specs=(split, split, split, split),
        check_vma=False,
    )
```

```python
import functools

import jax
import jax.numpy as jnp
from jax import lax
from jax.experimental import pallas as pl
from jax.experimental.pallas import tpu as pltpu
from jax.sharding import PartitionSpec as P

HEADS = 16
FEAT = 64
ROWS = 256
WIDTH = 1024
NEAR_RATE = 64
FAR_RATE = 256
SEQ = 32
OUTER = 8
SLOTS = 8
FAR_SLOT = 4
STAT_SLOT = 5
NEAR_LANE = 48
FAR_LANE = 49
GROUP = 4
GROUPS = HEADS // GROUP
GLANES = GROUP * FEAT
GSLOTS = GROUP * SLOTS
SCALE = FEAT**-0.5
LOW = -1e30
F32 = jnp.float32
BF16 = jnp.bfloat16
VMEM_BYTES = 24 * 1024 * 1024


def pinned(space, *arrays):
    return tuple(pltpu.with_memory_space_constraint(x, space) for x in arrays)


def iota(shape, axis):
    return lax.broadcasted_iota(jnp.int32, shape, axis)


def dot_nn(a, b):
    return lax.dot_general(a, b, (((1,), (0,)), ((), ())), preferred_element_type=F32)


def dot_nt(a, b):
    return lax.dot_general(a, b, (((1,), (1,)), ((), ())), preferred_element_type=F32)


def dot_tn(a, b):
    return lax.dot_general(a, b, (((0,), (0,)), ((), ())), preferred_element_type=F32)


def parts_of(value):
    high = value.astype(BF16).astype(F32)
    rest = value - high
    middle = rest.astype(BF16).astype(F32)
    return high, middle, rest - middle


def part_lanes(lse, d, at):
    out = jnp.zeros((lse.shape[0], at.shape[1]), F32)
    for index, part in enumerate(parts_of(lse) + parts_of(d)):
        out = jnp.where(at == index, part, out)
    return out


def read_parts(lanes, at):
    lse = jnp.sum(jnp.where((at >= 0) & (at < 3), lanes, 0.0), axis=1, keepdims=True)
    d = jnp.sum(jnp.where((at >= 3) & (at < 6), lanes, 0.0), axis=1, keepdims=True)
    return lse, d


def pack_stats(lse, d):
    rows = lse.shape[0]
    row, lane = iota((rows, 128), 0), iota((rows, 128), 1)
    at = jnp.where(lane // 8 == row % SLOTS, lane % 8, -1)
    spread = part_lanes(lse, d, at).reshape(rows // SLOTS, SLOTS, 128)
    total = jnp.sum(spread, axis=1, keepdims=True)
    return jnp.broadcast_to(total, spread.shape).reshape(rows, 128)


def unpack_stats(block):
    groups = block.shape[0]
    lanes = jnp.broadcast_to(block[:, STAT_SLOT : STAT_SLOT + 1, :], (groups, SLOTS, 128))
    lanes = lanes.reshape(groups * SLOTS, 128)
    row, lane = iota(lanes.shape, 0), iota(lanes.shape, 1)
    return read_parts(lanes, jnp.where(lane // 8 == row % SLOTS, lane % 8, -1))


def swap_halves(x):
    return pltpu.roll(x, FEAT, 1)


def group_offsets(near_ref, far_ref, first):
    index = iota((GSLOTS, 1), 0)
    near = jnp.zeros((GSLOTS, 1), jnp.int32)
    far = jnp.zeros((GSLOTS, 1), jnp.int32)
    for h in range(GROUP):
        here = index // SLOTS == h
        near = jnp.where(here, near_ref[first + h], near)
        far = jnp.where(here, far_ref[first + h], far)
    return near, far


def slot_rows(near_ref, far_ref, first):
    near, far = group_offsets(near_ref, far_ref, first)
    slot = iota((GSLOTS, 1), 0) % SLOTS
    row = jnp.where(slot < FAR_SLOT, near + NEAR_RATE * slot, jnp.where(slot == FAR_SLOT, far, -1))
    repeat = (slot == FAR_SLOT) & (far % NEAR_RATE == near)
    return row, repeat, slot


def head_mask():
    return iota((GSLOTS, GLANES), 1) // FEAT == iota((GSLOTS, GLANES), 0) // SLOTS


def softmax_terms(scores, allowed, weight_grads):
    masked = jnp.where(allowed, scores, LOW)
    top = jnp.max(masked, axis=1, keepdims=True)
    weights = jnp.where(allowed, jnp.exp(masked - top), 0.0)
    total = jnp.sum(weights, axis=1, keepdims=True)
    return top, total, jnp.sum(weights * weight_grads, axis=1, keepdims=True)


def merge_terms(lse, d, top, total, grad_total):
    overall = jnp.maximum(lse, top)
    old, new = jnp.exp(lse - overall), jnp.exp(top - overall)
    mass = old + new * total
    return overall + jnp.log(mass), (old * d + new * grad_total) / mass


OFFSET_SCRATCH = [
    pltpu.SMEM((HEADS,), jnp.int32),
    pltpu.SMEM((HEADS,), jnp.int32),
    pltpu.SemaphoreType.DMA((2,)),
]


def start_offsets(near_in, far_in, near_ref, far_ref, sems):
    copies = [
        pltpu.make_async_copy(near_in, near_ref, sems.at[0]),
        pltpu.make_async_copy(far_in, far_ref, sems.at[1]),
    ]
    for copy in copies:
        copy.start()
    return copies


def start_copies(sources, base, count, buffer, sems):
    copies = []
    for b in range(count):
        here = pl.ds(b * GLANES, GLANES)
        there = pl.ds((base + b) * GLANES, GLANES)
        copies.append(
            [
                pltpu.make_async_copy(source.at[:, there], buffer.at[i, :, here], sems.at[b, i])
                for i, source in enumerate(sources)
            ]
        )
    for group in copies:
        for copy in group:
            copy.start()
    return copies


def start_whole(sources, buffer, sems):
    copies = [
        pltpu.make_async_copy(source, buffer.at[i], sems.at[i]) for i, source in enumerate(sources)
    ]
    for copy in copies:
        copy.start()
    return copies


def select_kernel(
    near_in, far_in, q_ref, k_ref, v_ref, g_ref, pay_ref, near_ref, far_ref, offset_sems, buffer, sems
):
    offset_copies = start_offsets(near_in, far_in, near_ref, far_ref, offset_sems)
    copies = start_whole((q_ref, k_ref, v_ref, g_ref), buffer, sems)
    for copy in offset_copies:
        copy.wait()
    mask = head_mask()
    for b in range(GROUPS):
        row, _, slot = slot_rows(near_ref, far_ref, b * GROUP)
        pick = jnp.where(iota((GSLOTS, ROWS), 1) == row, 1.0, 0.0).astype(BF16)
        if b == 0:
            for copy in copies:
                copy.wait()
        q, k, v, g = (buffer[i, :, b * GLANES : (b + 1) * GLANES] for i in range(4))

        def selected(x):
            return jnp.where(mask, dot_nn(pick, x), 0.0)

        def folded(x):
            x = x[:, :128] + x[:, 128:]
            return x + swap_halves(x)

        qs, ks, vs, gs = selected(q), selected(k), selected(v), selected(g)
        qb, gb = qs.astype(BF16), gs.astype(BF16)
        allowed = iota((GSLOTS, ROWS), 1) <= row
        scores = jnp.where(allowed, dot_nt(qb, k) * SCALE, LOW)
        grads = dot_nt(gb, v)
        top, total, grad_total = softmax_terms(scores, allowed, grads)
        used = slot <= FAR_SLOT
        total = jnp.where(used, total, 1.0)
        lse = jnp.where(used, top + jnp.log(total), 0.0)
        stats = pack_stats(lse, jnp.where(used, grad_total / total, 0.0))
        lane = iota((GSLOTS, 128), 1)
        near, far = group_offsets(near_ref, far_ref, b * GROUP)
        stats = jnp.where(lane == NEAR_LANE, near, jnp.where(lane == FAR_LANE, far, stats))
        low_half = iota((GSLOTS, 128), 1) < FEAT
        qk = jnp.where(low_half, folded(qs), folded(ks))
        vg = jnp.where(low_half, folded(vs), folded(gs))
        qk = jnp.where(slot == STAT_SLOT, stats, qk)
        block = jnp.concatenate(
            [qk.reshape(GROUP, SLOTS, 128), vg.reshape(GROUP, SLOTS, 128)], axis=1
        ).astype(BF16)
        pay_ref[0, b * GROUP : (b + 1) * GROUP] = block
        pay_ref[1, b * GROUP : (b + 1) * GROUP] = block


def select_call(near, far, q, k, v, g):
    hbm = pl.BlockSpec(memory_space=pltpu.HBM)
    vmem = pl.BlockSpec(memory_space=pltpu.VMEM)
    return pl.pallas_call(
        select_kernel,
        in_specs=[hbm] * 6,
        out_specs=vmem,
        out_shape=pltpu.VMEM((2, HEADS, 2 * SLOTS, 128), BF16),
        scratch_shapes=OFFSET_SCRATCH
        + [pltpu.VMEM((4, ROWS, WIDTH), BF16), pltpu.SemaphoreType.DMA((4,))],
        compiler_params=pltpu.CompilerParams(vmem_limit_bytes=VMEM_BYTES),
        name="select_rows",
    )(*pinned(pltpu.HBM, near, far, q, k, v, g))


def local_group(near_ref, far_ref, first, q, k, v, g):
    lane = iota((1, GLANES), 1)
    query = iota((1, ROWS), 1)
    allowed = iota((ROWS, ROWS), 0) <= iota((ROWS, ROWS), 1)
    q = (q.astype(F32) * SCALE).astype(BF16)
    row_of = iota((GLANES, 1), 0)
    kt, vt = jnp.transpose(k), jnp.transpose(v)
    zero = jnp.zeros((), BF16)
    out_t = jnp.zeros((GLANES, ROWS), F32)
    dq_t = jnp.zeros((GLANES, ROWS), F32)
    dk = jnp.zeros((ROWS, GLANES), F32)
    dv = jnp.zeros((ROWS, GLANES), F32)
    for h in range(GROUP):
        near, far = near_ref[first + h], far_ref[first + h]
        special = (query % NEAR_RATE == near) | (query == far)
        here = lane // FEAT == h
        here_t = row_of // FEAT == h
        scores = jnp.where(allowed, dot_nt(jnp.where(here, k, zero), q), LOW)
        grads = dot_nt(jnp.where(here, v, zero), g)
        weights = jnp.exp(scores - jnp.max(scores, axis=0, keepdims=True))
        total = jnp.sum(weights, axis=0, keepdims=True)
        weights = weights * jnp.where(special, 0.0, 1.0 / total)
        delta = jnp.sum(weights * grads, axis=0, keepdims=True)
        dscores = (weights * (grads - delta)).astype(BF16)
        weights = weights.astype(BF16)
        out_t += dot_nn(jnp.where(here_t, vt, zero), weights)
        dq_t += dot_nn(jnp.where(here_t, kt, zero), dscores)
        dk += dot_nn(dscores, jnp.where(here, q, zero))
        dv += dot_nn(weights, jnp.where(here, g, zero))
    return jnp.transpose(out_t), jnp.transpose(dq_t) * SCALE, dk, dv


def local_kernel(
    base, count, near_in, far_in, q_ref, k_ref, v_ref, g_ref,
    query_ref, key_ref, near_ref, far_ref, offset_sems, buffer, sems
):
    offset_copies = start_offsets(near_in, far_in, near_ref, far_ref, offset_sems)
    start_copies((q_ref, k_ref, v_ref, g_ref), base, count, buffer, sems)
    for copy in offset_copies:
        copy.wait()

    def one_group(b, carry):
        here = pl.ds(pl.multiple_of(b * GLANES, GLANES), GLANES)
        for i, source in enumerate((q_ref, k_ref, v_ref, g_ref)):
            there = pl.ds(pl.multiple_of((base + b) * GLANES, GLANES), GLANES)
            pltpu.make_async_copy(source.at[:, there], buffer.at[i, :, here], sems.at[b, i]).wait()
        arrays = tuple(buffer[i, :, here] for i in range(4))
        row, _, _ = slot_rows(near_ref, far_ref, (base + b) * GROUP)
        pick = jnp.where(iota((GSLOTS, ROWS), 1) == row, 1.0, 0.0).astype(BF16)
        mask = head_mask()
        qs = jnp.where(mask, dot_nn(pick, arrays[0]), 0.0)
        gs = jnp.where(mask, dot_nn(pick, arrays[3]), 0.0)
        scores = dot_nt(qs.astype(BF16), arrays[1]) * SCALE
        scores = jnp.where(iota((GSLOTS, ROWS), 1) <= row, scores, LOW)
        slots = (scores, dot_nt(gs.astype(BF16), arrays[2]), qs * SCALE, gs)
        key_ref[2 * ROWS :, here] = jnp.concatenate(slots, axis=0)
        out, dq, dk, dv = local_group(near_ref, far_ref, (base + b) * GROUP, *arrays)
        query_ref[0, :, here] = out.astype(BF16)
        query_ref[1, :, here] = dq.astype(BF16)
        key_ref[:ROWS, here] = dk
        key_ref[ROWS : 2 * ROWS, here] = dv
        return carry

    lax.fori_loop(0, count, one_group, 0)


def local_call(base, count, near, far, q, k, v, g):
    hbm = pl.BlockSpec(memory_space=pltpu.HBM)
    vmem = pl.BlockSpec(memory_space=pltpu.VMEM)
    shape = (ROWS, count * GLANES)
    return pl.pallas_call(
        functools.partial(local_kernel, base, count),
        in_specs=[hbm] * 6,
        out_specs=[vmem] * 2,
        out_shape=[
            pltpu.VMEM((2,) + shape, BF16),
            pltpu.VMEM((2 * ROWS + 4 * GSLOTS, count * GLANES), F32),
        ],
        scratch_shapes=OFFSET_SCRATCH
        + [pltpu.VMEM((4,) + shape, BF16), pltpu.SemaphoreType.DMA((count, 4))],
        compiler_params=pltpu.CompilerParams(vmem_limit_bytes=VMEM_BYTES),
        cost_estimate=pl.CostEstimate(
            flops=count * GROUP * 14 * ROWS * ROWS * FEAT,
            bytes_accessed=count * 7 * ROWS * GLANES * 2,
            transcendentals=count * GROUP * ROWS * ROWS,
        ),
        name="local_level",
    )(*pinned(pltpu.HBM, near, far, q, k, v, g))


def slot_positions(near, far):
    col = iota((SEQ * SLOTS, 1), 0)
    line = iota((1, SEQ * SLOTS), 1)

    def position(index):
        slot = index % SLOTS
        return index // SLOTS * ROWS + jnp.where(slot < FAR_SLOT, near + NEAR_RATE * slot, far)

    return col, line, position(col), position(line)


def pair_halves(qk, vg):
    low = iota(qk.shape, 1) < FEAT
    q0 = jnp.where(low, qk, 0.0)
    k0 = jnp.where(low, swap_halves(qk), 0.0)
    g0 = jnp.where(low, swap_halves(vg), 0.0)
    v0 = jnp.where(low, vg, 0.0)
    k1 = jnp.where(low, 0.0, qk)
    g1 = jnp.where(low, 0.0, vg)
    return tuple(x.astype(BF16) for x in (q0, k0, v0, g0, k1, g1))


def read_offsets(got):
    line = got[0, STAT_SLOT : STAT_SLOT + 1, :].astype(jnp.int32)
    return line[:, NEAR_LANE : NEAR_LANE + 1], line[:, FAR_LANE : FAR_LANE + 1]


def near_kernel(got_ref, send_ref, stat_ref):
    got = got_ref[...].astype(F32)
    near, far = read_offsets(got)
    qk, vg = got[:, :SLOTS].reshape(SEQ * SLOTS, 128), got[:, SLOTS:].reshape(SEQ * SLOTS, 128)
    lse, d = unpack_stats(got)
    q0, k0, v0, g0, _, _ = pair_halves(qk, vg)
    col, line, col_at, line_at = slot_positions(near, far)
    asks = (col % SLOTS < FAR_SLOT) | ((col % SLOTS == FAR_SLOT) & (far % NEAR_RATE == near))
    allowed = asks & (line % SLOTS < FAR_SLOT) & (line_at <= col_at)
    terms = softmax_terms(dot_nt(q0, k0) * SCALE, allowed, dot_nt(g0, v0))
    lse, d = merge_terms(lse, d, *terms)
    lane = iota((SEQ * SLOTS, 128), 1)
    stats = part_lanes(lse, d, lane)
    stat_ref[...] = stats
    rows = SEQ * SLOTS
    pick = iota((SEQ, rows), 1) == iota((SEQ, rows), 0) * SLOTS + FAR_SLOT
    pick = jnp.where(pick, 1.0, 0.0).astype(BF16)
    block = jnp.concatenate([dot_nn(pick, x.astype(BF16)) for x in (qk, vg, stats)], axis=0)
    block = block.astype(BF16)
    for o in range(OUTER):
        send_ref[o] = block


def near_call(got):
    return pl.pallas_call(
        near_kernel,
        in_specs=[pl.BlockSpec(memory_space=pltpu.VMEM)],
        out_specs=[pl.BlockSpec(memory_space=pltpu.VMEM)] * 2,
        out_shape=[
            pltpu.VMEM((OUTER, 3 * SEQ, 128), BF16),
            pltpu.VMEM((SEQ * SLOTS, 128), F32),
        ],
        compiler_params=pltpu.CompilerParams(vmem_limit_bytes=VMEM_BYTES),
        name="near_forward",
    )(got)


def level_grads(halves, scores, allowed, grads, lse, delta):
    q0, k0, v0, g0, k1, g1 = halves
    weights = jnp.where(allowed, jnp.exp(jnp.where(allowed, scores - lse, 0.0)), 0.0)
    dscores = (weights * (grads - delta)).astype(BF16)
    weights = weights.astype(BF16)
    query_side = dot_nn(weights, v0) + dot_nn(dscores, k1)
    key_side = dot_tn(dscores, q0) + dot_tn(weights, g1)
    low = iota((1, 128), 1) < FEAT
    return query_side * jnp.where(low, 1.0, SCALE), key_side * jnp.where(low, SCALE, 1.0)


def owner_kernel(got_ref, stat_ref, far_got_ref, send_ref):
    segment = lax.axis_index("outer")
    got = got_ref[...].astype(F32)
    near, far = read_offsets(got)
    rows = SEQ * SLOTS
    lane = iota((rows, 128), 1)

    far_qk = far_got_ref[:, :SEQ].reshape(rows, 128).astype(F32)
    far_vg = far_got_ref[:, SEQ : 2 * SEQ].reshape(rows, 128).astype(F32)
    far_stats = far_got_ref[:, 2 * SEQ :].reshape(rows, 128).astype(F32)
    far_halves = pair_halves(far_qk, far_vg)
    scores = dot_nt(far_halves[0], far_halves[1]) * SCALE
    grads = dot_nt(far_halves[3], far_halves[2])
    allowed = iota((rows, rows), 1) <= iota((rows, rows), 0)
    top, total, grad_total = softmax_terms(scores, allowed, grads)
    lse, delta = merge_terms(*read_parts(far_stats, lane), top, total, grad_total)
    query_side, key_side = level_grads(far_halves, scores, allowed, grads, lse, delta)
    own_stats = part_lanes(top + jnp.log(total), grad_total / total, lane).astype(BF16)

    row, column = iota((rows, rows), 0), iota((rows, rows), 1)
    own = column == segment * SEQ + row // SLOTS
    to_far = jnp.where(own & (row % SLOTS == FAR_SLOT), 1.0, 0.0).astype(BF16)
    to_all = jnp.where(own, 1.0, 0.0).astype(BF16)
    first = dot_nn(to_far, query_side.astype(BF16))
    second = dot_nn(to_far, key_side.astype(BF16))
    far_lse, far_d = read_parts(dot_nn(to_all, own_stats), lane)

    col, line, col_at, line_at = slot_positions(near, far)
    slot = col % SLOTS
    active = (slot == FAR_SLOT) | ((slot < FAR_SLOT) & (near + NEAR_RATE * slot == far))
    lse, d = read_parts(stat_ref[...], lane)
    merged_lse, merged_d = merge_terms(lse, d, far_lse, 1.0, far_d)
    lse, delta = jnp.where(active, merged_lse, lse), jnp.where(active, merged_d, d)

    halves = pair_halves(got[:, :SLOTS].reshape(rows, 128), got[:, SLOTS:].reshape(rows, 128))
    allowed = (slot < FAR_SLOT) & (line % SLOTS < FAR_SLOT) & (line_at <= col_at)
    query_side, key_side = level_grads(
        halves, dot_nt(halves[0], halves[1]) * SCALE, allowed, dot_nt(halves[3], halves[2]), lse, delta
    )
    first += query_side
    second += key_side
    used = slot <= FAR_SLOT
    stats = pack_stats(jnp.where(used, lse, 0.0), jnp.where(used, delta, 0.0))
    first = jnp.where(slot == STAT_SLOT, stats, first)
    send_ref[...] = jnp.concatenate(
        [first.reshape(SEQ, SLOTS, 128), second.reshape(SEQ, SLOTS, 128)], axis=1
    ).astype(BF16)


def owner_call(got, stats, far_got):
    vmem = pl.BlockSpec(memory_space=pltpu.VMEM)
    return pl.pallas_call(
        owner_kernel,
        in_specs=[vmem, vmem, vmem],
        out_specs=vmem,
        out_shape=pltpu.VMEM((SEQ, 2 * SLOTS, 128), BF16),
        compiler_params=pltpu.CompilerParams(vmem_limit_bytes=VMEM_BYTES),
        name="owner_level",
    )(got, stats, far_got)


def finish_kernel(
    near_in, far_in, got_ref, k_ref, v_ref, *refs
):
    parts, outs = (refs[:2], refs[2:4]), refs[4:8]
    near_ref, far_ref, offset_sems, buffer, sems, results, out_sems = refs[8:]
    offset_copies = start_offsets(near_in, far_in, near_ref, far_ref, offset_sems)
    copies = start_whole((k_ref, v_ref), buffer, sems)
    for copy in offset_copies:
        copy.wait()
    mask = head_mask()
    low = iota((GSLOTS, 128), 1) < FEAT
    sends = []

    def finished(i, b, value):
        here = slice(b * GLANES, (b + 1) * GLANES)
        results[i, :, here] = value.astype(BF16)
        send = pltpu.make_async_copy(results.at[i, :, here], outs[i].at[:, here], out_sems.at[b, i])
        send.start()
        sends.append(send)

    held = []
    for b in range(GROUPS):
        row, repeat, slot = slot_rows(near_ref, far_ref, b * GROUP)
        pick = jnp.where(iota((GSLOTS, ROWS), 1) == row, 1.0, 0.0).astype(BF16)
        got = got_ref[b * GROUP : (b + 1) * GROUP].astype(F32)
        lse, delta = unpack_stats(got)
        used = slot <= FAR_SLOT

        def spread(x, keep_low):
            x = jnp.where(used & (low if keep_low else ~low), x, 0.0)
            x = x + swap_halves(x)
            return jnp.where(mask, jnp.concatenate([x, x], axis=1), 0.0)

        first = got[:, :SLOTS].reshape(GSLOTS, 128)
        second = got[:, SLOTS:].reshape(GSLOTS, 128)
        half, at = divmod(b, GROUPS // 2)
        there = slice(at * GLANES, (at + 1) * GLANES)
        query_part, key_part = parts[half]
        scores, grads, qs, gs = (
            key_part[2 * ROWS + i * GSLOTS : 2 * ROWS + (i + 1) * GSLOTS, there] for i in range(4)
        )
        weights = jnp.where(repeat, 0.0, jnp.exp(scores - lse))
        dscores = (weights * (grads - delta)).astype(BF16)
        weights = weights.astype(BF16)

        def key_side(slots, rows, extra):
            left = jnp.concatenate([slots, pick], axis=0)
            right = jnp.concatenate([rows.astype(BF16), extra.astype(BF16)], axis=0)
            return dot_tn(left, right)

        finished(2, b, key_part[:ROWS, there] + key_side(dscores, qs, spread(second, True)))
        finished(
            3, b, key_part[ROWS : 2 * ROWS, there] + key_side(weights, gs, spread(second, False))
        )
        held.append((pick, weights, dscores, spread(first, True), spread(first, False)))
    for copy in copies:
        copy.wait()
    for b in range(GROUPS):
        here = slice(b * GLANES, (b + 1) * GLANES)
        pick, weights, dscores, out, dq = held[b]
        half, at = divmod(b, GROUPS // 2)
        there = slice(at * GLANES, (at + 1) * GLANES)
        query_part = parts[half][0]
        out += jnp.where(mask, dot_nn(weights, buffer[1, :, here]), 0.0)
        dq += jnp.where(mask, dot_nn(dscores, buffer[0, :, here]), 0.0) * SCALE
        finished(0, b, query_part[0, :, there].astype(F32) + dot_tn(pick, out.astype(BF16)))
        finished(1, b, query_part[1, :, there].astype(F32) + dot_tn(pick, dq.astype(BF16)))
    for send in sends:
        send.wait()


def finish_call(near, far, got, k, v, parts):
    hbm = pl.BlockSpec(memory_space=pltpu.HBM)
    vmem = pl.BlockSpec(memory_space=pltpu.VMEM)
    return pl.pallas_call(
        finish_kernel,
        in_specs=[hbm, hbm, vmem, hbm, hbm] + [vmem] * 4,
        out_specs=[hbm] * 4,
        out_shape=[jax.ShapeDtypeStruct((ROWS, WIDTH), BF16)] * 4,
        scratch_shapes=OFFSET_SCRATCH
        + [
            pltpu.VMEM((2, ROWS, WIDTH), BF16),
            pltpu.SemaphoreType.DMA((2,)),
            pltpu.VMEM((4, ROWS, WIDTH), BF16),
            pltpu.SemaphoreType.DMA((GROUPS, 4)),
        ],
        compiler_params=pltpu.CompilerParams(vmem_limit_bytes=VMEM_BYTES),
        name="finish_rows",
    )(*pinned(pltpu.HBM, near, far), got, *pinned(pltpu.HBM, k, v), *pinned(pltpu.VMEM, *parts))


def exchange(x, axis):
    return lax.all_to_all(x, axis, split_axis=0, concat_axis=0, tiled=True)


def on_device(queries, keys, values, out_grad, near_offsets, far_offsets):
    arrays = (queries, keys, values, out_grad)
    half = GROUPS // 2
    pay = select_call(near_offsets, far_offsets, *arrays)
    got = exchange(pay.reshape(SEQ, 2 * SLOTS, 128), "seq")
    (near_1, far_1), _ = lax.optimization_barrier(((near_offsets, far_offsets), pay))
    parts = tuple(local_call(0, half, near_1, far_1, *arrays))
    got, parts = lax.optimization_barrier((got, parts))
    far_pay, stats = near_call(got)
    far_got = exchange(far_pay, "outer")
    back = owner_call(got, stats, far_got)
    (near_2, far_2), back = lax.optimization_barrier(((near_offsets, far_offsets), back))
    back_got = exchange(back, "seq")
    parts += tuple(local_call(half, GROUPS - half, near_2, far_2, *arrays))
    return finish_call(near_offsets, far_offsets, back_got, keys, values, parts)


def solution(mesh):
    split = P(("outer", "seq"), None)
    return jax.shard_map(
        on_device,
        mesh=mesh,
        in_specs=(split, split, split, split, P(), P()),
        out_specs=(split, split, split, split),
        check_vma=False,
    )
```

```python
import functools

import jax
import jax.numpy as jnp
from jax import lax
from jax.experimental import pallas as pl
from jax.experimental.pallas import tpu as pltpu
from jax.sharding import PartitionSpec as P

HEADS = 16
FEAT = 64
ROWS = 256
WIDTH = 1024
NEAR_RATE = 64
FAR_RATE = 256
SEQ = 32
OUTER = 8
SLOTS = 8
FAR_SLOT = 4
STAT_SLOT = 5
NEAR_LANE = 48
FAR_LANE = 49
GROUP = 4
GROUPS = HEADS // GROUP
GLANES = GROUP * FEAT
GSLOTS = GROUP * SLOTS
SCALE = FEAT**-0.5
LOW = -1e30
SLOT_PARTS = 8
F32 = jnp.float32
BF16 = jnp.bfloat16
VMEM_BYTES = 24 * 1024 * 1024


def pinned(space, *arrays):
    return tuple(pltpu.with_memory_space_constraint(x, space) for x in arrays)


def iota(shape, axis):
    return lax.broadcasted_iota(jnp.int32, shape, axis)


def dot_nn(a, b):
    return lax.dot_general(a, b, (((1,), (0,)), ((), ())), preferred_element_type=F32)


def dot_nt(a, b):
    return lax.dot_general(a, b, (((1,), (1,)), ((), ())), preferred_element_type=F32)


def dot_tn(a, b):
    return lax.dot_general(a, b, (((0,), (0,)), ((), ())), preferred_element_type=F32)


def parts_of(value):
    high = value.astype(BF16).astype(F32)
    rest = value - high
    middle = rest.astype(BF16).astype(F32)
    return high, middle, rest - middle


def part_lanes(lse, d, at):
    out = jnp.zeros((lse.shape[0], at.shape[1]), F32)
    for index, part in enumerate(parts_of(lse) + parts_of(d)):
        out = jnp.where(at == index, part, out)
    return out


def read_parts(lanes, at):
    lse = jnp.sum(jnp.where((at >= 0) & (at < 3), lanes, 0.0), axis=1, keepdims=True)
    d = jnp.sum(jnp.where((at >= 3) & (at < 6), lanes, 0.0), axis=1, keepdims=True)
    return lse, d


def pack_stats(lse, d):
    rows = lse.shape[0]
    row, lane = iota((rows, 128), 0), iota((rows, 128), 1)
    at = jnp.where(lane // 8 == row % SLOTS, lane % 8, -1)
    spread = part_lanes(lse, d, at).reshape(rows // SLOTS, SLOTS, 128)
    total = jnp.sum(spread, axis=1, keepdims=True)
    return jnp.broadcast_to(total, spread.shape).reshape(rows, 128)


def unpack_stats(block):
    groups = block.shape[0]
    lanes = jnp.broadcast_to(block[:, STAT_SLOT : STAT_SLOT + 1, :], (groups, SLOTS, 128))
    lanes = lanes.reshape(groups * SLOTS, 128)
    row, lane = iota(lanes.shape, 0), iota(lanes.shape, 1)
    return read_parts(lanes, jnp.where(lane // 8 == row % SLOTS, lane % 8, -1))


def swap_halves(x):
    return pltpu.roll(x, FEAT, 1)


def group_offsets(near_ref, far_ref, first):
    index = iota((GSLOTS, 1), 0)
    near = jnp.zeros((GSLOTS, 1), jnp.int32)
    far = jnp.zeros((GSLOTS, 1), jnp.int32)
    for h in range(GROUP):
        here = index // SLOTS == h
        near = jnp.where(here, near_ref[first + h], near)
        far = jnp.where(here, far_ref[first + h], far)
    return near, far


def slot_rows(near_ref, far_ref, first):
    near, far = group_offsets(near_ref, far_ref, first)
    slot = iota((GSLOTS, 1), 0) % SLOTS
    row = jnp.where(slot < FAR_SLOT, near + NEAR_RATE * slot, jnp.where(slot == FAR_SLOT, far, -1))
    repeat = (slot == FAR_SLOT) & (far % NEAR_RATE == near)
    return row, repeat, slot


def head_mask():
    return iota((GSLOTS, GLANES), 1) // FEAT == iota((GSLOTS, GLANES), 0) // SLOTS


def softmax_terms(scores, allowed, weight_grads):
    masked = jnp.where(allowed, scores, LOW)
    top = jnp.max(masked, axis=1, keepdims=True)
    weights = jnp.where(allowed, jnp.exp(masked - top), 0.0)
    total = jnp.sum(weights, axis=1, keepdims=True)
    return top, total, jnp.sum(weights * weight_grads, axis=1, keepdims=True)


def merge_terms(lse, d, top, total, grad_total):
    overall = jnp.maximum(lse, top)
    old, new = jnp.exp(lse - overall), jnp.exp(top - overall)
    mass = old + new * total
    return overall + jnp.log(mass), (old * d + new * grad_total) / mass


OFFSET_SCRATCH = [
    pltpu.SMEM((HEADS,), jnp.int32),
    pltpu.SMEM((HEADS,), jnp.int32),
    pltpu.SemaphoreType.DMA((2,)),
]


def start_offsets(near_in, far_in, near_ref, far_ref, sems):
    copies = [
        pltpu.make_async_copy(near_in, near_ref, sems.at[0]),
        pltpu.make_async_copy(far_in, far_ref, sems.at[1]),
    ]
    for copy in copies:
        copy.start()
    return copies


def pick_matrix(row):
    return jnp.where(iota((GSLOTS, ROWS), 1) == row, 1.0, 0.0).astype(BF16)


def slot_stats(scores, row, grads, live):
    allowed = iota((GSLOTS, ROWS), 1) <= row
    masked = jnp.where(allowed, scores, LOW)
    top = jnp.max(masked, axis=1, keepdims=True)
    weights = jnp.where(allowed & live, jnp.exp(masked - top), 0.0)
    total = jnp.where(live, jnp.sum(weights, axis=1, keepdims=True), 1.0)
    scale = 1.0 / total
    d = jnp.sum(weights * grads, axis=1, keepdims=True) * scale
    return jnp.where(live, top + jnp.log(total), 0.0), d, weights * scale, grads - d


def start_copies(sources, base, count, buffer, sems):
    copies = []
    for b in range(count):
        here = pl.ds(b * GLANES, GLANES)
        there = pl.ds((base + b) * GLANES, GLANES)
        copies.append(
            [
                pltpu.make_async_copy(source.at[:, there], buffer.at[i, :, here], sems.at[b, i])
                for i, source in enumerate(sources)
            ]
        )
    for group in copies:
        for copy in group:
            copy.start()
    return copies


def start_whole(sources, buffer, sems):
    copies = [
        pltpu.make_async_copy(source, buffer.at[i], sems.at[i]) for i, source in enumerate(sources)
    ]
    for copy in copies:
        copy.start()
    return copies


def select_kernel(
    near_in, far_in, q_ref, k_ref, v_ref, g_ref, pay_ref, near_ref, far_ref, offset_sems, buffer, sems
):
    offset_copies = start_offsets(near_in, far_in, near_ref, far_ref, offset_sems)
    copies = start_whole((q_ref, g_ref, k_ref, v_ref), buffer, sems)
    for copy in offset_copies:
        copy.wait()
    groups = range(GROUPS)
    rows = [slot_rows(near_ref, far_ref, b * GROUP)[0] for b in groups]
    picks = [pick_matrix(row) for row in rows]
    mask = head_mask()
    lane = iota((GSLOTS, 128), 1)
    slot = iota((GSLOTS, 1), 0) % SLOTS

    def columns(i, b):
        return buffer[i, :, b * GLANES : (b + 1) * GLANES]

    def selected(i):
        copies[i].wait()
        return [jnp.where(mask, dot_nn(picks[b], columns(i, b)), 0.0) for b in groups]

    def folded(x):
        x = x[:, :128] + x[:, 128:]
        return x + swap_halves(x)

    qs, gs, ks = selected(0), selected(1), selected(2)
    scores = [dot_nt(qs[b].astype(BF16), columns(2, b)) * SCALE for b in groups]
    vs = selected(3)
    grads = [dot_nt(gs[b].astype(BF16), columns(3, b)) for b in groups]
    for b in groups:
        lse, d, _, _ = slot_stats(scores[b], rows[b], grads[b], slot <= FAR_SLOT)
        stats = pack_stats(lse, d)
        near, far = group_offsets(near_ref, far_ref, b * GROUP)
        stats = jnp.where(lane == NEAR_LANE, near, jnp.where(lane == FAR_LANE, far, stats))
        qk = jnp.where(lane < FEAT, folded(qs[b]), folded(ks[b]))
        vg = jnp.where(lane < FEAT, folded(vs[b]), folded(gs[b]))
        qk = jnp.where(slot == STAT_SLOT, stats, qk)
        block = jnp.concatenate(
            [qk.reshape(GROUP, SLOTS, 128), vg.reshape(GROUP, SLOTS, 128)], axis=1
        ).astype(BF16)
        pay_ref[0, b * GROUP : (b + 1) * GROUP] = block
        pay_ref[1, b * GROUP : (b + 1) * GROUP] = block


def select_call(near, far, q, k, v, g):
    hbm = pl.BlockSpec(memory_space=pltpu.HBM)
    vmem = pl.BlockSpec(memory_space=pltpu.VMEM)
    return pl.pallas_call(
        select_kernel,
        in_specs=[hbm] * 6,
        out_specs=vmem,
        out_shape=pltpu.VMEM((2, HEADS, 2 * SLOTS, 128), BF16),
        scratch_shapes=OFFSET_SCRATCH
        + [pltpu.VMEM((4, ROWS, WIDTH), BF16), pltpu.SemaphoreType.DMA((4,))],
        compiler_params=pltpu.CompilerParams(vmem_limit_bytes=VMEM_BYTES),
        name="select_rows",
    )(*pinned(pltpu.HBM, near, far, q, k, v, g))


def local_head(head, here, near_ref, far_ref, q, k, v, g):
    half = ROWS // 2
    query = iota((1, ROWS), 1)
    zero = jnp.zeros((), BF16)
    special = (query % NEAR_RATE == near_ref[head]) | (query == far_ref[head])
    kh, vh, qh, gh = (jnp.where(here, x, zero) for x in (k, v, q, g))
    triangle = iota((half, half), 0) <= iota((half, half), 1)
    top, bottom = dot_nt(kh[:half], q), dot_nt(kh[half:], q[half:])
    early, late = jnp.where(triangle, top[:, :half], LOW), top[:, half:]
    bottom = jnp.where(triangle, bottom, LOW)
    early_top = jnp.max(early, axis=0, keepdims=True)
    late_top = jnp.maximum(jnp.max(late, axis=0, keepdims=True), jnp.max(bottom, axis=0, keepdims=True))
    early, late, bottom = jnp.exp(early - early_top), jnp.exp(late - late_top), jnp.exp(bottom - late_top)
    early_total = jnp.sum(early, axis=0, keepdims=True)
    late_total = jnp.sum(late, axis=0, keepdims=True) + jnp.sum(bottom, axis=0, keepdims=True)
    scale = jnp.where(special, 0.0, 1.0 / jnp.concatenate([early_total, late_total], axis=1))
    grads, grads_b = dot_nt(vh[:half], g), dot_nt(vh[half:], g[half:])
    top = jnp.concatenate([early, late], axis=1) * scale
    bottom = bottom * scale[:, half:]
    delta = jnp.sum(top * grads, axis=0, keepdims=True)
    late_delta = delta[:, half:] + jnp.sum(bottom * grads_b, axis=0, keepdims=True)
    delta = jnp.concatenate([delta[:, :half], late_delta], axis=1)
    blank = jnp.zeros((half, half), BF16)

    def square(top, bottom):
        bottom = jnp.concatenate([blank, bottom.astype(BF16)], axis=1)
        return jnp.concatenate([top.astype(BF16), bottom], axis=0)

    dscores = square(top * (grads - delta), bottom * (grads_b - late_delta))
    return square(top, bottom), dscores, qh, kh, vh, gh


def joined(heads):
    weights, dscores, q, k, v, g = zip(*heads)
    over_keys = jnp.concatenate(weights, axis=0), jnp.concatenate(dscores, axis=0)
    over_queries = jnp.concatenate(weights, axis=1), jnp.concatenate(dscores, axis=1)
    out = dot_tn(over_keys[0], jnp.concatenate(v, axis=0))
    dq = dot_tn(over_keys[1], jnp.concatenate(k, axis=0)) * SCALE
    dk = dot_nn(over_queries[1], jnp.concatenate(q, axis=0))
    return out, dq, dk, dot_nn(over_queries[0], jnp.concatenate(g, axis=0))


def local_group(near_ref, far_ref, first, q, k, v, g):
    half = ROWS // 2
    query = iota((1, ROWS), 1)
    q = (q.astype(F32) * SCALE).astype(BF16)
    zero = jnp.zeros((), BF16)
    triangle = iota((half, half), 0) <= iota((half, half), 1)
    blank = jnp.zeros((half, half), BF16)
    lane = iota((1, GLANES), 1) // FEAT
    heads = [local_head(first + h, lane == h, near_ref, far_ref, q, k, v, g) for h in range(GROUP)]
    return joined(heads)


def slot_part(i, count=1):
    return slice(i * GSLOTS, (i + count) * GSLOTS)


def local_kernel(
    base, count, near_in, far_in, q_ref, k_ref, v_ref, g_ref, query_ref, key_ref, slot_ref,
    near_ref, far_ref, offset_sems, buffer, sems, *query_scratch
):
    offset_copies = start_offsets(near_in, far_in, near_ref, far_ref, offset_sems)
    start_copies((q_ref, k_ref, v_ref, g_ref), base, count, buffer, sems)
    for copy in offset_copies:
        copy.wait()
    mask = head_mask()

    query_buffer = query_scratch[0] if query_scratch else query_ref

    def query_copy(b):
        _, query_sems = query_scratch
        here = pl.ds(pl.multiple_of(b * GLANES, GLANES), GLANES)
        return pltpu.make_async_copy(query_buffer.at[:, :, here], query_ref.at[:, :, here], query_sems.at[b])

    def one_group(b, carry):
        here = pl.ds(pl.multiple_of(b * GLANES, GLANES), GLANES)
        for i, source in enumerate((q_ref, k_ref, v_ref, g_ref)):
            there = pl.ds(pl.multiple_of((base + b) * GLANES, GLANES), GLANES)
            pltpu.make_async_copy(source.at[:, there], buffer.at[i, :, here], sems.at[b, i]).wait()
        q, k, v, g = (buffer[i, :, here] for i in range(4))
        first = (base + b) * GROUP
        row, repeat, slot = slot_rows(near_ref, far_ref, first)
        pick = pick_matrix(row)
        qs = jnp.where(mask, dot_nn(pick, q), 0.0)
        gs = jnp.where(mask, dot_nn(pick, g), 0.0)
        live = (slot <= FAR_SLOT) & ~repeat
        scores = dot_nt(qs.astype(BF16), k) * SCALE
        grads = dot_nt(gs.astype(BF16), v)
        lse, d, weights, grads = slot_stats(scores, row, grads, live)
        dscores = (weights * grads).astype(BF16)
        weights = weights.astype(BF16)
        lane = iota((GSLOTS, GLANES), 1)
        parts = (
            weights,
            dscores,
            pick,
            (qs * SCALE).astype(BF16),
            gs.astype(BF16),
            jnp.where(mask, dot_nn(weights, v), 0.0).astype(BF16),
            (jnp.where(mask, dot_nn(dscores, k), 0.0) * SCALE).astype(BF16),
            (jnp.where(mask, dot_nn(weights, k), 0.0) * SCALE).astype(BF16),
        )
        for i, part in enumerate(parts):
            slot_ref[slot_part(i), here] = part
        key_ref[2 * ROWS :, here] = jnp.where(lane == 0, jnp.where(live, lse, LOW), d)
        out, dq, dk, dv = local_group(near_ref, far_ref, first, q, k, v, g)
        query_buffer[0, :, here] = out.astype(BF16)
        query_buffer[1, :, here] = dq.astype(BF16)
        if query_scratch:
            query_copy(b).start()
        key_ref[:ROWS, here] = dk
        key_ref[ROWS : 2 * ROWS, here] = dv
        return carry

    lax.fori_loop(0, count, one_group, 0)
    if query_scratch:
        for b in range(count):
            query_copy(b).wait()


def local_call(base, count, near, far, q, k, v, g, keep):
    hbm = pl.BlockSpec(memory_space=pltpu.HBM)
    vmem = pl.BlockSpec(memory_space=pltpu.VMEM)
    shape = (ROWS, count * GLANES)
    return pl.pallas_call(
        functools.partial(local_kernel, base, count),
        in_specs=[hbm] * 6,
        out_specs=[vmem if keep else hbm, vmem, vmem],
        out_shape=[
            (pltpu.VMEM if keep else pltpu.HBM)((2,) + shape, BF16),
            pltpu.VMEM((2 * ROWS + GSLOTS, count * GLANES), F32),
            pltpu.VMEM((SLOT_PARTS * GSLOTS, count * GLANES), BF16),
        ],
        scratch_shapes=OFFSET_SCRATCH
        + [pltpu.VMEM((4,) + shape, BF16), pltpu.SemaphoreType.DMA((count, 4))]
        + ([] if keep else [pltpu.VMEM((2,) + shape, BF16), pltpu.SemaphoreType.DMA((count,))]),
        compiler_params=pltpu.CompilerParams(vmem_limit_bytes=VMEM_BYTES),
        cost_estimate=pl.CostEstimate(
            flops=count * GROUP * 14 * ROWS * ROWS * FEAT,
            bytes_accessed=count * 7 * ROWS * GLANES * 2,
            transcendentals=count * GROUP * ROWS * ROWS,
        ),
        name="local_level",
    )(*pinned(pltpu.HBM, near, far, q, k, v, g))


def slot_positions(near, far):
    col = iota((SEQ * SLOTS, 1), 0)
    line = iota((1, SEQ * SLOTS), 1)

    def position(index):
        slot = index % SLOTS
        return index // SLOTS * ROWS + jnp.where(slot < FAR_SLOT, near + NEAR_RATE * slot, far)

    return col, line, position(col), position(line)


def pair_halves(qk, vg):
    low = iota(qk.shape, 1) < FEAT
    q0 = jnp.where(low, qk, 0.0)
    k0 = jnp.where(low, swap_halves(qk), 0.0)
    g0 = jnp.where(low, swap_halves(vg), 0.0)
    v0 = jnp.where(low, vg, 0.0)
    k1 = jnp.where(low, 0.0, qk)
    g1 = jnp.where(low, 0.0, vg)
    return tuple(x.astype(BF16) for x in (q0, k0, v0, g0, k1, g1))


def read_offsets(got):
    line = got[0, STAT_SLOT : STAT_SLOT + 1, :].astype(jnp.int32)
    return line[:, NEAR_LANE : NEAR_LANE + 1], line[:, FAR_LANE : FAR_LANE + 1]


def near_kernel(got_ref, send_ref, stat_ref):
    got = got_ref[...].astype(F32)
    near, far = read_offsets(got)
    qk, vg = got[:, :SLOTS].reshape(SEQ * SLOTS, 128), got[:, SLOTS:].reshape(SEQ * SLOTS, 128)
    lse, d = unpack_stats(got)
    q0, k0, v0, g0, _, _ = pair_halves(qk, vg)
    col, line, col_at, line_at = slot_positions(near, far)
    asks = (col % SLOTS < FAR_SLOT) | ((col % SLOTS == FAR_SLOT) & (far % NEAR_RATE == near))
    allowed = asks & (line % SLOTS < FAR_SLOT) & (line_at <= col_at)
    terms = softmax_terms(dot_nt(q0, k0) * SCALE, allowed, dot_nt(g0, v0))
    lse, d = merge_terms(lse, d, *terms)
    lane = iota((SEQ * SLOTS, 128), 1)
    stats = part_lanes(lse, d, lane)
    stat_ref[...] = stats
    rows = SEQ * SLOTS
    pick = iota((SEQ, rows), 1) == iota((SEQ, rows), 0) * SLOTS + FAR_SLOT
    pick = jnp.where(pick, 1.0, 0.0).astype(BF16)
    block = jnp.concatenate([dot_nn(pick, x.astype(BF16)) for x in (qk, vg, stats)], axis=0)
    block = block.astype(BF16)
    for o in range(OUTER):
        send_ref[o] = block


def near_call(got):
    return pl.pallas_call(
        near_kernel,
        in_specs=[pl.BlockSpec(memory_space=pltpu.VMEM)],
        out_specs=[pl.BlockSpec(memory_space=pltpu.VMEM)] * 2,
        out_shape=[
            pltpu.VMEM((OUTER, 3 * SEQ, 128), BF16),
            pltpu.VMEM((SEQ * SLOTS, 128), F32),
        ],
        compiler_params=pltpu.CompilerParams(vmem_limit_bytes=VMEM_BYTES),
        name="near_forward",
    )(got)


def level_grads(halves, scores, allowed, grads, lse, delta):
    q0, k0, v0, g0, k1, g1 = halves
    weights = jnp.where(allowed, jnp.exp(jnp.where(allowed, scores - lse, 0.0)), 0.0)
    dscores = (weights * (grads - delta)).astype(BF16)
    weights = weights.astype(BF16)
    query_side = dot_nn(weights, v0) + dot_nn(dscores, k1)
    key_side = dot_tn(dscores, q0) + dot_tn(weights, g1)
    low = iota((1, 128), 1) < FEAT
    return query_side * jnp.where(low, 1.0, SCALE), key_side * jnp.where(low, SCALE, 1.0)


def owner_kernel(got_ref, stat_ref, far_got_ref, send_ref):
    segment = lax.axis_index("outer")
    got = got_ref[...].astype(F32)
    near, far = read_offsets(got)
    rows = SEQ * SLOTS
    lane = iota((rows, 128), 1)

    far_qk = far_got_ref[:, :SEQ].reshape(rows, 128).astype(F32)
    far_vg = far_got_ref[:, SEQ : 2 * SEQ].reshape(rows, 128).astype(F32)
    far_stats = far_got_ref[:, 2 * SEQ :].reshape(rows, 128).astype(F32)
    far_halves = pair_halves(far_qk, far_vg)
    scores = dot_nt(far_halves[0], far_halves[1]) * SCALE
    grads = dot_nt(far_halves[3], far_halves[2])
    allowed = iota((rows, rows), 1) <= iota((rows, rows), 0)
    top, total, grad_total = softmax_terms(scores, allowed, grads)
    lse, delta = merge_terms(*read_parts(far_stats, lane), top, total, grad_total)
    query_side, key_side = level_grads(far_halves, scores, allowed, grads, lse, delta)
    own_stats = part_lanes(top + jnp.log(total), grad_total / total, lane).astype(BF16)

    row, column = iota((rows, rows), 0), iota((rows, rows), 1)
    own = column == segment * SEQ + row // SLOTS
    to_far = jnp.where(own & (row % SLOTS == FAR_SLOT), 1.0, 0.0).astype(BF16)
    to_all = jnp.where(own, 1.0, 0.0).astype(BF16)
    first = dot_nn(to_far, query_side.astype(BF16))
    second = dot_nn(to_far, key_side.astype(BF16))
    far_lse, far_d = read_parts(dot_nn(to_all, own_stats), lane)

    col, line, col_at, line_at = slot_positions(near, far)
    slot = col % SLOTS
    active = (slot == FAR_SLOT) | ((slot < FAR_SLOT) & (near + NEAR_RATE * slot == far))
    lse, d = read_parts(stat_ref[...], lane)
    merged_lse, merged_d = merge_terms(lse, d, far_lse, 1.0, far_d)
    lse, delta = jnp.where(active, merged_lse, lse), jnp.where(active, merged_d, d)

    halves = pair_halves(got[:, :SLOTS].reshape(rows, 128), got[:, SLOTS:].reshape(rows, 128))
    allowed = (slot < FAR_SLOT) & (line % SLOTS < FAR_SLOT) & (line_at <= col_at)
    query_side, key_side = level_grads(
        halves, dot_nt(halves[0], halves[1]) * SCALE, allowed, dot_nt(halves[3], halves[2]), lse, delta
    )
    first += query_side
    second += key_side
    used = slot <= FAR_SLOT
    stats = pack_stats(jnp.where(used, lse, 0.0), jnp.where(used, delta, 0.0))
    first = jnp.where(slot == STAT_SLOT, stats, first)
    send_ref[...] = jnp.concatenate(
        [first.reshape(SEQ, SLOTS, 128), second.reshape(SEQ, SLOTS, 128)], axis=1
    ).astype(BF16)


def owner_call(got, stats, far_got):
    vmem = pl.BlockSpec(memory_space=pltpu.VMEM)
    return pl.pallas_call(
        owner_kernel,
        in_specs=[vmem, vmem, vmem],
        out_specs=vmem,
        out_shape=pltpu.VMEM((SEQ, 2 * SLOTS, 128), BF16),
        compiler_params=pltpu.CompilerParams(vmem_limit_bytes=VMEM_BYTES),
        name="owner_level",
    )(got, stats, far_got)


def finish_kernel(got_ref, *refs):
    early, keys, slots, late = refs[0], (refs[1], refs[4]), (refs[2], refs[5]), refs[3]
    outs, (held, held_sem, results, out_sems) = refs[6:10], refs[10:]
    early_copy = pltpu.make_async_copy(early, held, held_sem)
    early_copy.start()
    mask = head_mask()
    low = iota((GSLOTS, 128), 1) < FEAT
    used = iota((GSLOTS, 128), 0) % SLOTS <= FAR_SLOT
    zero = jnp.zeros((GSLOTS, GLANES), F32)
    sends = []

    def finished(i, b, value):
        here = slice(b * GLANES, (b + 1) * GLANES)
        results[i, :, here] = value.astype(BF16)
        send = pltpu.make_async_copy(results.at[i, :, here], outs[i].at[:, here], out_sems.at[b, i])
        send.start()
        sends.append(send)

    def spread(x, keep_low):
        x = jnp.where(used & (low if keep_low else ~low), x, 0.0)
        x = x + swap_halves(x)
        return jnp.where(mask, jnp.concatenate([x, x], axis=1), 0.0)

    picked = []
    for b in range(GROUPS):
        got = got_ref[b * GROUP : (b + 1) * GROUP].astype(F32)
        lse, delta = unpack_stats(got)
        first = got[:, :SLOTS].reshape(GSLOTS, 128)
        second = got[:, SLOTS:].reshape(GSLOTS, 128)
        half, at = divmod(b, GROUPS // 2)
        there = slice(at * GLANES, (at + 1) * GLANES)
        key_part, slot_ref = keys[half], slots[half]
        qs, gs, out, dq, mean = (slot_ref[slot_part(i), there].astype(F32) for i in range(3, 8))
        stats = key_part[2 * ROWS :, there]
        factor = jnp.exp(stats[:, :1] - lse)
        shift = factor * (stats[:, 1:2] - delta)
        left = slot_ref[slot_part(0, 3), there]
        right = jnp.concatenate(
            [
                jnp.concatenate([shift * qs, factor * qs, spread(second, True)], axis=0),
                jnp.concatenate([factor * gs, zero, spread(second, False)], axis=0),
            ],
            axis=1,
        )
        sums = dot_tn(left, right.astype(BF16))
        finished(2, b, key_part[:ROWS, there] + sums[:, :GLANES])
        finished(3, b, key_part[ROWS : 2 * ROWS, there] + sums[:, GLANES:])
        out = factor * out + spread(first, True)
        dq = factor * dq + shift * mean + spread(first, False)
        right = jnp.concatenate([out, dq], axis=1).astype(BF16)
        picked.append((left[2 * GSLOTS :], right))
    for b in (2, 3, 0, 1):
        half, at = divmod(b, GROUPS // 2)
        there = slice(at * GLANES, (at + 1) * GLANES)
        if b == 0:
            early_copy.wait()
        query_part = late if half else held
        sums = dot_tn(*picked[b])
        finished(0, b, query_part[0, :, there].astype(F32) + sums[:, :GLANES])
        finished(1, b, query_part[1, :, there].astype(F32) + sums[:, GLANES:])
    for send in sends:
        send.wait()


def finish_call(got, parts):
    hbm = pl.BlockSpec(memory_space=pltpu.HBM)
    vmem = pl.BlockSpec(memory_space=pltpu.VMEM)
    return pl.pallas_call(
        finish_kernel,
        in_specs=[vmem, hbm] + [vmem] * 5,
        out_specs=[hbm] * 4,
        out_shape=[jax.ShapeDtypeStruct((ROWS, WIDTH), BF16)] * 4,
        scratch_shapes=[
            pltpu.VMEM((2, ROWS, WIDTH // 2), BF16),
            pltpu.SemaphoreType.DMA,
            pltpu.VMEM((4, ROWS, WIDTH), BF16),
            pltpu.SemaphoreType.DMA((GROUPS, 4)),
        ],
        compiler_params=pltpu.CompilerParams(vmem_limit_bytes=VMEM_BYTES),
        name="finish_rows",
    )(got, *pinned(pltpu.HBM, parts[0]), *parts[1:])


def exchange(x, axis):
    return lax.all_to_all(x, axis, split_axis=0, concat_axis=0, tiled=True)


def on_device(queries, keys, values, out_grad, near_offsets, far_offsets):
    arrays = (queries, keys, values, out_grad)
    half = GROUPS // 2
    pay = select_call(near_offsets, far_offsets, *arrays)
    got = exchange(pay.reshape(SEQ, 2 * SLOTS, 128), "seq")
    (near_1, far_1), _ = lax.optimization_barrier(((near_offsets, far_offsets), pay))
    parts = tuple(local_call(0, half, near_1, far_1, *arrays, False))
    got, parts = lax.optimization_barrier((got, parts))
    far_pay, stats = near_call(got)
    far_got = exchange(far_pay, "outer")
    back = owner_call(got, stats, far_got)
    (near_2, far_2), back = lax.optimization_barrier(((near_offsets, far_offsets), back))
    back_got = exchange(back, "seq")
    parts += tuple(local_call(half, GROUPS - half, near_2, far_2, *arrays, True))
    return finish_call(back_got, parts)


def solution(mesh):
    split = P(("outer", "seq"), None)
    return jax.shard_map(
        on_device,
        mesh=mesh,
        in_specs=(split, split, split, split, P(), P()),
        out_specs=(split, split, split, split),
        check_vma=False,
    )
```

```python
import functools

import jax
import jax.numpy as jnp
from jax import lax
from jax.experimental import pallas as pl
from jax.experimental.pallas import tpu as pltpu
from jax.sharding import PartitionSpec as P

HEADS = 16
FEAT = 64
ROWS = 256
WIDTH = 1024
NEAR_RATE = 64
FAR_RATE = 256
SEQ = 32
OUTER = 8
SLOTS = 8
FAR_SLOT = 4
STAT_SLOT = 5
NEAR_LANE = 48
FAR_LANE = 49
COPY_LANE = 50
GROUP = 4
GROUPS = HEADS // GROUP
GLANES = GROUP * FEAT
GSLOTS = GROUP * SLOTS
SCALE = FEAT**-0.5
LOW = -1e30
SLOT_PARTS = 5
TERMS = 4 * GSLOTS
F32 = jnp.float32
BF16 = jnp.bfloat16
VMEM_BYTES = 24 * 1024 * 1024


def pinned(space, *arrays):
    return tuple(pltpu.with_memory_space_constraint(x, space) for x in arrays)


def iota(shape, axis):
    return lax.broadcasted_iota(jnp.int32, shape, axis)


def dot_nn(a, b):
    return lax.dot_general(a, b, (((1,), (0,)), ((), ())), preferred_element_type=F32)


def dot_nt(a, b):
    return lax.dot_general(a, b, (((1,), (1,)), ((), ())), preferred_element_type=F32)


def dot_tn(a, b):
    return lax.dot_general(a, b, (((0,), (0,)), ((), ())), preferred_element_type=F32)


def parts_of(value):
    high = value.astype(BF16).astype(F32)
    rest = value - high
    middle = rest.astype(BF16).astype(F32)
    return high, middle, rest - middle


def part_lanes(lse, d, at):
    out = jnp.zeros((lse.shape[0], at.shape[1]), F32)
    for index, part in enumerate(parts_of(lse) + parts_of(d)):
        out = jnp.where(at == index, part, out)
    return out


def read_parts(lanes, at):
    lse = jnp.sum(jnp.where((at >= 0) & (at < 3), lanes, 0.0), axis=1, keepdims=True)
    d = jnp.sum(jnp.where((at >= 3) & (at < 6), lanes, 0.0), axis=1, keepdims=True)
    return lse, d


def pack_stats(lse, d):
    rows = lse.shape[0]
    row, lane = iota((rows, 128), 0), iota((rows, 128), 1)
    at = jnp.where(lane // 8 == row % SLOTS, lane % 8, -1)
    spread = part_lanes(lse, d, at).reshape(rows // SLOTS, SLOTS, 128)
    total = jnp.sum(spread, axis=1, keepdims=True)
    return jnp.broadcast_to(total, spread.shape).reshape(rows, 128)


def unpack_stats(block, at=STAT_SLOT):
    lanes = jnp.broadcast_to(block[:, at : at + 1, :], (block.shape[0], SLOTS, 128))
    lanes = lanes.reshape(block.shape[0] * SLOTS, 128)
    row, lane = iota(lanes.shape, 0), iota(lanes.shape, 1)
    return read_parts(lanes, jnp.where(lane // 8 == row % SLOTS, lane % 8, -1))


def swap_halves(x):
    return pltpu.roll(x, FEAT, 1)


def group_offsets(near_ref, far_ref, first):
    index = iota((GSLOTS, 1), 0)
    near = jnp.zeros((GSLOTS, 1), jnp.int32)
    far = jnp.zeros((GSLOTS, 1), jnp.int32)
    for h in range(GROUP):
        here = index // SLOTS == h
        near = jnp.where(here, near_ref[first + h], near)
        far = jnp.where(here, far_ref[first + h], far)
    return near, far


def slot_rows(near_ref, far_ref, first):
    near, far = group_offsets(near_ref, far_ref, first)
    slot = iota((GSLOTS, 1), 0) % SLOTS
    row = jnp.where(slot < FAR_SLOT, near + NEAR_RATE * slot, jnp.where(slot == FAR_SLOT, far, -1))
    repeat = (slot == FAR_SLOT) & (far % NEAR_RATE == near)
    return row, repeat, slot


def head_mask():
    return iota((GSLOTS, GLANES), 1) // FEAT == iota((GSLOTS, GLANES), 0) // SLOTS


def softmax_terms(scores, allowed, weight_grads):
    masked = jnp.where(allowed, scores, LOW)
    top = jnp.max(masked, axis=1, keepdims=True)
    weights = jnp.where(allowed, jnp.exp(masked - top), 0.0)
    total = jnp.sum(weights, axis=1, keepdims=True)
    return top, total, jnp.sum(weights * weight_grads, axis=1, keepdims=True)


def merge_terms(lse, d, top, total, grad_total):
    overall = jnp.maximum(lse, top)
    old, new = jnp.exp(lse - overall), jnp.exp(top - overall)
    mass = old + new * total
    return overall + jnp.log(mass), (old * d + new * grad_total) / mass


OFFSET_SCRATCH = [
    pltpu.SMEM((HEADS,), jnp.int32),
    pltpu.SMEM((HEADS,), jnp.int32),
    pltpu.SemaphoreType.DMA((2,)),
]


def start_offsets(near_in, far_in, near_ref, far_ref, sems):
    copies = [
        pltpu.make_async_copy(near_in, near_ref, sems.at[0]),
        pltpu.make_async_copy(far_in, far_ref, sems.at[1]),
    ]
    for copy in copies:
        copy.start()
    return copies


def pick_matrix(row):
    return jnp.where(iota((GSLOTS, ROWS), 1) == row, 1.0, 0.0).astype(BF16)


def slot_stats(scores, row, grads, live):
    allowed = iota((GSLOTS, ROWS), 1) <= row
    masked = jnp.where(allowed, scores, LOW)
    top = jnp.max(masked, axis=1, keepdims=True)
    weights = jnp.where(allowed & live, jnp.exp(masked - top), 0.0)
    total = jnp.where(live, jnp.sum(weights, axis=1, keepdims=True), 1.0)
    scale = 1.0 / total
    d = jnp.sum(weights * grads, axis=1, keepdims=True) * scale
    return jnp.where(live, top + jnp.log(total), 0.0), d, weights * scale, grads - d


def start_copies(sources, base, count, buffer, sems):
    copies = []
    for b in range(count):
        here = pl.ds(b * GLANES, GLANES)
        there = pl.ds((base + b) * GLANES, GLANES)
        copies.append(
            [
                pltpu.make_async_copy(source.at[:, there], buffer.at[i, :, here], sems.at[b, i])
                for i, source in enumerate(sources)
            ]
        )
    for group in copies:
        for copy in group:
            copy.start()
    return copies


def start_whole(sources, buffer, sems):
    copies = [
        pltpu.make_async_copy(source, buffer.at[i], sems.at[i]) for i, source in enumerate(sources)
    ]
    for copy in copies:
        copy.start()
    return copies


def select_kernel(
    near_in, far_in, q_ref, k_ref, v_ref, g_ref, pay_ref, near_ref, far_ref, offset_sems, buffer, sems
):
    offset_copies = start_offsets(near_in, far_in, near_ref, far_ref, offset_sems)
    copies = start_whole((q_ref, g_ref, k_ref, v_ref), buffer, sems)
    for copy in offset_copies:
        copy.wait()
    groups = range(GROUPS)
    rows = [slot_rows(near_ref, far_ref, b * GROUP)[0] for b in groups]
    picks = [pick_matrix(row) for row in rows]
    mask = head_mask()
    lane = iota((GSLOTS, 128), 1)
    slot = iota((GSLOTS, 1), 0) % SLOTS

    def columns(i, b):
        return buffer[i, :, b * GLANES : (b + 1) * GLANES]

    def selected(i):
        copies[i].wait()
        return [jnp.where(mask, dot_nn(picks[b], columns(i, b)), 0.0) for b in groups]

    def folded(x):
        x = x[:, :128] + x[:, 128:]
        return x + swap_halves(x)

    qs, gs, ks = selected(0), selected(1), selected(2)
    scores = [dot_nt(qs[b].astype(BF16), columns(2, b)) * SCALE for b in groups]
    vs = selected(3)
    grads = [dot_nt(gs[b].astype(BF16), columns(3, b)) for b in groups]
    for b in groups:
        lse, d, _, _ = slot_stats(scores[b], rows[b], grads[b], slot <= FAR_SLOT)
        stats = pack_stats(lse, d)
        near, far = group_offsets(near_ref, far_ref, b * GROUP)
        stats = jnp.where(lane == NEAR_LANE, near, jnp.where(lane == FAR_LANE, far, stats))
        qk = jnp.where(lane < FEAT, folded(qs[b]), folded(ks[b]))
        vg = jnp.where(lane < FEAT, folded(vs[b]), folded(gs[b]))
        qk = jnp.where(slot == STAT_SLOT, stats, qk)
        block = jnp.concatenate(
            [qk.reshape(GROUP, SLOTS, 128), vg.reshape(GROUP, SLOTS, 128)], axis=1
        ).astype(BF16)
        pay_ref[0, b * GROUP : (b + 1) * GROUP] = block
        mark = (iota(block.shape, 1) == STAT_SLOT) & (iota(block.shape, 2) == COPY_LANE)
        pay_ref[1, b * GROUP : (b + 1) * GROUP] = jnp.where(mark, jnp.ones((), BF16), block)


def select_call(near, far, q, k, v, g):
    hbm = pl.BlockSpec(memory_space=pltpu.HBM)
    vmem = pl.BlockSpec(memory_space=pltpu.VMEM)
    return pl.pallas_call(
        select_kernel,
        in_specs=[hbm] * 6,
        out_specs=vmem,
        out_shape=pltpu.VMEM((2, HEADS, 2 * SLOTS, 128), BF16),
        scratch_shapes=OFFSET_SCRATCH
        + [pltpu.VMEM((4, ROWS, WIDTH), BF16), pltpu.SemaphoreType.DMA((4,))],
        compiler_params=pltpu.CompilerParams(vmem_limit_bytes=VMEM_BYTES),
        name="select_rows",
    )(*pinned(pltpu.HBM, near, far, q, k, v, g))


def local_head(head, here, near_ref, far_ref, q, k, v, g):
    half = ROWS // 2
    query = iota((1, ROWS), 1)
    zero = jnp.zeros((), BF16)
    special = (query % NEAR_RATE == near_ref[head]) | (query == far_ref[head])
    kh, vh, qh, gh = (jnp.where(here, x, zero) for x in (k, v, q, g))
    triangle = iota((half, half), 0) <= iota((half, half), 1)
    top, bottom = dot_nt(kh[:half], q), dot_nt(kh[half:], q[half:])
    early, late = jnp.where(triangle, top[:, :half], LOW), top[:, half:]
    bottom = jnp.where(triangle, bottom, LOW)
    early_top = jnp.max(early, axis=0, keepdims=True)
    late_top = jnp.maximum(jnp.max(late, axis=0, keepdims=True), jnp.max(bottom, axis=0, keepdims=True))
    early, late, bottom = jnp.exp(early - early_top), jnp.exp(late - late_top), jnp.exp(bottom - late_top)
    early_total = jnp.sum(early, axis=0, keepdims=True)
    late_total = jnp.sum(late, axis=0, keepdims=True) + jnp.sum(bottom, axis=0, keepdims=True)
    scale = jnp.where(special, 0.0, 1.0 / jnp.concatenate([early_total, late_total], axis=1))
    grads, grads_b = dot_nt(vh[:half], g), dot_nt(vh[half:], g[half:])
    top = jnp.concatenate([early, late], axis=1) * scale
    bottom = bottom * scale[:, half:]
    delta = jnp.sum(top * grads, axis=0, keepdims=True)
    late_delta = delta[:, half:] + jnp.sum(bottom * grads_b, axis=0, keepdims=True)
    delta = jnp.concatenate([delta[:, :half], late_delta], axis=1)
    blank = jnp.zeros((half, half), BF16)

    def square(top, bottom):
        bottom = jnp.concatenate([blank, bottom.astype(BF16)], axis=1)
        return jnp.concatenate([top.astype(BF16), bottom], axis=0)

    dscores = square(top * (grads - delta), bottom * (grads_b - late_delta))
    return square(top, bottom), dscores, qh, kh, vh, gh


def joined(heads):
    weights, dscores, q, k, v, g = zip(*heads)
    over_keys = jnp.concatenate(weights, axis=0), jnp.concatenate(dscores, axis=0)
    over_queries = jnp.concatenate(weights, axis=1), jnp.concatenate(dscores, axis=1)
    out = dot_tn(over_keys[0], jnp.concatenate(v, axis=0))
    dq = dot_tn(over_keys[1], jnp.concatenate(k, axis=0)) * SCALE
    dk = dot_nn(over_queries[1], jnp.concatenate(q, axis=0))
    return out, dq, dk, dot_nn(over_queries[0], jnp.concatenate(g, axis=0))


def local_group(near_ref, far_ref, first, q, k, v, g):
    half = ROWS // 2
    query = iota((1, ROWS), 1)
    q = (q.astype(F32) * SCALE).astype(BF16)
    zero = jnp.zeros((), BF16)
    triangle = iota((half, half), 0) <= iota((half, half), 1)
    blank = jnp.zeros((half, half), BF16)
    lane = iota((1, GLANES), 1) // FEAT
    heads = [local_head(first + h, lane == h, near_ref, far_ref, q, k, v, g) for h in range(GROUP)]
    return joined(heads)


def slot_part(i, count=1):
    return slice(i * GSLOTS, (i + count) * GSLOTS)


def local_kernel(
    base, count, near_in, far_in, q_ref, k_ref, v_ref, g_ref, query_ref, key_ref, stat_ref, slot_ref,
    left_ref, place_ref, near_ref, far_ref, offset_sems, buffer, sems
):
    place_ref[...] = jnp.full(place_ref.shape, lax.axis_index("outer") * SEQ, jnp.int32)
    offset_copies = start_offsets(near_in, far_in, near_ref, far_ref, offset_sems)
    start_copies((q_ref, k_ref, v_ref, g_ref), base, count, buffer, sems)
    for copy in offset_copies:
        copy.wait()
    mask = head_mask()

    def one_group(b, carry):
        here = pl.ds(pl.multiple_of(b * GLANES, GLANES), GLANES)
        for i, source in enumerate((q_ref, k_ref, v_ref, g_ref)):
            there = pl.ds(pl.multiple_of((base + b) * GLANES, GLANES), GLANES)
            pltpu.make_async_copy(source.at[:, there], buffer.at[i, :, here], sems.at[b, i]).wait()
        q, k, v, g = (buffer[i, :, here] for i in range(4))
        first = (base + b) * GROUP
        row, repeat, slot = slot_rows(near_ref, far_ref, first)
        pick = pick_matrix(row)
        qs = jnp.where(mask, dot_nn(pick, q), 0.0)
        gs = jnp.where(mask, dot_nn(pick, g), 0.0)
        live = (slot <= FAR_SLOT) & ~repeat
        scores = dot_nt(qs.astype(BF16), k) * SCALE
        grads = dot_nt(gs.astype(BF16), v)
        lse, d, weights, grads = slot_stats(scores, row, grads, live)
        dscores = (weights * grads).astype(BF16)
        weights = weights.astype(BF16)
        lane = iota((GSLOTS, GLANES), 1)
        near, far = group_offsets(near_ref, far_ref, first)
        key_row = jnp.where(slot >= FAR_SLOT, near + NEAR_RATE * (slot - FAR_SLOT), -1)
        key_pick = pick_matrix(jnp.where(slot == 0, far, key_row))
        left = jnp.concatenate([weights, dscores, pick, key_pick], axis=0)
        left_ref[:, pl.ds(pl.multiple_of(b * TERMS, TERMS), TERMS)] = jnp.transpose(left)
        parts = (
            (qs * SCALE).astype(BF16),
            gs.astype(BF16),
            jnp.where(mask, dot_nn(weights, v), 0.0).astype(BF16),
            (jnp.where(mask, dot_nn(dscores, k), 0.0) * SCALE).astype(BF16),
            (jnp.where(mask, dot_nn(weights, k), 0.0) * SCALE).astype(BF16),
        )
        for i, part in enumerate(parts):
            slot_ref[slot_part(i), here] = part
        stat_ref[:, here] = jnp.where(lane == 0, jnp.where(live, lse, LOW), d)
        out, dq, dk, dv = local_group(near_ref, far_ref, first, q, k, v, g)
        query_ref[0, :, here] = out.astype(BF16)
        query_ref[1, :, here] = dq.astype(BF16)
        key_ref[0, :, here] = dk.astype(key_ref.dtype)
        key_ref[1, :, here] = dv.astype(key_ref.dtype)
        return carry

    lax.fori_loop(0, count, one_group, 0)


def local_call(base, count, near, far, q, k, v, g, key_type):
    hbm = pl.BlockSpec(memory_space=pltpu.HBM)
    vmem = pl.BlockSpec(memory_space=pltpu.VMEM)
    shape = (ROWS, count * GLANES)
    return pl.pallas_call(
        functools.partial(local_kernel, base, count),
        in_specs=[hbm] * 6,
        out_specs=[vmem] * 6,
        out_shape=[
            pltpu.VMEM((2,) + shape, BF16),
            pltpu.VMEM((2,) + shape, key_type),
            pltpu.VMEM((GSLOTS, count * GLANES), F32),
            pltpu.VMEM((SLOT_PARTS * GSLOTS, count * GLANES), BF16),
            pltpu.VMEM((ROWS, count * TERMS), BF16),
            pltpu.VMEM((8, 128), jnp.int32),
        ],
        scratch_shapes=OFFSET_SCRATCH
        + [pltpu.VMEM((4,) + shape, BF16), pltpu.SemaphoreType.DMA((count, 4))],
        compiler_params=pltpu.CompilerParams(vmem_limit_bytes=VMEM_BYTES),
        cost_estimate=pl.CostEstimate(
            flops=count * GROUP * 14 * ROWS * ROWS * FEAT,
            bytes_accessed=count * 7 * ROWS * GLANES * 2,
            transcendentals=count * GROUP * ROWS * ROWS,
        ),
        name="local_level",
    )(*pinned(pltpu.HBM, near, far, q, k, v, g))


def slot_positions(near, far):
    col = iota((SEQ * SLOTS, 1), 0)
    line = iota((1, SEQ * SLOTS), 1)

    def position(index):
        slot = index % SLOTS
        return index // SLOTS * ROWS + jnp.where(slot < FAR_SLOT, near + NEAR_RATE * slot, far)

    return col, line, position(col), position(line)


def pair_halves(qk, vg):
    low = iota(qk.shape, 1) < FEAT
    q0 = jnp.where(low, qk, 0.0)
    k0 = jnp.where(low, swap_halves(qk), 0.0)
    g0 = jnp.where(low, swap_halves(vg), 0.0)
    v0 = jnp.where(low, vg, 0.0)
    k1 = jnp.where(low, 0.0, qk)
    g1 = jnp.where(low, 0.0, vg)
    return tuple(x.astype(BF16) for x in (q0, k0, v0, g0, k1, g1))


def read_offsets(got):
    line = got[0, STAT_SLOT : STAT_SLOT + 1, :].astype(jnp.int32)
    return tuple(line[:, at : at + 1] for at in (NEAR_LANE, FAR_LANE, COPY_LANE))


def near_kernel(got_ref, send_ref, stat_ref):
    got = got_ref[...].astype(F32)
    near, far, _ = read_offsets(got)
    qk, vg = got[:, :SLOTS].reshape(SEQ * SLOTS, 128), got[:, SLOTS:].reshape(SEQ * SLOTS, 128)
    lse, d = unpack_stats(got)
    q0, k0, v0, g0, _, _ = pair_halves(qk, vg)
    col, line, col_at, line_at = slot_positions(near, far)
    asks = (col % SLOTS < FAR_SLOT) | ((col % SLOTS == FAR_SLOT) & (far % NEAR_RATE == near))
    allowed = asks & (line % SLOTS < FAR_SLOT) & (line_at <= col_at)
    terms = softmax_terms(dot_nt(q0, k0) * SCALE, allowed, dot_nt(g0, v0))
    lse, d = merge_terms(lse, d, *terms)
    lane = iota((SEQ * SLOTS, 128), 1)
    stats = part_lanes(lse, d, lane)
    stat_ref[...] = stats
    rows = SEQ * SLOTS
    pick = iota((SEQ, rows), 1) == iota((SEQ, rows), 0) * SLOTS + FAR_SLOT
    pick = jnp.where(pick, 1.0, 0.0).astype(BF16)
    block = jnp.concatenate([dot_nn(pick, x.astype(BF16)) for x in (qk, vg, stats)], axis=0)
    block = block.astype(BF16)
    for o in range(OUTER):
        send_ref[o] = block


def near_call(got):
    return pl.pallas_call(
        near_kernel,
        in_specs=[pl.BlockSpec(memory_space=pltpu.VMEM)],
        out_specs=[pl.BlockSpec(memory_space=pltpu.VMEM)] * 2,
        out_shape=[
            pltpu.VMEM((OUTER, 3 * SEQ, 128), BF16),
            pltpu.VMEM((SEQ * SLOTS, 128), F32),
        ],
        compiler_params=pltpu.CompilerParams(vmem_limit_bytes=VMEM_BYTES),
        name="near_forward",
    )(got)


def level_grads(halves, scores, allowed, grads, lse, delta):
    q0, k0, v0, g0, k1, g1 = halves
    weights = jnp.where(allowed, jnp.exp(jnp.where(allowed, scores - lse, 0.0)), 0.0)
    dscores = (weights * (grads - delta)).astype(BF16)
    weights = weights.astype(BF16)
    query_side = dot_nn(weights, v0) + dot_nn(dscores, k1)
    key_side = dot_tn(dscores, q0) + dot_tn(weights, g1)
    low = iota((1, 128), 1) < FEAT
    return query_side * jnp.where(low, 1.0, SCALE), key_side * jnp.where(low, SCALE, 1.0)


def owner_kernel(place_ref, got_ref, stat_ref, far_got_ref, send_ref):
    place = place_ref[:1, :1]
    got = got_ref[...].astype(F32)
    near, far, copy = read_offsets(got)
    rows = SEQ * SLOTS
    lane = iota((rows, 128), 1)

    far_qk = far_got_ref[:, :SEQ].reshape(rows, 128).astype(F32)
    far_vg = far_got_ref[:, SEQ : 2 * SEQ].reshape(rows, 128).astype(F32)
    far_stats = far_got_ref[:, 2 * SEQ :].reshape(rows, 128).astype(F32)
    far_halves = pair_halves(far_qk, far_vg)
    scores = dot_nt(far_halves[0], far_halves[1]) * SCALE
    grads = dot_nt(far_halves[3], far_halves[2])
    allowed = iota((rows, rows), 1) <= iota((rows, rows), 0)
    top, total, grad_total = softmax_terms(scores, allowed, grads)
    lse, delta = merge_terms(*read_parts(far_stats, lane), top, total, grad_total)
    query_side, key_side = level_grads(far_halves, scores, allowed, grads, lse, delta)
    own_stats = part_lanes(top + jnp.log(total), grad_total / total, lane).astype(BF16)

    row, column = iota((rows, rows), 0), iota((rows, rows), 1)
    own = column == place + row // SLOTS
    to_far = jnp.where(own & (row % SLOTS == FAR_SLOT), 1.0, 0.0).astype(BF16)
    to_all = jnp.where(own, 1.0, 0.0).astype(BF16)
    first = dot_nn(to_far, query_side.astype(BF16))
    second = dot_nn(to_far, key_side.astype(BF16))
    far_lse, far_d = read_parts(dot_nn(to_all, own_stats), lane)

    col, line, col_at, line_at = slot_positions(near, far)
    slot = col % SLOTS
    active = (slot == FAR_SLOT) | ((slot < FAR_SLOT) & (near + NEAR_RATE * slot == far))
    lse, d = read_parts(stat_ref[...], lane)
    merged_lse, merged_d = merge_terms(lse, d, far_lse, 1.0, far_d)
    lse, delta = jnp.where(active, merged_lse, lse), jnp.where(active, merged_d, d)

    halves = pair_halves(got[:, :SLOTS].reshape(rows, 128), got[:, SLOTS:].reshape(rows, 128))
    allowed = (slot < FAR_SLOT) & (line % SLOTS < FAR_SLOT) & (line_at <= col_at)
    query_side, key_side = level_grads(
        halves, dot_nt(halves[0], halves[1]) * SCALE, allowed, dot_nt(halves[3], halves[2]), lse, delta
    )
    first += query_side
    second += key_side
    used = slot <= FAR_SLOT
    stats = pack_stats(jnp.where(used, lse, 0.0), jnp.where(used, delta, 0.0))
    near_block = jnp.where(slot < FAR_SLOT, first, pltpu.roll(second, FAR_SLOT, 0))
    far_block = jnp.where(slot == 0, pltpu.roll(second, rows - FAR_SLOT, 0), stats)
    far_block = jnp.where(slot == FAR_SLOT, first, far_block)
    send_ref[...] = jnp.where(copy == 0, near_block, far_block).astype(BF16)


def owner_call(place, got, stats, far_got):
    vmem = pl.BlockSpec(memory_space=pltpu.VMEM)
    return pl.pallas_call(
        owner_kernel,
        in_specs=[vmem, vmem, vmem, vmem],
        out_specs=vmem,
        out_shape=pltpu.VMEM((SEQ * SLOTS, 128), BF16),
        compiler_params=pltpu.CompilerParams(vmem_limit_bytes=VMEM_BYTES),
        name="owner_level",
    )(place, got, stats, far_got)


def finish_kernel(got_ref, *refs):
    halves, outs, (results, out_sems) = (refs[:5], refs[5:10]), refs[10:14], refs[14:]
    mask = head_mask()
    low = iota((GSLOTS, 128), 1) < FEAT
    slot = iota((GSLOTS, 128), 0) % SLOTS
    zero = jnp.zeros((GSLOTS, GLANES), F32)
    sends = []

    def finished(i, b, value):
        results[i, :, b * GLANES : (b + 1) * GLANES] = value.astype(BF16)

    def send(arrays, first, count):
        here = slice(first * GLANES, (first + count) * GLANES)
        for i in arrays:
            copy = pltpu.make_async_copy(
                results.at[i, :, here], outs[i].at[:, here], out_sems.at[first, i]
            )
            copy.start()
            sends.append(copy)

    def spread(x):
        swapped = swap_halves(x)
        for half in (jnp.where(low, x, swapped), jnp.where(low, swapped, x)):
            yield jnp.where(mask, jnp.concatenate([half, half], axis=1), 0.0)

    for b in range(GROUPS):
        half, at = divmod(b, GROUPS // 2)
        there = slice(at * GLANES, (at + 1) * GLANES)
        query_part, key_part, stat_ref, slot_ref, left_ref = halves[half]
        near = got_ref[b * GSLOTS : (b + 1) * GSLOTS].astype(F32)
        far = got_ref[HEADS * SLOTS + b * GSLOTS : HEADS * SLOTS + (b + 1) * GSLOTS].astype(F32)
        lse, delta = unpack_stats(far.reshape(GROUP, SLOTS, 128), 2)
        query_side = tuple(spread(jnp.where(slot < FAR_SLOT, near, far)))
        key_side = tuple(spread(jnp.where(slot < FAR_SLOT, far, near)))
        qs, gs, out, dq, mean = (slot_ref[slot_part(i), there].astype(F32) for i in range(5))
        stats = stat_ref[:, there]
        factor = jnp.exp(stats[:, :1] - lse)
        shift = factor * (stats[:, 1:2] - delta)
        out = factor * out + query_side[0]
        dq = factor * dq + shift * mean + query_side[1]
        right = (
            (zero, zero, shift * qs, factor * gs),
            (zero, zero, factor * qs, zero),
            (out, dq, zero, zero),
            (zero, zero) + key_side,
        )
        right = jnp.concatenate([jnp.concatenate(x, axis=1) for x in right], axis=0)
        sums = dot_nn(left_ref[:, at * TERMS : (at + 1) * TERMS], right.astype(BF16))
        if b:
            send((0, 1, 2, 3), b - 1, 1)
        for i in range(4):
            bulk = (query_part if i < 2 else key_part)[i % 2, :, there].astype(F32)
            finished(i, b, bulk + sums[:, i * GLANES : (i + 1) * GLANES])
    send((0, 1, 2, 3), 3, 1)
    for copy in sends:
        copy.wait()


def finish_call(got, parts):
    hbm = pl.BlockSpec(memory_space=pltpu.HBM)
    vmem = pl.BlockSpec(memory_space=pltpu.VMEM)
    return pl.pallas_call(
        finish_kernel,
        in_specs=[vmem] * 11,
        out_specs=[hbm] * 4,
        out_shape=[jax.ShapeDtypeStruct((ROWS, WIDTH), BF16)] * 4,
        scratch_shapes=[
            pltpu.VMEM((4, ROWS, WIDTH), BF16),
            pltpu.SemaphoreType.DMA((GROUPS, 4)),
        ],
        compiler_params=pltpu.CompilerParams(vmem_limit_bytes=VMEM_BYTES),
        name="finish_rows",
    )(got, *parts)


def exchange(x, axis):
    return lax.all_to_all(x, axis, split_axis=0, concat_axis=0, tiled=True)


def on_device(queries, keys, values, out_grad, near_offsets, far_offsets):
    arrays = (queries, keys, values, out_grad)
    half = GROUPS // 2
    pay = select_call(near_offsets, far_offsets, *arrays)
    got = exchange(pay.reshape(SEQ, 2 * SLOTS, 128), "seq")
    (near_1, far_1), _ = lax.optimization_barrier(((near_offsets, far_offsets), pay))
    *parts, place = local_call(0, half, near_1, far_1, *arrays, BF16)
    got, parts, place = lax.optimization_barrier((got, parts, place))
    far_pay, stats = near_call(got)
    far_got = exchange(far_pay, "outer")
    back = owner_call(place, got, stats, far_got)
    (near_2, far_2), back = lax.optimization_barrier(((near_offsets, far_offsets), back))
    back_got = exchange(back, "seq")
    parts += local_call(half, GROUPS - half, near_2, far_2, *arrays, F32)[:-1]
    return finish_call(back_got, parts)


def solution(mesh):
    split = P(("outer", "seq"), None)
    return jax.shard_map(
        on_device,
        mesh=mesh,
        in_specs=(split, split, split, split, P(), P()),
        out_specs=(split, split, split, split),
        check_vma=False,
    )
```

```python
import functools

import jax
import jax.numpy as jnp
from jax import lax
from jax.experimental import pallas as pl
from jax.experimental.pallas import tpu as pltpu
from jax.sharding import PartitionSpec as P

HEADS = 16
FEAT = 64
ROWS = 256
WIDTH = 1024
NEAR_RATE = 64
FAR_RATE = 256
SEQ = 32
OUTER = 8
SLOTS = 8
FAR_SLOT = 4
STAT_SLOT = 5
NEAR_LANE = 48
FAR_LANE = 49
COPY_LANE = 50
GROUP = 4
GROUPS = HEADS // GROUP
EARLY = 0
GLANES = GROUP * FEAT
GSLOTS = GROUP * SLOTS
SCALE = FEAT**-0.5
LOW = -1e30
SLOT_PARTS = 5
TERMS = 4 * GSLOTS
F32 = jnp.float32
BF16 = jnp.bfloat16
VMEM_BYTES = 24 * 1024 * 1024


def pinned(space, *arrays):
    return tuple(pltpu.with_memory_space_constraint(x, space) for x in arrays)


def iota(shape, axis):
    return lax.broadcasted_iota(jnp.int32, shape, axis)


def dot_nn(a, b):
    return lax.dot_general(a, b, (((1,), (0,)), ((), ())), preferred_element_type=F32)


def dot_nt(a, b):
    return lax.dot_general(a, b, (((1,), (1,)), ((), ())), preferred_element_type=F32)


def dot_tn(a, b):
    return lax.dot_general(a, b, (((0,), (0,)), ((), ())), preferred_element_type=F32)


def parts_of(value):
    high = value.astype(BF16).astype(F32)
    rest = value - high
    middle = rest.astype(BF16).astype(F32)
    return high, middle, rest - middle


def part_lanes(lse, d, at):
    out = jnp.zeros((lse.shape[0], at.shape[1]), F32)
    for index, part in enumerate(parts_of(lse) + parts_of(d)):
        out = jnp.where(at == index, part, out)
    return out


def read_parts(lanes, at):
    lse = jnp.sum(jnp.where((at >= 0) & (at < 3), lanes, 0.0), axis=1, keepdims=True)
    d = jnp.sum(jnp.where((at >= 3) & (at < 6), lanes, 0.0), axis=1, keepdims=True)
    return lse, d


def pack_stats(lse, d):
    rows = lse.shape[0]
    row, lane = iota((rows, 128), 0), iota((rows, 128), 1)
    at = jnp.where(lane // 8 == row % SLOTS, lane % 8, -1)
    spread = part_lanes(lse, d, at).reshape(rows // SLOTS, SLOTS, 128)
    total = jnp.sum(spread, axis=1, keepdims=True)
    return jnp.broadcast_to(total, spread.shape).reshape(rows, 128)


def unpack_stats(block, at=STAT_SLOT):
    lanes = jnp.broadcast_to(block[:, at : at + 1, :], (block.shape[0], SLOTS, 128))
    lanes = lanes.reshape(block.shape[0] * SLOTS, 128)
    row, lane = iota(lanes.shape, 0), iota(lanes.shape, 1)
    return read_parts(lanes, jnp.where(lane // 8 == row % SLOTS, lane % 8, -1))


def swap_halves(x):
    return pltpu.roll(x, FEAT, 1)


def group_offsets(near_ref, far_ref, first):
    index = iota((GSLOTS, 1), 0)
    near = jnp.zeros((GSLOTS, 1), jnp.int32)
    far = jnp.zeros((GSLOTS, 1), jnp.int32)
    for h in range(GROUP):
        here = index // SLOTS == h
        near = jnp.where(here, near_ref[first + h], near)
        far = jnp.where(here, far_ref[first + h], far)
    return near, far


def slot_rows(near_ref, far_ref, first):
    near, far = group_offsets(near_ref, far_ref, first)
    slot = iota((GSLOTS, 1), 0) % SLOTS
    row = jnp.where(slot < FAR_SLOT, near + NEAR_RATE * slot, jnp.where(slot == FAR_SLOT, far, -1))
    repeat = (slot == FAR_SLOT) & (far % NEAR_RATE == near)
    return row, repeat, slot


def head_mask():
    return iota((GSLOTS, GLANES), 1) // FEAT == iota((GSLOTS, GLANES), 0) // SLOTS


def softmax_terms(scores, allowed, weight_grads):
    masked = jnp.where(allowed, scores, LOW)
    top = jnp.max(masked, axis=1, keepdims=True)
    weights = jnp.where(allowed, jnp.exp(masked - top), 0.0)
    total = jnp.sum(weights, axis=1, keepdims=True)
    return top, total, jnp.sum(weights * weight_grads, axis=1, keepdims=True)


def merge_terms(lse, d, top, total, grad_total):
    overall = jnp.maximum(lse, top)
    old, new = jnp.exp(lse - overall), jnp.exp(top - overall)
    mass = old + new * total
    return overall + jnp.log(mass), (old * d + new * grad_total) / mass


OFFSET_SCRATCH = [
    pltpu.SMEM((HEADS,), jnp.int32),
    pltpu.SMEM((HEADS,), jnp.int32),
    pltpu.SemaphoreType.DMA((2,)),
]


def start_offsets(near_in, far_in, near_ref, far_ref, sems):
    copies = [
        pltpu.make_async_copy(near_in, near_ref, sems.at[0]),
        pltpu.make_async_copy(far_in, far_ref, sems.at[1]),
    ]
    for copy in copies:
        copy.start()
    return copies


def pick_matrix(row):
    return jnp.where(iota((GSLOTS, ROWS), 1) == row, 1.0, 0.0).astype(BF16)


def slot_stats(scores, row, grads, live):
    allowed = iota((GSLOTS, ROWS), 1) <= row
    masked = jnp.where(allowed, scores, LOW)
    top = jnp.max(masked, axis=1, keepdims=True)
    weights = jnp.where(allowed & live, jnp.exp(masked - top), 0.0)
    total = jnp.where(live, jnp.sum(weights, axis=1, keepdims=True), 1.0)
    scale = 1.0 / total
    d = jnp.sum(weights * grads, axis=1, keepdims=True) * scale
    return jnp.where(live, top + jnp.log(total), 0.0), d, weights * scale, grads - d


def start_copies(sources, base, count, buffer, sems):
    copies = []
    for b in range(count):
        here = pl.ds(b * GLANES, GLANES)
        there = pl.ds((base + b) * GLANES, GLANES)
        copies.append(
            [
                pltpu.make_async_copy(source.at[:, there], buffer.at[i, :, here], sems.at[b, i])
                for i, source in enumerate(sources)
            ]
        )
    for group in copies:
        for copy in group:
            copy.start()
    return copies


def start_whole(sources, buffer, sems):
    copies = [
        pltpu.make_async_copy(source, buffer.at[i], sems.at[i]) for i, source in enumerate(sources)
    ]
    for copy in copies:
        copy.start()
    return copies


def select_kernel(
    near_in, far_in, q_ref, k_ref, v_ref, g_ref, pay_ref, near_ref, far_ref, offset_sems, buffer, sems
):
    offset_copies = start_offsets(near_in, far_in, near_ref, far_ref, offset_sems)
    copies = start_whole((q_ref, g_ref, k_ref, v_ref), buffer, sems)
    for copy in offset_copies:
        copy.wait()
    groups = range(GROUPS)
    rows = [slot_rows(near_ref, far_ref, b * GROUP)[0] for b in groups]
    picks = [pick_matrix(row) for row in rows]
    mask = head_mask()
    lane = iota((GSLOTS, 128), 1)
    slot = iota((GSLOTS, 1), 0) % SLOTS

    def columns(i, b):
        return buffer[i, :, b * GLANES : (b + 1) * GLANES]

    def selected(i):
        copies[i].wait()
        return [jnp.where(mask, dot_nn(picks[b], columns(i, b)), 0.0) for b in groups]

    def folded(x):
        x = x[:, :128] + x[:, 128:]
        return x + swap_halves(x)

    qs, gs, ks = selected(0), selected(1), selected(2)
    scores = [dot_nt(qs[b].astype(BF16), columns(2, b)) * SCALE for b in groups]
    vs = selected(3)
    grads = [dot_nt(gs[b].astype(BF16), columns(3, b)) for b in groups]
    for b in groups:
        lse, d, _, _ = slot_stats(scores[b], rows[b], grads[b], slot <= FAR_SLOT)
        stats = pack_stats(lse, d)
        near, far = group_offsets(near_ref, far_ref, b * GROUP)
        stats = jnp.where(lane == NEAR_LANE, near, jnp.where(lane == FAR_LANE, far, stats))
        qk = jnp.where(lane < FEAT, folded(qs[b]), folded(ks[b]))
        vg = jnp.where(lane < FEAT, folded(vs[b]), folded(gs[b]))
        qk = jnp.where(slot == STAT_SLOT, stats, qk)
        block = jnp.concatenate(
            [qk.reshape(GROUP, SLOTS, 128), vg.reshape(GROUP, SLOTS, 128)], axis=1
        ).astype(BF16)
        pay_ref[0, b * GROUP : (b + 1) * GROUP] = block
        mark = (iota(block.shape, 1) == STAT_SLOT) & (iota(block.shape, 2) == COPY_LANE)
        pay_ref[1, b * GROUP : (b + 1) * GROUP] = jnp.where(mark, jnp.ones((), BF16), block)


def select_call(near, far, q, k, v, g):
    hbm = pl.BlockSpec(memory_space=pltpu.HBM)
    vmem = pl.BlockSpec(memory_space=pltpu.VMEM)
    return pl.pallas_call(
        select_kernel,
        in_specs=[hbm] * 6,
        out_specs=vmem,
        out_shape=pltpu.VMEM((2, HEADS, 2 * SLOTS, 128), BF16),
        scratch_shapes=OFFSET_SCRATCH
        + [pltpu.VMEM((4, ROWS, WIDTH), BF16), pltpu.SemaphoreType.DMA((4,))],
        compiler_params=pltpu.CompilerParams(vmem_limit_bytes=VMEM_BYTES),
        name="select_rows",
    )(*pinned(pltpu.HBM, near, far, q, k, v, g))


def local_head(head, here, near_ref, far_ref, q, k, v, g):
    half = ROWS // 2
    query = iota((1, ROWS), 1)
    zero = jnp.zeros((), BF16)
    special = (query % NEAR_RATE == near_ref[head]) | (query == far_ref[head])
    kh, vh, qh, gh = (jnp.where(here, x, zero) for x in (k, v, q, g))
    triangle = iota((half, half), 0) <= iota((half, half), 1)
    top, bottom = dot_nt(kh[:half], q), dot_nt(kh[half:], q[half:])
    early, late = jnp.where(triangle, top[:, :half], LOW), top[:, half:]
    bottom = jnp.where(triangle, bottom, LOW)
    early_top = jnp.max(early, axis=0, keepdims=True)
    late_top = jnp.maximum(jnp.max(late, axis=0, keepdims=True), jnp.max(bottom, axis=0, keepdims=True))
    early, late, bottom = jnp.exp(early - early_top), jnp.exp(late - late_top), jnp.exp(bottom - late_top)
    early_total = jnp.sum(early, axis=0, keepdims=True)
    late_total = jnp.sum(late, axis=0, keepdims=True) + jnp.sum(bottom, axis=0, keepdims=True)
    scale = jnp.where(special, 0.0, 1.0 / jnp.concatenate([early_total, late_total], axis=1))
    grads, grads_b = dot_nt(vh[:half], g), dot_nt(vh[half:], g[half:])
    top = jnp.concatenate([early, late], axis=1) * scale
    bottom = bottom * scale[:, half:]
    delta = jnp.sum(top * grads, axis=0, keepdims=True)
    late_delta = delta[:, half:] + jnp.sum(bottom * grads_b, axis=0, keepdims=True)
    delta = jnp.concatenate([delta[:, :half], late_delta], axis=1)
    blank = jnp.zeros((half, half), BF16)

    def square(top, bottom):
        bottom = jnp.concatenate([blank, bottom.astype(BF16)], axis=1)
        return jnp.concatenate([top.astype(BF16), bottom], axis=0)

    dscores = square(top * (grads - delta), bottom * (grads_b - late_delta))
    return square(top, bottom), dscores, qh, kh, vh, gh


def joined(heads):
    weights, dscores, q, k, v, g = zip(*heads)
    over_keys = jnp.concatenate(weights, axis=0), jnp.concatenate(dscores, axis=0)
    over_queries = jnp.concatenate(weights, axis=1), jnp.concatenate(dscores, axis=1)
    out = dot_tn(over_keys[0], jnp.concatenate(v, axis=0))
    dq = dot_tn(over_keys[1], jnp.concatenate(k, axis=0)) * SCALE
    dk = dot_nn(over_queries[1], jnp.concatenate(q, axis=0))
    return out, dq, dk, dot_nn(over_queries[0], jnp.concatenate(g, axis=0))


def local_group(near_ref, far_ref, first, q, k, v, g):
    half = ROWS // 2
    query = iota((1, ROWS), 1)
    q = (q.astype(F32) * SCALE).astype(BF16)
    zero = jnp.zeros((), BF16)
    triangle = iota((half, half), 0) <= iota((half, half), 1)
    blank = jnp.zeros((half, half), BF16)
    lane = iota((1, GLANES), 1) // FEAT
    heads = [local_head(first + h, lane == h, near_ref, far_ref, q, k, v, g) for h in range(GROUP)]
    return joined(heads)


def slot_part(i, count=1):
    return slice(i * GSLOTS, (i + count) * GSLOTS)


def local_kernel(
    base, count, near_in, far_in, q_ref, k_ref, v_ref, g_ref, query_ref, key_ref, stat_ref, slot_ref,
    left_ref, near_ref, far_ref, offset_sems, buffer, sems
):
    offset_copies = start_offsets(near_in, far_in, near_ref, far_ref, offset_sems)
    start_copies((q_ref, k_ref, v_ref, g_ref), base, count, buffer, sems)
    for copy in offset_copies:
        copy.wait()
    mask = head_mask()

    def one_group(b, carry):
        here = pl.ds(pl.multiple_of(b * GLANES, GLANES), GLANES)
        for i, source in enumerate((q_ref, k_ref, v_ref, g_ref)):
            there = pl.ds(pl.multiple_of((base + b) * GLANES, GLANES), GLANES)
            pltpu.make_async_copy(source.at[:, there], buffer.at[i, :, here], sems.at[b, i]).wait()
        q, k, v, g = (buffer[i, :, here] for i in range(4))
        first = (base + b) * GROUP
        row, repeat, slot = slot_rows(near_ref, far_ref, first)
        pick = pick_matrix(row)
        qs = jnp.where(mask, dot_nn(pick, q), 0.0)
        gs = jnp.where(mask, dot_nn(pick, g), 0.0)
        live = (slot <= FAR_SLOT) & ~repeat
        scores = dot_nt(qs.astype(BF16), k) * SCALE
        grads = dot_nt(gs.astype(BF16), v)
        lse, d, weights, grads = slot_stats(scores, row, grads, live)
        dscores = (weights * grads).astype(BF16)
        weights = weights.astype(BF16)
        lane = iota((GSLOTS, GLANES), 1)
        near, far = group_offsets(near_ref, far_ref, first)
        key_row = jnp.where(slot >= FAR_SLOT, near + NEAR_RATE * (slot - FAR_SLOT), -1)
        key_pick = pick_matrix(jnp.where(slot == 0, far, key_row))
        left = jnp.concatenate([weights, dscores, pick, key_pick], axis=0)
        left_ref[:, pl.ds(pl.multiple_of(b * TERMS, TERMS), TERMS)] = jnp.transpose(left)
        parts = (
            (qs * SCALE).astype(BF16),
            gs.astype(BF16),
            jnp.where(mask, dot_nn(weights, v), 0.0).astype(BF16),
            (jnp.where(mask, dot_nn(dscores, k), 0.0) * SCALE).astype(BF16),
            (jnp.where(mask, dot_nn(weights, k), 0.0) * SCALE).astype(BF16),
        )
        for i, part in enumerate(parts):
            slot_ref[slot_part(i), here] = part
        stat_ref[:, here] = jnp.where(lane == 0, jnp.where(live, lse, LOW), d)
        out, dq, dk, dv = local_group(near_ref, far_ref, first, q, k, v, g)
        query_ref[0, :, here] = out.astype(BF16)
        query_ref[1, :, here] = dq.astype(BF16)
        key_ref[0, :, here] = dk.astype(key_ref.dtype)
        key_ref[1, :, here] = dv.astype(key_ref.dtype)
        return carry

    lax.fori_loop(0, count, one_group, 0)


def local_call(base, count, near, far, q, k, v, g, key_type):
    hbm = pl.BlockSpec(memory_space=pltpu.HBM)
    vmem = pl.BlockSpec(memory_space=pltpu.VMEM)
    shape = (ROWS, count * GLANES)
    return pl.pallas_call(
        functools.partial(local_kernel, base, count),
        in_specs=[hbm] * 6,
        out_specs=[vmem] * 5,
        out_shape=[
            pltpu.VMEM((2,) + shape, BF16),
            pltpu.VMEM((2,) + shape, key_type),
            pltpu.VMEM((GSLOTS, count * GLANES), F32),
            pltpu.VMEM((SLOT_PARTS * GSLOTS, count * GLANES), BF16),
            pltpu.VMEM((ROWS, count * TERMS), BF16),
        ],
        scratch_shapes=OFFSET_SCRATCH
        + [pltpu.VMEM((4,) + shape, BF16), pltpu.SemaphoreType.DMA((count, 4))],
        compiler_params=pltpu.CompilerParams(vmem_limit_bytes=VMEM_BYTES),
        cost_estimate=pl.CostEstimate(
            flops=count * GROUP * 14 * ROWS * ROWS * FEAT,
            bytes_accessed=count * 7 * ROWS * GLANES * 2,
            transcendentals=count * GROUP * ROWS * ROWS,
        ),
        name="local_level",
    )(*pinned(pltpu.HBM, near, far, q, k, v, g))


def slot_positions(near, far):
    col = iota((SEQ * SLOTS, 1), 0)
    line = iota((1, SEQ * SLOTS), 1)

    def position(index):
        slot = index % SLOTS
        return index // SLOTS * ROWS + jnp.where(slot < FAR_SLOT, near + NEAR_RATE * slot, far)

    return col, line, position(col), position(line)


def pair_halves(qk, vg):
    low = iota(qk.shape, 1) < FEAT
    q0 = jnp.where(low, qk, 0.0)
    k0 = jnp.where(low, swap_halves(qk), 0.0)
    g0 = jnp.where(low, swap_halves(vg), 0.0)
    v0 = jnp.where(low, vg, 0.0)
    k1 = jnp.where(low, 0.0, qk)
    g1 = jnp.where(low, 0.0, vg)
    return tuple(x.astype(BF16) for x in (q0, k0, v0, g0, k1, g1))


def read_offsets(got):
    line = got[0, STAT_SLOT : STAT_SLOT + 1, :].astype(jnp.int32)
    return tuple(line[:, at : at + 1] for at in (NEAR_LANE, FAR_LANE, COPY_LANE))


def near_kernel(got_ref, send_ref, stat_ref):
    got = got_ref[...].astype(F32)
    near, far, _ = read_offsets(got)
    qk, vg = got[:, :SLOTS].reshape(SEQ * SLOTS, 128), got[:, SLOTS:].reshape(SEQ * SLOTS, 128)
    lse, d = unpack_stats(got)
    q0, k0, v0, g0, _, _ = pair_halves(qk, vg)
    col, line, col_at, line_at = slot_positions(near, far)
    asks = (col % SLOTS < FAR_SLOT) | ((col % SLOTS == FAR_SLOT) & (far % NEAR_RATE == near))
    allowed = asks & (line % SLOTS < FAR_SLOT) & (line_at <= col_at)
    terms = softmax_terms(dot_nt(q0, k0) * SCALE, allowed, dot_nt(g0, v0))
    lse, d = merge_terms(lse, d, *terms)
    lane = iota((SEQ * SLOTS, 128), 1)
    stats = part_lanes(lse, d, lane)
    stat_ref[...] = stats
    rows = SEQ * SLOTS
    pick = iota((SEQ, rows), 1) == iota((SEQ, rows), 0) * SLOTS + FAR_SLOT
    pick = jnp.where(pick, 1.0, 0.0).astype(BF16)
    block = jnp.concatenate([dot_nn(pick, x.astype(BF16)) for x in (qk, vg, stats)], axis=0)
    block = block.astype(BF16)
    for o in range(OUTER):
        send_ref[o] = block


def near_call(got):
    return pl.pallas_call(
        near_kernel,
        in_specs=[pl.BlockSpec(memory_space=pltpu.VMEM)],
        out_specs=[pl.BlockSpec(memory_space=pltpu.VMEM)] * 2,
        out_shape=[
            pltpu.VMEM((OUTER, 3 * SEQ, 128), BF16),
            pltpu.VMEM((SEQ * SLOTS, 128), F32),
        ],
        compiler_params=pltpu.CompilerParams(vmem_limit_bytes=VMEM_BYTES),
        name="near_forward",
    )(got)


def level_grads(halves, scores, allowed, grads, lse, delta):
    q0, k0, v0, g0, k1, g1 = halves
    weights = jnp.where(allowed, jnp.exp(jnp.where(allowed, scores - lse, 0.0)), 0.0)
    dscores = (weights * (grads - delta)).astype(BF16)
    weights = weights.astype(BF16)
    query_side = dot_nn(weights, v0) + dot_nn(dscores, k1)
    key_side = dot_tn(dscores, q0) + dot_tn(weights, g1)
    low = iota((1, 128), 1) < FEAT
    return query_side * jnp.where(low, 1.0, SCALE), key_side * jnp.where(low, SCALE, 1.0)


def owner_kernel(got_ref, stat_ref, far_got_ref, send_ref):
    place = lax.axis_index("outer") * SEQ
    got = got_ref[...].astype(F32)
    near, far, copy = read_offsets(got)
    rows = SEQ * SLOTS
    lane = iota((rows, 128), 1)

    far_qk = far_got_ref[:, :SEQ].reshape(rows, 128).astype(F32)
    far_vg = far_got_ref[:, SEQ : 2 * SEQ].reshape(rows, 128).astype(F32)
    far_stats = far_got_ref[:, 2 * SEQ :].reshape(rows, 128).astype(F32)
    far_halves = pair_halves(far_qk, far_vg)
    scores = dot_nt(far_halves[0], far_halves[1]) * SCALE
    grads = dot_nt(far_halves[3], far_halves[2])
    allowed = iota((rows, rows), 1) <= iota((rows, rows), 0)
    top, total, grad_total = softmax_terms(scores, allowed, grads)
    lse, delta = merge_terms(*read_parts(far_stats, lane), top, total, grad_total)
    query_side, key_side = level_grads(far_halves, scores, allowed, grads, lse, delta)
    own_stats = part_lanes(top + jnp.log(total), grad_total / total, lane).astype(BF16)

    row, column = iota((rows, rows), 0), iota((rows, rows), 1)
    own = column == place + row // SLOTS
    to_far = jnp.where(own & (row % SLOTS == FAR_SLOT), 1.0, 0.0).astype(BF16)
    to_all = jnp.where(own, 1.0, 0.0).astype(BF16)
    first = dot_nn(to_far, query_side.astype(BF16))
    second = dot_nn(to_far, key_side.astype(BF16))
    far_lse, far_d = read_parts(dot_nn(to_all, own_stats), lane)

    col, line, col_at, line_at = slot_positions(near, far)
    slot = col % SLOTS
    active = (slot == FAR_SLOT) | ((slot < FAR_SLOT) & (near + NEAR_RATE * slot == far))
    lse, d = read_parts(stat_ref[...], lane)
    merged_lse, merged_d = merge_terms(lse, d, far_lse, 1.0, far_d)
    lse, delta = jnp.where(active, merged_lse, lse), jnp.where(active, merged_d, d)

    halves = pair_halves(got[:, :SLOTS].reshape(rows, 128), got[:, SLOTS:].reshape(rows, 128))
    allowed = (slot < FAR_SLOT) & (line % SLOTS < FAR_SLOT) & (line_at <= col_at)
    query_side, key_side = level_grads(
        halves, dot_nt(halves[0], halves[1]) * SCALE, allowed, dot_nt(halves[3], halves[2]), lse, delta
    )
    first += query_side
    second += key_side
    used = slot <= FAR_SLOT
    stats = pack_stats(jnp.where(used, lse, 0.0), jnp.where(used, delta, 0.0))
    near_block = jnp.where(slot < FAR_SLOT, first, pltpu.roll(second, FAR_SLOT, 0))
    far_block = jnp.where(slot == 0, pltpu.roll(second, rows - FAR_SLOT, 0), stats)
    far_block = jnp.where(slot == FAR_SLOT, first, far_block)
    send_ref[...] = jnp.where(copy == 0, near_block, far_block).astype(BF16)


def owner_call(got, stats, far_got):
    vmem = pl.BlockSpec(memory_space=pltpu.VMEM)
    return pl.pallas_call(
        owner_kernel,
        in_specs=[vmem, vmem, vmem],
        out_specs=vmem,
        out_shape=pltpu.VMEM((SEQ * SLOTS, 128), BF16),
        compiler_params=pltpu.CompilerParams(vmem_limit_bytes=VMEM_BYTES),
        name="owner_level",
    )(got, stats, far_got)


def finish_kernel(got_ref, *refs):
    halves, outs, (results, out_sems) = (refs[:5],), refs[5:9], refs[9:]
    mask = head_mask()
    low = iota((GSLOTS, 128), 1) < FEAT
    slot = iota((GSLOTS, 128), 0) % SLOTS
    zero = jnp.zeros((GSLOTS, GLANES), F32)
    sends = []

    def finished(i, b, value):
        results[i, :, b * GLANES : (b + 1) * GLANES] = value.astype(BF16)

    def send(arrays, first, count):
        here = slice(first * GLANES, (first + count) * GLANES)
        for i in arrays:
            copy = pltpu.make_async_copy(
                results.at[i, :, here], outs[i].at[:, here], out_sems.at[first, i]
            )
            copy.start()
            sends.append(copy)

    def spread(x):
        swapped = swap_halves(x)
        for half in (jnp.where(low, x, swapped), jnp.where(low, swapped, x)):
            yield jnp.where(mask, jnp.concatenate([half, half], axis=1), 0.0)

    for b in range(GROUPS):
        half, at = 0, b
        there = slice(at * GLANES, (at + 1) * GLANES)
        query_part, key_part, stat_ref, slot_ref, left_ref = halves[half]
        near = got_ref[b * GSLOTS : (b + 1) * GSLOTS].astype(F32)
        far = got_ref[HEADS * SLOTS + b * GSLOTS : HEADS * SLOTS + (b + 1) * GSLOTS].astype(F32)
        lse, delta = unpack_stats(far.reshape(GROUP, SLOTS, 128), 2)
        query_side = tuple(spread(jnp.where(slot < FAR_SLOT, near, far)))
        key_side = tuple(spread(jnp.where(slot < FAR_SLOT, far, near)))
        qs, gs, out, dq, mean = (slot_ref[slot_part(i), there].astype(F32) for i in range(5))
        stats = stat_ref[:, there]
        factor = jnp.exp(stats[:, :1] - lse)
        shift = factor * (stats[:, 1:2] - delta)
        out = factor * out + query_side[0]
        dq = factor * dq + shift * mean + query_side[1]
        right = (
            (zero, zero, shift * qs, factor * gs),
            (zero, zero, factor * qs, zero),
            (out, dq, zero, zero),
            (zero, zero) + key_side,
        )
        right = jnp.concatenate([jnp.concatenate(x, axis=1) for x in right], axis=0)
        sums = dot_nn(left_ref[:, at * TERMS : (at + 1) * TERMS], right.astype(BF16))
        if b:
            send((0, 1, 2, 3), b - 1, 1)
        for i in range(4):
            bulk = (query_part if i < 2 else key_part)[i % 2, :, there].astype(F32)
            finished(i, b, bulk + sums[:, i * GLANES : (i + 1) * GLANES])
    send((0, 1, 2, 3), 3, 1)
    for copy in sends:
        copy.wait()


def finish_call(got, parts):
    hbm = pl.BlockSpec(memory_space=pltpu.HBM)
    vmem = pl.BlockSpec(memory_space=pltpu.VMEM)
    return pl.pallas_call(
        finish_kernel,
        in_specs=[vmem] * 6,
        out_specs=[hbm] * 4,
        out_shape=[jax.ShapeDtypeStruct((ROWS, WIDTH), BF16)] * 4,
        scratch_shapes=[
            pltpu.VMEM((4, ROWS, WIDTH), BF16),
            pltpu.SemaphoreType.DMA((GROUPS, 4)),
        ],
        compiler_params=pltpu.CompilerParams(vmem_limit_bytes=VMEM_BYTES),
        name="finish_rows",
    )(got, *parts)


def exchange(x, axis):
    return lax.all_to_all(x, axis, split_axis=0, concat_axis=0, tiled=True)


def on_device(queries, keys, values, out_grad, near_offsets, far_offsets):
    arrays = (queries, keys, values, out_grad)
    pay = select_call(near_offsets, far_offsets, *arrays)
    got = exchange(pay.reshape(SEQ, 2 * SLOTS, 128), "seq")
    parts = []
    far_pay, stats = near_call(got)
    far_got = exchange(far_pay, "outer")
    back = owner_call(got, stats, far_got)
    (near_2, far_2), back = lax.optimization_barrier(((near_offsets, far_offsets), back))
    back_got = exchange(back, "seq")
    parts += local_call(EARLY, GROUPS - EARLY, near_2, far_2, *arrays, BF16)
    return finish_call(back_got, parts)


def solution(mesh):
    split = P(("outer", "seq"), None)
    return jax.shard_map(
        on_device,
        mesh=mesh,
        in_specs=(split, split, split, split, P(), P()),
        out_specs=(split, split, split, split),
        check_vma=False,
    )
```

```python
import functools

import jax
import jax.numpy as jnp
from jax import lax
from jax.experimental import pallas as pl
from jax.experimental.pallas import tpu as pltpu
from jax.sharding import PartitionSpec as P

HEADS = 16
FEAT = 64
ROWS = 256
WIDTH = 1024
NEAR_RATE = 64
FAR_RATE = 256
SEQ = 32
OUTER = 8
SLOTS = 8
FAR_SLOT = 4
STAT_SLOT = 5
NEAR_LANE = 48
FAR_LANE = 49
COPY_LANE = 50
GROUP = 4
GROUPS = HEADS // GROUP
EARLY = 2
GLANES = GROUP * FEAT
GSLOTS = GROUP * SLOTS
SCALE = FEAT**-0.5
LOW = -1e30
BACKWARDS = [list(range(SEQ - 1, -1, -1))]
SLOT_PARTS = 5
TERMS = 4 * GSLOTS
F32 = jnp.float32
BF16 = jnp.bfloat16
VMEM_BYTES = 24 * 1024 * 1024


def pinned(space, *arrays):
    return tuple(pltpu.with_memory_space_constraint(x, space) for x in arrays)


def iota(shape, axis):
    return lax.broadcasted_iota(jnp.int32, shape, axis)


def dot_nn(a, b):
    return lax.dot_general(a, b, (((1,), (0,)), ((), ())), preferred_element_type=F32)


def dot_nt(a, b):
    return lax.dot_general(a, b, (((1,), (1,)), ((), ())), preferred_element_type=F32)


def dot_tn(a, b):
    return lax.dot_general(a, b, (((0,), (0,)), ((), ())), preferred_element_type=F32)


def parts_of(value):
    high = value.astype(BF16).astype(F32)
    rest = value - high
    middle = rest.astype(BF16).astype(F32)
    return high, middle, rest - middle


def part_lanes(lse, d, at):
    out = jnp.zeros((lse.shape[0], at.shape[1]), F32)
    for index, part in enumerate(parts_of(lse) + parts_of(d)):
        out = jnp.where(at == index, part, out)
    return out


def read_parts(lanes, at):
    lse = jnp.sum(jnp.where((at >= 0) & (at < 3), lanes, 0.0), axis=1, keepdims=True)
    d = jnp.sum(jnp.where((at >= 3) & (at < 6), lanes, 0.0), axis=1, keepdims=True)
    return lse, d


def pack_stats(lse, d):
    rows = lse.shape[0]
    row, lane = iota((rows, 128), 0), iota((rows, 128), 1)
    at = jnp.where(lane // 8 == row % SLOTS, lane % 8, -1)
    spread = part_lanes(lse, d, at).reshape(rows // SLOTS, SLOTS, 128)
    total = jnp.sum(spread, axis=1, keepdims=True)
    return jnp.broadcast_to(total, spread.shape).reshape(rows, 128)


def unpack_stats(block, at=STAT_SLOT):
    lanes = jnp.broadcast_to(block[:, at : at + 1, :], (block.shape[0], SLOTS, 128))
    lanes = lanes.reshape(block.shape[0] * SLOTS, 128)
    row, lane = iota(lanes.shape, 0), iota(lanes.shape, 1)
    return read_parts(lanes, jnp.where(lane // 8 == row % SLOTS, lane % 8, -1))


def swap_halves(x):
    return pltpu.roll(x, FEAT, 1)


def group_offsets(near_ref, far_ref, first):
    index = iota((GSLOTS, 1), 0)
    near = jnp.zeros((GSLOTS, 1), jnp.int32)
    far = jnp.zeros((GSLOTS, 1), jnp.int32)
    for h in range(GROUP):
        here = index // SLOTS == h
        near = jnp.where(here, near_ref[first + h], near)
        far = jnp.where(here, far_ref[first + h], far)
    return near, far


def slot_rows(near_ref, far_ref, first):
    near, far = group_offsets(near_ref, far_ref, first)
    slot = iota((GSLOTS, 1), 0) % SLOTS
    row = jnp.where(slot < FAR_SLOT, near + NEAR_RATE * slot, jnp.where(slot == FAR_SLOT, far, -1))
    repeat = (slot == FAR_SLOT) & (far % NEAR_RATE == near)
    return row, repeat, slot


def head_mask():
    return iota((GSLOTS, GLANES), 1) // FEAT == iota((GSLOTS, GLANES), 0) // SLOTS


def softmax_terms(scores, allowed, weight_grads):
    masked = jnp.where(allowed, scores, LOW)
    top = jnp.max(masked, axis=1, keepdims=True)
    weights = jnp.where(allowed, jnp.exp(masked - top), 0.0)
    total = jnp.sum(weights, axis=1, keepdims=True)
    return top, total, jnp.sum(weights * weight_grads, axis=1, keepdims=True)


def merge_terms(lse, d, top, total, grad_total):
    overall = jnp.maximum(lse, top)
    old, new = jnp.exp(lse - overall), jnp.exp(top - overall)
    mass = old + new * total
    return overall + jnp.log(mass), (old * d + new * grad_total) / mass


OFFSET_SCRATCH = [
    pltpu.SMEM((HEADS,), jnp.int32),
    pltpu.SMEM((HEADS,), jnp.int32),
    pltpu.SemaphoreType.DMA((2,)),
]


def start_offsets(near_in, far_in, near_ref, far_ref, sems):
    copies = [
        pltpu.make_async_copy(near_in, near_ref, sems.at[0]),
        pltpu.make_async_copy(far_in, far_ref, sems.at[1]),
    ]
    for copy in copies:
        copy.start()
    return copies


def pick_matrix(row):
    return jnp.where(iota((GSLOTS, ROWS), 1) == row, 1.0, 0.0).astype(BF16)


def slot_stats(scores, row, grads, live):
    allowed = iota((GSLOTS, ROWS), 1) <= row
    masked = jnp.where(allowed, scores, LOW)
    top = jnp.max(masked, axis=1, keepdims=True)
    weights = jnp.where(allowed & live, jnp.exp(masked - top), 0.0)
    total = jnp.where(live, jnp.sum(weights, axis=1, keepdims=True), 1.0)
    scale = 1.0 / total
    d = jnp.sum(weights * grads, axis=1, keepdims=True) * scale
    return jnp.where(live, top + jnp.log(total), 0.0), d, weights * scale, grads - d


def start_copies(sources, base, count, buffer, sems):
    copies = []
    for b in range(count):
        here = pl.ds(b * GLANES, GLANES)
        there = pl.ds((base + b) * GLANES, GLANES)
        copies.append(
            [
                pltpu.make_async_copy(source.at[:, there], buffer.at[i, :, here], sems.at[b, i])
                for i, source in enumerate(sources)
            ]
        )
    for group in copies:
        for copy in group:
            copy.start()
    return copies


def start_whole(sources, buffer, sems):
    copies = [
        pltpu.make_async_copy(source, buffer.at[i], sems.at[i]) for i, source in enumerate(sources)
    ]
    for copy in copies:
        copy.start()
    return copies


def select_kernel(
    near_in, far_in, q_ref, k_ref, v_ref, g_ref, pay_ref, near_ref, far_ref, offset_sems, buffer, sems
):
    offset_copies = start_offsets(near_in, far_in, near_ref, far_ref, offset_sems)
    copies = start_whole((q_ref, g_ref, k_ref, v_ref), buffer, sems)
    for copy in offset_copies:
        copy.wait()
    groups = range(GROUPS)
    rows = [slot_rows(near_ref, far_ref, b * GROUP)[0] for b in groups]
    picks = [pick_matrix(row) for row in rows]
    mask = head_mask()
    lane = iota((GSLOTS, 128), 1)
    slot = iota((GSLOTS, 1), 0) % SLOTS

    def columns(i, b):
        return buffer[i, :, b * GLANES : (b + 1) * GLANES]

    def selected(i):
        copies[i].wait()
        return [jnp.where(mask, dot_nn(picks[b], columns(i, b)), 0.0) for b in groups]

    def folded(x):
        x = x[:, :128] + x[:, 128:]
        return x + swap_halves(x)

    qs, gs, ks = selected(0), selected(1), selected(2)
    scores = [dot_nt(qs[b].astype(BF16), columns(2, b)) * SCALE for b in groups]
    vs = selected(3)
    grads = [dot_nt(gs[b].astype(BF16), columns(3, b)) for b in groups]
    for b in groups:
        lse, d, _, _ = slot_stats(scores[b], rows[b], grads[b], slot <= FAR_SLOT)
        stats = pack_stats(lse, d)
        near, far = group_offsets(near_ref, far_ref, b * GROUP)
        stats = jnp.where(lane == NEAR_LANE, near, jnp.where(lane == FAR_LANE, far, stats))
        qk = jnp.where(lane < FEAT, folded(qs[b]), folded(ks[b]))
        vg = jnp.where(lane < FEAT, folded(vs[b]), folded(gs[b]))
        qk = jnp.where(slot == STAT_SLOT, stats, qk)
        block = jnp.concatenate(
            [qk.reshape(GROUP, SLOTS, 128), vg.reshape(GROUP, SLOTS, 128)], axis=1
        ).astype(BF16)
        pay_ref[0, b * GROUP : (b + 1) * GROUP] = block
        mark = (iota(block.shape, 1) == STAT_SLOT) & (iota(block.shape, 2) == COPY_LANE)
        pay_ref[1, b * GROUP : (b + 1) * GROUP] = jnp.where(mark, jnp.ones((), BF16), block)


def select_call(near, far, q, k, v, g):
    hbm = pl.BlockSpec(memory_space=pltpu.HBM)
    vmem = pl.BlockSpec(memory_space=pltpu.VMEM)
    return pl.pallas_call(
        select_kernel,
        in_specs=[hbm] * 6,
        out_specs=vmem,
        out_shape=pltpu.VMEM((2, HEADS, 2 * SLOTS, 128), BF16),
        scratch_shapes=OFFSET_SCRATCH
        + [pltpu.VMEM((4, ROWS, WIDTH), BF16), pltpu.SemaphoreType.DMA((4,))],
        compiler_params=pltpu.CompilerParams(vmem_limit_bytes=VMEM_BYTES),
        name="select_rows",
    )(*pinned(pltpu.HBM, near, far, q, k, v, g))


def local_head(head, here, near_ref, far_ref, q, k, v, g):
    half = ROWS // 2
    query = iota((1, ROWS), 1)
    zero = jnp.zeros((), BF16)
    special = (query % NEAR_RATE == near_ref[head]) | (query == far_ref[head])
    kh, vh, qh, gh = (jnp.where(here, x, zero) for x in (k, v, q, g))
    triangle = iota((half, half), 0) <= iota((half, half), 1)
    top, bottom = dot_nt(kh[:half], q), dot_nt(kh[half:], q[half:])
    early, late = jnp.where(triangle, top[:, :half], LOW), top[:, half:]
    bottom = jnp.where(triangle, bottom, LOW)
    early_top = jnp.max(early, axis=0, keepdims=True)
    late_top = jnp.maximum(jnp.max(late, axis=0, keepdims=True), jnp.max(bottom, axis=0, keepdims=True))
    early, late, bottom = jnp.exp(early - early_top), jnp.exp(late - late_top), jnp.exp(bottom - late_top)
    early_total = jnp.sum(early, axis=0, keepdims=True)
    late_total = jnp.sum(late, axis=0, keepdims=True) + jnp.sum(bottom, axis=0, keepdims=True)
    scale = jnp.where(special, 0.0, 1.0 / jnp.concatenate([early_total, late_total], axis=1))
    grads, grads_b = dot_nt(vh[:half], g), dot_nt(vh[half:], g[half:])
    top = jnp.concatenate([early, late], axis=1) * scale
    bottom = bottom * scale[:, half:]
    delta = jnp.sum(top * grads, axis=0, keepdims=True)
    late_delta = delta[:, half:] + jnp.sum(bottom * grads_b, axis=0, keepdims=True)
    delta = jnp.concatenate([delta[:, :half], late_delta], axis=1)
    blank = jnp.zeros((half, half), BF16)

    def square(top, bottom):
        bottom = jnp.concatenate([blank, bottom.astype(BF16)], axis=1)
        return jnp.concatenate([top.astype(BF16), bottom], axis=0)

    dscores = square(top * (grads - delta), bottom * (grads_b - late_delta))
    return square(top, bottom), dscores, qh, kh, vh, gh


def joined(heads):
    weights, dscores, q, k, v, g = zip(*heads)
    over_keys = jnp.concatenate(weights, axis=0), jnp.concatenate(dscores, axis=0)
    over_queries = jnp.concatenate(weights, axis=1), jnp.concatenate(dscores, axis=1)
    out = dot_tn(over_keys[0], jnp.concatenate(v, axis=0))
    dq = dot_tn(over_keys[1], jnp.concatenate(k, axis=0)) * SCALE
    dk = dot_nn(over_queries[1], jnp.concatenate(q, axis=0))
    return out, dq, dk, dot_nn(over_queries[0], jnp.concatenate(g, axis=0))


def local_group(near_ref, far_ref, first, q, k, v, g):
    half = ROWS // 2
    query = iota((1, ROWS), 1)
    q = (q.astype(F32) * SCALE).astype(BF16)
    zero = jnp.zeros((), BF16)
    triangle = iota((half, half), 0) <= iota((half, half), 1)
    blank = jnp.zeros((half, half), BF16)
    lane = iota((1, GLANES), 1) // FEAT
    heads = [local_head(first + h, lane == h, near_ref, far_ref, q, k, v, g) for h in range(GROUP)]
    return joined(heads)


def slot_part(i, count=1):
    return slice(i * GSLOTS, (i + count) * GSLOTS)


def local_kernel(
    base, count, near_in, far_in, q_ref, k_ref, v_ref, g_ref, query_ref, key_ref, stat_ref, slot_ref,
    left_ref, near_ref, far_ref, offset_sems, buffer, sems
):
    offset_copies = start_offsets(near_in, far_in, near_ref, far_ref, offset_sems)
    start_copies((q_ref, k_ref, v_ref, g_ref), base, count, buffer, sems)
    for copy in offset_copies:
        copy.wait()
    mask = head_mask()

    def one_group(b, carry):
        here = pl.ds(pl.multiple_of(b * GLANES, GLANES), GLANES)
        for i, source in enumerate((q_ref, k_ref, v_ref, g_ref)):
            there = pl.ds(pl.multiple_of((base + b) * GLANES, GLANES), GLANES)
            pltpu.make_async_copy(source.at[:, there], buffer.at[i, :, here], sems.at[b, i]).wait()
        q, k, v, g = (buffer[i, :, here] for i in range(4))
        first = (base + b) * GROUP
        row, repeat, slot = slot_rows(near_ref, far_ref, first)
        pick = pick_matrix(row)
        qs = jnp.where(mask, dot_nn(pick, q), 0.0)
        gs = jnp.where(mask, dot_nn(pick, g), 0.0)
        live = (slot <= FAR_SLOT) & ~repeat
        scores = dot_nt(qs.astype(BF16), k) * SCALE
        grads = dot_nt(gs.astype(BF16), v)
        lse, d, weights, grads = slot_stats(scores, row, grads, live)
        dscores = (weights * grads).astype(BF16)
        weights = weights.astype(BF16)
        lane = iota((GSLOTS, GLANES), 1)
        near, far = group_offsets(near_ref, far_ref, first)
        key_row = jnp.where(slot >= FAR_SLOT, near + NEAR_RATE * (slot - FAR_SLOT), -1)
        key_pick = pick_matrix(jnp.where(slot == 0, far, key_row))
        left = jnp.concatenate([weights, dscores, pick, key_pick], axis=0)
        left_ref[:, pl.ds(pl.multiple_of(b * TERMS, TERMS), TERMS)] = jnp.transpose(left)
        parts = (
            (qs * SCALE).astype(BF16),
            gs.astype(BF16),
            jnp.where(mask, dot_nn(weights, v), 0.0).astype(BF16),
            (jnp.where(mask, dot_nn(dscores, k), 0.0) * SCALE).astype(BF16),
            (jnp.where(mask, dot_nn(weights, k), 0.0) * SCALE).astype(BF16),
        )
        for i, part in enumerate(parts):
            slot_ref[slot_part(i), here] = part
        stat_ref[:, here] = jnp.where(lane == 0, jnp.where(live, lse, LOW), d)
        out, dq, dk, dv = local_group(near_ref, far_ref, first, q, k, v, g)
        query_ref[0, :, here] = out.astype(BF16)
        query_ref[1, :, here] = dq.astype(BF16)
        key_ref[0, :, here] = dk.astype(key_ref.dtype)
        key_ref[1, :, here] = dv.astype(key_ref.dtype)
        return carry

    lax.fori_loop(0, count, one_group, 0)


def local_call(base, count, near, far, q, k, v, g, key_type):
    hbm = pl.BlockSpec(memory_space=pltpu.HBM)
    vmem = pl.BlockSpec(memory_space=pltpu.VMEM)
    shape = (ROWS, count * GLANES)
    return pl.pallas_call(
        functools.partial(local_kernel, base, count),
        in_specs=[hbm] * 6,
        out_specs=[vmem] * 5,
        out_shape=[
            pltpu.VMEM((2,) + shape, BF16),
            pltpu.VMEM((2,) + shape, key_type),
            pltpu.VMEM((GSLOTS, count * GLANES), F32),
            pltpu.VMEM((SLOT_PARTS * GSLOTS, count * GLANES), BF16),
            pltpu.VMEM((ROWS, count * TERMS), BF16),
        ],
        scratch_shapes=OFFSET_SCRATCH
        + [pltpu.VMEM((4,) + shape, BF16), pltpu.SemaphoreType.DMA((count, 4))],
        compiler_params=pltpu.CompilerParams(vmem_limit_bytes=VMEM_BYTES),
        cost_estimate=pl.CostEstimate(
            flops=count * GROUP * 14 * ROWS * ROWS * FEAT,
            bytes_accessed=count * 7 * ROWS * GLANES * 2,
            transcendentals=count * GROUP * ROWS * ROWS,
        ),
        name="local_level",
    )(*pinned(pltpu.HBM, near, far, q, k, v, g))


def slot_positions(near, far):
    col = iota((SEQ * SLOTS, 1), 0)
    line = iota((1, SEQ * SLOTS), 1)

    def position(index):
        slot = index % SLOTS
        return (SEQ - 1 - index // SLOTS) * ROWS + jnp.where(slot < FAR_SLOT, near + NEAR_RATE * slot, far)

    return col, line, position(col), position(line)


def pair_halves(qk, vg):
    low = iota(qk.shape, 1) < FEAT
    q0 = jnp.where(low, qk, 0.0)
    k0 = jnp.where(low, swap_halves(qk), 0.0)
    g0 = jnp.where(low, swap_halves(vg), 0.0)
    v0 = jnp.where(low, vg, 0.0)
    k1 = jnp.where(low, 0.0, qk)
    g1 = jnp.where(low, 0.0, vg)
    return tuple(x.astype(BF16) for x in (q0, k0, v0, g0, k1, g1))


def read_offsets(got):
    line = got[0, STAT_SLOT : STAT_SLOT + 1, :].astype(jnp.int32)
    return tuple(line[:, at : at + 1] for at in (NEAR_LANE, FAR_LANE, COPY_LANE))


def near_kernel(got_ref, send_ref, stat_ref):
    got = got_ref[...].astype(F32)
    near, far, _ = read_offsets(got)
    qk, vg = got[:, :SLOTS].reshape(SEQ * SLOTS, 128), got[:, SLOTS:].reshape(SEQ * SLOTS, 128)
    lse, d = unpack_stats(got)
    q0, k0, v0, g0, _, _ = pair_halves(qk, vg)
    col, line, col_at, line_at = slot_positions(near, far)
    asks = (col % SLOTS < FAR_SLOT) | ((col % SLOTS == FAR_SLOT) & (far % NEAR_RATE == near))
    allowed = asks & (line % SLOTS < FAR_SLOT) & (line_at <= col_at)
    terms = softmax_terms(dot_nt(q0, k0) * SCALE, allowed, dot_nt(g0, v0))
    lse, d = merge_terms(lse, d, *terms)
    lane = iota((SEQ * SLOTS, 128), 1)
    stats = part_lanes(lse, d, lane)
    stat_ref[...] = stats
    rows = SEQ * SLOTS
    pick = iota((SEQ, rows), 1) == iota((SEQ, rows), 0) * SLOTS + FAR_SLOT
    pick = jnp.where(pick, 1.0, 0.0).astype(BF16)
    block = jnp.concatenate([dot_nn(pick, x.astype(BF16)) for x in (qk, vg, stats)], axis=0)
    block = block.astype(BF16)
    for o in range(OUTER):
        send_ref[o] = block


def near_call(got):
    return pl.pallas_call(
        near_kernel,
        in_specs=[pl.BlockSpec(memory_space=pltpu.VMEM)],
        out_specs=[pl.BlockSpec(memory_space=pltpu.VMEM)] * 2,
        out_shape=[
            pltpu.VMEM((OUTER, 3 * SEQ, 128), BF16),
            pltpu.VMEM((SEQ * SLOTS, 128), F32),
        ],
        compiler_params=pltpu.CompilerParams(vmem_limit_bytes=VMEM_BYTES),
        name="near_forward",
    )(got)


def level_grads(halves, scores, allowed, grads, lse, delta):
    q0, k0, v0, g0, k1, g1 = halves
    weights = jnp.where(allowed, jnp.exp(jnp.where(allowed, scores - lse, 0.0)), 0.0)
    dscores = (weights * (grads - delta)).astype(BF16)
    weights = weights.astype(BF16)
    query_side = dot_nn(weights, v0) + dot_nn(dscores, k1)
    key_side = dot_tn(dscores, q0) + dot_tn(weights, g1)
    low = iota((1, 128), 1) < FEAT
    return query_side * jnp.where(low, 1.0, SCALE), key_side * jnp.where(low, SCALE, 1.0)


def far_order(index):
    return SEQ * OUTER - 1 - index


def owner_kernel(got_ref, stat_ref, far_got_ref, send_ref):
    place = (OUTER - 1 - lax.axis_index("outer")) * SEQ
    got = got_ref[...].astype(F32)
    near, far, copy = read_offsets(got)
    rows = SEQ * SLOTS
    lane = iota((rows, 128), 1)

    far_qk = far_got_ref[:, :SEQ].reshape(rows, 128).astype(F32)
    far_vg = far_got_ref[:, SEQ : 2 * SEQ].reshape(rows, 128).astype(F32)
    far_stats = far_got_ref[:, 2 * SEQ :].reshape(rows, 128).astype(F32)
    far_halves = pair_halves(far_qk, far_vg)
    scores = dot_nt(far_halves[0], far_halves[1]) * SCALE
    grads = dot_nt(far_halves[3], far_halves[2])
    ask, key = far_order(iota((rows, rows), 0)), far_order(iota((rows, rows), 1))
    allowed = key <= ask
    top, total, grad_total = softmax_terms(scores, allowed, grads)
    lse, delta = merge_terms(*read_parts(far_stats, lane), top, total, grad_total)
    query_side, key_side = level_grads(far_halves, scores, allowed, grads, lse, delta)
    own_stats = part_lanes(top + jnp.log(total), grad_total / total, lane).astype(BF16)

    row, column = iota((rows, rows), 0), iota((rows, rows), 1)
    own = column == place + row // SLOTS
    to_far = jnp.where(own & (row % SLOTS == FAR_SLOT), 1.0, 0.0).astype(BF16)
    to_all = jnp.where(own, 1.0, 0.0).astype(BF16)
    first = dot_nn(to_far, query_side.astype(BF16))
    second = dot_nn(to_far, key_side.astype(BF16))
    far_lse, far_d = read_parts(dot_nn(to_all, own_stats), lane)

    col, line, col_at, line_at = slot_positions(near, far)
    slot = col % SLOTS
    active = (slot == FAR_SLOT) | ((slot < FAR_SLOT) & (near + NEAR_RATE * slot == far))
    lse, d = read_parts(stat_ref[...], lane)
    merged_lse, merged_d = merge_terms(lse, d, far_lse, 1.0, far_d)
    lse, delta = jnp.where(active, merged_lse, lse), jnp.where(active, merged_d, d)

    halves = pair_halves(got[:, :SLOTS].reshape(rows, 128), got[:, SLOTS:].reshape(rows, 128))
    allowed = (slot < FAR_SLOT) & (line % SLOTS < FAR_SLOT) & (line_at <= col_at)
    query_side, key_side = level_grads(
        halves, dot_nt(halves[0], halves[1]) * SCALE, allowed, dot_nt(halves[3], halves[2]), lse, delta
    )
    first += query_side
    second += key_side
    used = slot <= FAR_SLOT
    stats = pack_stats(jnp.where(used, lse, 0.0), jnp.where(used, delta, 0.0))
    near_block = jnp.where(slot < FAR_SLOT, first, pltpu.roll(second, FAR_SLOT, 0))
    far_block = jnp.where(slot == 0, pltpu.roll(second, rows - FAR_SLOT, 0), stats)
    far_block = jnp.where(slot == FAR_SLOT, first, far_block)
    send_ref[...] = jnp.where(copy == 0, near_block, far_block).astype(BF16)


def owner_call(got, stats, far_got):
    vmem = pl.BlockSpec(memory_space=pltpu.VMEM)
    return pl.pallas_call(
        owner_kernel,
        in_specs=[vmem, vmem, vmem],
        out_specs=vmem,
        out_shape=pltpu.VMEM((SEQ * SLOTS, 128), BF16),
        compiler_params=pltpu.CompilerParams(vmem_limit_bytes=VMEM_BYTES),
        name="owner_level",
    )(got, stats, far_got)


def finish_kernel(got_ref, *refs):
    halves, outs, (results, out_sems) = (refs[:5], refs[5:10]), refs[10:14], refs[14:]
    mask = head_mask()
    low = iota((GSLOTS, 128), 1) < FEAT
    slot = iota((GSLOTS, 128), 0) % SLOTS
    zero = jnp.zeros((GSLOTS, GLANES), F32)
    sends = []

    def finished(i, b, value):
        results[i, :, b * GLANES : (b + 1) * GLANES] = value.astype(BF16)

    def send(arrays, first, count):
        here = slice(first * GLANES, (first + count) * GLANES)
        for i in arrays:
            copy = pltpu.make_async_copy(
                results.at[i, :, here], outs[i].at[:, here], out_sems.at[first, i]
            )
            copy.start()
            sends.append(copy)

    def spread(x):
        swapped = swap_halves(x)
        for half in (jnp.where(low, x, swapped), jnp.where(low, swapped, x)):
            yield jnp.where(mask, jnp.concatenate([half, half], axis=1), 0.0)

    for b in range(GROUPS):
        half, at = (0, b) if b < EARLY else (1, b - EARLY)
        there = slice(at * GLANES, (at + 1) * GLANES)
        query_part, key_part, stat_ref, slot_ref, left_ref = halves[half]
        near = got_ref[b * GSLOTS : (b + 1) * GSLOTS].astype(F32)
        far = got_ref[HEADS * SLOTS + b * GSLOTS : HEADS * SLOTS + (b + 1) * GSLOTS].astype(F32)
        lse, delta = unpack_stats(far.reshape(GROUP, SLOTS, 128), 2)
        query_side = tuple(spread(jnp.where(slot < FAR_SLOT, near, far)))
        key_side = tuple(spread(jnp.where(slot < FAR_SLOT, far, near)))
        qs, gs, out, dq, mean = (slot_ref[slot_part(i), there].astype(F32) for i in range(5))
        stats = stat_ref[:, there]
        factor = jnp.exp(stats[:, :1] - lse)
        shift = factor * (stats[:, 1:2] - delta)
        out = factor * out + query_side[0]
        dq = factor * dq + shift * mean + query_side[1]
        right = (
            (zero, zero, shift * qs, factor * gs),
            (zero, zero, factor * qs, zero),
            (out, dq, zero, zero),
            (zero, zero) + key_side,
        )
        right = jnp.concatenate([jnp.concatenate(x, axis=1) for x in right], axis=0)
        sums = dot_nn(left_ref[:, at * TERMS : (at + 1) * TERMS], right.astype(BF16))
        if b:
            send((0, 1, 2, 3), b - 1, 1)
        for i in range(4):
            bulk = (query_part if i < 2 else key_part)[i % 2, :, there].astype(F32)
            finished(i, b, bulk + sums[:, i * GLANES : (i + 1) * GLANES])
    send((0, 1, 2, 3), 3, 1)
    for copy in sends:
        copy.wait()


def finish_call(got, parts):
    hbm = pl.BlockSpec(memory_space=pltpu.HBM)
    vmem = pl.BlockSpec(memory_space=pltpu.VMEM)
    return pl.pallas_call(
        finish_kernel,
        in_specs=[vmem] * 11,
        out_specs=[hbm] * 4,
        out_shape=[jax.ShapeDtypeStruct((ROWS, WIDTH), BF16)] * 4,
        scratch_shapes=[
            pltpu.VMEM((4, ROWS, WIDTH), BF16),
            pltpu.SemaphoreType.DMA((GROUPS, 4)),
        ],
        compiler_params=pltpu.CompilerParams(vmem_limit_bytes=VMEM_BYTES),
        name="finish_rows",
    )(got, *parts)


def exchange(x, axis, groups=None):
    return lax.all_to_all(
        x, axis, split_axis=0, concat_axis=0, axis_index_groups=groups, tiled=True
    )


def on_device(queries, keys, values, out_grad, near_offsets, far_offsets):
    arrays = (queries, keys, values, out_grad)
    pay = select_call(near_offsets, far_offsets, *arrays)
    got = exchange(pay.reshape(SEQ, 2 * SLOTS, 128), "seq", BACKWARDS)
    (near_1, far_1), _ = lax.optimization_barrier(((near_offsets, far_offsets), pay))
    parts = local_call(0, EARLY, near_1, far_1, *arrays, BF16)
    got, parts = lax.optimization_barrier((got, parts))
    far_pay, stats = near_call(got)
    far_got = exchange(far_pay, "outer", [list(range(OUTER - 1, -1, -1))])
    back = owner_call(got, stats, far_got)
    (near_2, far_2), back = lax.optimization_barrier(((near_offsets, far_offsets), back))
    back_got = exchange(back, "seq", BACKWARDS)
    parts += local_call(EARLY, GROUPS - EARLY, near_2, far_2, *arrays, F32)
    return finish_call(back_got, parts)


def solution(mesh):
    split = P(("outer", "seq"), None)
    return jax.shard_map(
        on_device,
        mesh=mesh,
        in_specs=(split, split, split, split, P(), P()),
        out_specs=(split, split, split, split),
        check_vma=False,
    )
```

```python
import functools

import jax
import jax.numpy as jnp
from jax import lax
from jax.experimental import pallas as pl
from jax.experimental.pallas import tpu as pltpu
from jax.sharding import PartitionSpec as P

HEADS = 16
FEAT = 64
ROWS = 256
WIDTH = 1024
NEAR_RATE = 64
FAR_RATE = 256
SEQ = 32
OUTER = 8
SLOTS = 8
FAR_SLOT = 4
STAT_SLOT = 5
NEAR_LANE = 48
FAR_LANE = 49
COPY_LANE = 50
GROUP = 4
GROUPS = HEADS // GROUP
EARLY = 2
GLANES = GROUP * FEAT
GSLOTS = GROUP * SLOTS
SCALE = FEAT**-0.5
LOW = -1e30
BACKWARDS = [list(range(SEQ - 1, -1, -1))]
SLOT_PARTS = 5
TERMS = 4 * GSLOTS
F32 = jnp.float32
BF16 = jnp.bfloat16
VMEM_BYTES = 24 * 1024 * 1024


def pinned(space, *arrays):
    return tuple(pltpu.with_memory_space_constraint(x, space) for x in arrays)


def iota(shape, axis):
    return lax.broadcasted_iota(jnp.int32, shape, axis)


def dot_nn(a, b):
    return lax.dot_general(a, b, (((1,), (0,)), ((), ())), preferred_element_type=F32)


def dot_nt(a, b):
    return lax.dot_general(a, b, (((1,), (1,)), ((), ())), preferred_element_type=F32)


def dot_tn(a, b):
    return lax.dot_general(a, b, (((0,), (0,)), ((), ())), preferred_element_type=F32)


def parts_of(value):
    high = value.astype(BF16).astype(F32)
    rest = value - high
    middle = rest.astype(BF16).astype(F32)
    return high, middle, rest - middle


def part_lanes(lse, d, at):
    out = jnp.zeros((lse.shape[0], at.shape[1]), F32)
    for index, part in enumerate(parts_of(lse) + parts_of(d)):
        out = jnp.where(at == index, part, out)
    return out


def read_parts(lanes, at):
    lse = jnp.sum(jnp.where((at >= 0) & (at < 3), lanes, 0.0), axis=1, keepdims=True)
    d = jnp.sum(jnp.where((at >= 3) & (at < 6), lanes, 0.0), axis=1, keepdims=True)
    return lse, d


def pack_stats(lse, d):
    rows = lse.shape[0]
    row, lane = iota((rows, 128), 0), iota((rows, 128), 1)
    at = jnp.where(lane // 8 == row % SLOTS, lane % 8, -1)
    spread = part_lanes(lse, d, at).reshape(rows // SLOTS, SLOTS, 128)
    total = jnp.sum(spread, axis=1, keepdims=True)
    return jnp.broadcast_to(total, spread.shape).reshape(rows, 128)


def unpack_stats(block, at=STAT_SLOT):
    lanes = jnp.broadcast_to(block[:, at : at + 1, :], (block.shape[0], SLOTS, 128))
    lanes = lanes.reshape(block.shape[0] * SLOTS, 128)
    row, lane = iota(lanes.shape, 0), iota(lanes.shape, 1)
    return read_parts(lanes, jnp.where(lane // 8 == row % SLOTS, lane % 8, -1))


def swap_halves(x):
    return pltpu.roll(x, FEAT, 1)


def group_offsets(near_ref, far_ref, first):
    index = iota((GSLOTS, 1), 0)
    near = jnp.zeros((GSLOTS, 1), jnp.int32)
    far = jnp.zeros((GSLOTS, 1), jnp.int32)
    for h in range(GROUP):
        here = index // SLOTS == h
        near = jnp.where(here, near_ref[first + h], near)
        far = jnp.where(here, far_ref[first + h], far)
    return near, far


def slot_rows(near_ref, far_ref, first):
    near, far = group_offsets(near_ref, far_ref, first)
    slot = iota((GSLOTS, 1), 0) % SLOTS
    row = jnp.where(slot < FAR_SLOT, near + NEAR_RATE * slot, jnp.where(slot == FAR_SLOT, far, -1))
    repeat = (slot == FAR_SLOT) & (far % NEAR_RATE == near)
    return row, repeat, slot


def head_mask():
    return iota((GSLOTS, GLANES), 1) // FEAT == iota((GSLOTS, GLANES), 0) // SLOTS


def softmax_terms(scores, allowed, weight_grads):
    masked = jnp.where(allowed, scores, LOW)
    top = jnp.max(masked, axis=1, keepdims=True)
    weights = jnp.where(allowed, jnp.exp(masked - top), 0.0)
    total = jnp.sum(weights, axis=1, keepdims=True)
    return top, total, jnp.sum(weights * weight_grads, axis=1, keepdims=True)


def merge_terms(lse, d, top, total, grad_total):
    overall = jnp.maximum(lse, top)
    old, new = jnp.exp(lse - overall), jnp.exp(top - overall)
    mass = old + new * total
    return overall + jnp.log(mass), (old * d + new * grad_total) / mass


OFFSET_SCRATCH = [
    pltpu.SMEM((HEADS,), jnp.int32),
    pltpu.SMEM((HEADS,), jnp.int32),
    pltpu.SemaphoreType.DMA((2,)),
]


def start_offsets(near_in, far_in, near_ref, far_ref, sems):
    copies = [
        pltpu.make_async_copy(near_in, near_ref, sems.at[0]),
        pltpu.make_async_copy(far_in, far_ref, sems.at[1]),
    ]
    for copy in copies:
        copy.start()
    return copies


def pick_matrix(row):
    return jnp.where(iota((GSLOTS, ROWS), 1) == row, 1.0, 0.0).astype(BF16)


def slot_stats(scores, row, grads, live):
    allowed = iota((GSLOTS, ROWS), 1) <= row
    masked = jnp.where(allowed, scores, LOW)
    top = jnp.max(masked, axis=1, keepdims=True)
    weights = jnp.where(allowed & live, jnp.exp(masked - top), 0.0)
    total = jnp.where(live, jnp.sum(weights, axis=1, keepdims=True), 1.0)
    scale = 1.0 / total
    d = jnp.sum(weights * grads, axis=1, keepdims=True) * scale
    return jnp.where(live, top + jnp.log(total), 0.0), d, weights * scale, grads - d


def start_copies(sources, base, count, buffer, sems):
    copies = []
    for b in range(count):
        here = pl.ds(b * GLANES, GLANES)
        there = pl.ds((base + b) * GLANES, GLANES)
        copies.append(
            [
                pltpu.make_async_copy(source.at[:, there], buffer.at[i, :, here], sems.at[b, i])
                for i, source in enumerate(sources)
            ]
        )
    for group in copies:
        for copy in group:
            copy.start()
    return copies


def start_whole(sources, buffer, sems):
    copies = [
        pltpu.make_async_copy(source, buffer.at[i], sems.at[i]) for i, source in enumerate(sources)
    ]
    for copy in copies:
        copy.start()
    return copies


def select_kernel(
    near_in, far_in, q_ref, k_ref, v_ref, g_ref, pay_ref, near_ref, far_ref, offset_sems, buffer, sems
):
    offset_copies = start_offsets(near_in, far_in, near_ref, far_ref, offset_sems)
    copies = start_whole((q_ref, g_ref, k_ref, v_ref), buffer, sems)
    for copy in offset_copies:
        copy.wait()
    groups = range(GROUPS)
    rows = [slot_rows(near_ref, far_ref, b * GROUP)[0] for b in groups]
    picks = [pick_matrix(row) for row in rows]
    mask = head_mask()
    lane = iota((GSLOTS, 128), 1)
    slot = iota((GSLOTS, 1), 0) % SLOTS

    def columns(i, b):
        return buffer[i, :, b * GLANES : (b + 1) * GLANES]

    def selected(i):
        copies[i].wait()
        return [jnp.where(mask, dot_nn(picks[b], columns(i, b)), 0.0) for b in groups]

    def folded(x):
        x = x[:, :128] + x[:, 128:]
        return x + swap_halves(x)

    qs, gs, ks = selected(0), selected(1), selected(2)
    scores = [dot_nt(qs[b].astype(BF16), columns(2, b)) * SCALE for b in groups]
    vs = selected(3)
    grads = [dot_nt(gs[b].astype(BF16), columns(3, b)) for b in groups]
    for b in groups:
        lse, d, _, _ = slot_stats(scores[b], rows[b], grads[b], slot <= FAR_SLOT)
        stats = pack_stats(lse, d)
        near, far = group_offsets(near_ref, far_ref, b * GROUP)
        stats = jnp.where(lane == NEAR_LANE, near, jnp.where(lane == FAR_LANE, far, stats))
        qk = jnp.where(lane < FEAT, folded(qs[b]), folded(ks[b]))
        vg = jnp.where(lane < FEAT, folded(vs[b]), folded(gs[b]))
        qk = jnp.where(slot == STAT_SLOT, stats, qk)
        block = jnp.concatenate(
            [qk.reshape(GROUP, SLOTS, 128), vg.reshape(GROUP, SLOTS, 128)], axis=1
        ).astype(BF16)
        pay_ref[0, b * GROUP : (b + 1) * GROUP] = block
        mark = (iota(block.shape, 1) == STAT_SLOT) & (iota(block.shape, 2) == COPY_LANE)
        pay_ref[1, b * GROUP : (b + 1) * GROUP] = jnp.where(mark, jnp.ones((), BF16), block)


def select_call(near, far, q, k, v, g):
    hbm = pl.BlockSpec(memory_space=pltpu.HBM)
    vmem = pl.BlockSpec(memory_space=pltpu.VMEM)
    return pl.pallas_call(
        select_kernel,
        in_specs=[hbm] * 6,
        out_specs=vmem,
        out_shape=pltpu.VMEM((2, HEADS, 2 * SLOTS, 128), BF16),
        scratch_shapes=OFFSET_SCRATCH
        + [pltpu.VMEM((4, ROWS, WIDTH), BF16), pltpu.SemaphoreType.DMA((4,))],
        compiler_params=pltpu.CompilerParams(vmem_limit_bytes=VMEM_BYTES),
        name="select_rows",
    )(*pinned(pltpu.HBM, near, far, q, k, v, g))


def local_head(head, here, near_ref, far_ref, q, k, v, g):
    half = ROWS // 2
    query = iota((1, ROWS), 1)
    zero = jnp.zeros((), BF16)
    special = (query % NEAR_RATE == near_ref[head]) | (query == far_ref[head])
    kh, vh, qh, gh = (jnp.where(here, x, zero) for x in (k, v, q, g))
    triangle = iota((half, half), 0) <= iota((half, half), 1)
    top, bottom = dot_nt(kh[:half], q), dot_nt(kh[half:], q[half:])
    early, late = jnp.where(triangle, top[:, :half], LOW), top[:, half:]
    bottom = jnp.where(triangle, bottom, LOW)
    early_top = jnp.max(early, axis=0, keepdims=True)
    late_top = jnp.maximum(jnp.max(late, axis=0, keepdims=True), jnp.max(bottom, axis=0, keepdims=True))
    early, late, bottom = jnp.exp(early - early_top), jnp.exp(late - late_top), jnp.exp(bottom - late_top)
    early_total = jnp.sum(early, axis=0, keepdims=True)
    late_total = jnp.sum(late, axis=0, keepdims=True) + jnp.sum(bottom, axis=0, keepdims=True)
    scale = jnp.where(special, 0.0, 1.0 / jnp.concatenate([early_total, late_total], axis=1))
    grads, grads_b = dot_nt(vh[:half], g), dot_nt(vh[half:], g[half:])
    top = jnp.concatenate([early, late], axis=1) * scale
    bottom = bottom * scale[:, half:]
    delta = jnp.sum(top * grads, axis=0, keepdims=True)
    late_delta = delta[:, half:] + jnp.sum(bottom * grads_b, axis=0, keepdims=True)
    delta = jnp.concatenate([delta[:, :half], late_delta], axis=1)
    blank = jnp.zeros((half, half), BF16)

    def square(top, bottom):
        bottom = jnp.concatenate([blank, bottom.astype(BF16)], axis=1)
        return jnp.concatenate([top.astype(BF16), bottom], axis=0)

    dscores = square(top * (grads - delta), bottom * (grads_b - late_delta))
    return square(top, bottom), dscores, qh, kh, vh, gh


def joined(heads):
    weights, dscores, q, k, v, g = zip(*heads)
    over_keys = jnp.concatenate(weights, axis=0), jnp.concatenate(dscores, axis=0)
    over_queries = jnp.concatenate(weights, axis=1), jnp.concatenate(dscores, axis=1)
    out = dot_tn(over_keys[0], jnp.concatenate(v, axis=0))
    dq = dot_tn(over_keys[1], jnp.concatenate(k, axis=0)) * SCALE
    dk = dot_nn(over_queries[1], jnp.concatenate(q, axis=0))
    return out, dq, dk, dot_nn(over_queries[0], jnp.concatenate(g, axis=0))


def local_group(near_ref, far_ref, first, q, k, v, g):
    half = ROWS // 2
    query = iota((1, ROWS), 1)
    q = (q.astype(F32) * SCALE).astype(BF16)
    zero = jnp.zeros((), BF16)
    triangle = iota((half, half), 0) <= iota((half, half), 1)
    blank = jnp.zeros((half, half), BF16)
    lane = iota((1, GLANES), 1) // FEAT
    heads = [local_head(first + h, lane == h, near_ref, far_ref, q, k, v, g) for h in range(GROUP)]
    return joined(heads)


def slot_part(i, count=1):
    return slice(i * GSLOTS, (i + count) * GSLOTS)


def local_kernel(
    base, count, near_in, far_in, q_ref, k_ref, v_ref, g_ref, query_ref, key_ref, stat_ref, slot_ref,
    left_ref, near_ref, far_ref, offset_sems, buffer, sems
):
    offset_copies = start_offsets(near_in, far_in, near_ref, far_ref, offset_sems)
    start_copies((q_ref, k_ref, v_ref, g_ref), base, count, buffer, sems)
    for copy in offset_copies:
        copy.wait()
    mask = head_mask()

    def one_group(b, carry):
        here = pl.ds(pl.multiple_of(b * GLANES, GLANES), GLANES)
        for i, source in enumerate((q_ref, k_ref, v_ref, g_ref)):
            there = pl.ds(pl.multiple_of((base + b) * GLANES, GLANES), GLANES)
            pltpu.make_async_copy(source.at[:, there], buffer.at[i, :, here], sems.at[b, i]).wait()
        q, k, v, g = (buffer[i, :, here] for i in range(4))
        first = (base + b) * GROUP
        row, repeat, slot = slot_rows(near_ref, far_ref, first)
        pick = pick_matrix(row)
        qs = jnp.where(mask, dot_nn(pick, q), 0.0)
        gs = jnp.where(mask, dot_nn(pick, g), 0.0)
        live = (slot <= FAR_SLOT) & ~repeat
        scores = dot_nt(qs.astype(BF16), k) * SCALE
        grads = dot_nt(gs.astype(BF16), v)
        lse, d, weights, grads = slot_stats(scores, row, grads, live)
        dscores = (weights * grads).astype(BF16)
        weights = weights.astype(BF16)
        lane = iota((GSLOTS, GLANES), 1)
        near, far = group_offsets(near_ref, far_ref, first)
        key_row = jnp.where(slot >= FAR_SLOT, near + NEAR_RATE * (slot - FAR_SLOT), -1)
        key_pick = pick_matrix(jnp.where(slot == 0, far, key_row))
        left = jnp.concatenate([weights, dscores, pick, key_pick], axis=0)
        left_ref[:, pl.ds(pl.multiple_of(b * TERMS, TERMS), TERMS)] = jnp.transpose(left)
        parts = (
            (qs * SCALE).astype(BF16),
            gs.astype(BF16),
            jnp.where(mask, dot_nn(weights, v), 0.0).astype(BF16),
            (jnp.where(mask, dot_nn(dscores, k), 0.0) * SCALE).astype(BF16),
            (jnp.where(mask, dot_nn(weights, k), 0.0) * SCALE).astype(BF16),
        )
        for i, part in enumerate(parts):
            slot_ref[slot_part(i), here] = part
        stat_ref[:, here] = jnp.where(lane == 0, jnp.where(live, lse, LOW), d)
        out, dq, dk, dv = local_group(near_ref, far_ref, first, q, k, v, g)
        query_ref[0, :, here] = out.astype(BF16)
        query_ref[1, :, here] = dq.astype(BF16)
        key_ref[0, :, here] = dk.astype(key_ref.dtype)
        key_ref[1, :, here] = dv.astype(key_ref.dtype)
        return carry

    lax.fori_loop(0, count, one_group, 0)


def local_call(base, count, near, far, q, k, v, g, key_type):
    hbm = pl.BlockSpec(memory_space=pltpu.HBM)
    vmem = pl.BlockSpec(memory_space=pltpu.VMEM)
    shape = (ROWS, count * GLANES)
    return pl.pallas_call(
        functools.partial(local_kernel, base, count),
        in_specs=[hbm] * 6,
        out_specs=[vmem] * 5,
        out_shape=[
            pltpu.VMEM((2,) + shape, BF16),
            pltpu.VMEM((2,) + shape, key_type),
            pltpu.VMEM((GSLOTS, count * GLANES), F32),
            pltpu.VMEM((SLOT_PARTS * GSLOTS, count * GLANES), BF16),
            pltpu.VMEM((ROWS, count * TERMS), BF16),
        ],
        scratch_shapes=OFFSET_SCRATCH
        + [pltpu.VMEM((4,) + shape, BF16), pltpu.SemaphoreType.DMA((count, 4))],
        compiler_params=pltpu.CompilerParams(vmem_limit_bytes=VMEM_BYTES),
        cost_estimate=pl.CostEstimate(
            flops=count * GROUP * 14 * ROWS * ROWS * FEAT,
            bytes_accessed=count * 7 * ROWS * GLANES * 2,
            transcendentals=count * GROUP * ROWS * ROWS,
        ),
        name="local_level",
    )(*pinned(pltpu.HBM, near, far, q, k, v, g))


def slot_positions(near, far):
    col = iota((SEQ * SLOTS, 1), 0)
    line = iota((1, SEQ * SLOTS), 1)

    def position(index):
        slot = index % SLOTS
        return (SEQ - 1 - index // SLOTS) * ROWS + jnp.where(slot < FAR_SLOT, near + NEAR_RATE * slot, far)

    return col, line, position(col), position(line)


def pair_halves(qk, vg):
    low = iota(qk.shape, 1) < FEAT
    q0 = jnp.where(low, qk, 0.0)
    k0 = jnp.where(low, swap_halves(qk), 0.0)
    g0 = jnp.where(low, swap_halves(vg), 0.0)
    v0 = jnp.where(low, vg, 0.0)
    k1 = jnp.where(low, 0.0, qk)
    g1 = jnp.where(low, 0.0, vg)
    return tuple(x.astype(BF16) for x in (q0, k0, v0, g0, k1, g1))


def read_offsets(got):
    line = got[0, STAT_SLOT : STAT_SLOT + 1, :].astype(jnp.int32)
    return tuple(line[:, at : at + 1] for at in (NEAR_LANE, FAR_LANE, COPY_LANE))


def near_kernel(got_ref, send_ref, stat_ref):
    got = got_ref[...].astype(F32)
    near, far, _ = read_offsets(got)
    qk, vg = got[:, :SLOTS].reshape(SEQ * SLOTS, 128), got[:, SLOTS:].reshape(SEQ * SLOTS, 128)
    lse, d = unpack_stats(got)
    q0, k0, v0, g0, _, _ = pair_halves(qk, vg)
    col, line, col_at, line_at = slot_positions(near, far)
    asks = (col % SLOTS < FAR_SLOT) | ((col % SLOTS == FAR_SLOT) & (far % NEAR_RATE == near))
    allowed = asks & (line % SLOTS < FAR_SLOT) & (line_at <= col_at)
    terms = softmax_terms(dot_nt(q0, k0) * SCALE, allowed, dot_nt(g0, v0))
    lse, d = merge_terms(lse, d, *terms)
    lane = iota((SEQ * SLOTS, 128), 1)
    stats = part_lanes(lse, d, lane)
    stat_ref[...] = stats
    rows = SEQ * SLOTS
    pick = iota((SEQ, rows), 1) == iota((SEQ, rows), 0) * SLOTS + FAR_SLOT
    pick = jnp.where(pick, 1.0, 0.0).astype(BF16)
    qk, vg, stats = (dot_nn(pick, x.astype(BF16)) for x in (qk, vg, stats))
    stats = stats[: SEQ // 2] + swap_halves(stats[SEQ // 2 :])
    block = jnp.concatenate([qk, vg, stats], axis=0).astype(BF16)
    for o in range(OUTER):
        send_ref[o] = block


def near_call(got):
    return pl.pallas_call(
        near_kernel,
        in_specs=[pl.BlockSpec(memory_space=pltpu.VMEM)],
        out_specs=[pl.BlockSpec(memory_space=pltpu.VMEM)] * 2,
        out_shape=[
            pltpu.VMEM((OUTER, 5 * SEQ // 2, 128), BF16),
            pltpu.VMEM((SEQ * SLOTS, 128), F32),
        ],
        compiler_params=pltpu.CompilerParams(vmem_limit_bytes=VMEM_BYTES),
        name="near_forward",
    )(got)


def level_grads(halves, scores, allowed, grads, lse, delta):
    q0, k0, v0, g0, k1, g1 = halves
    weights = jnp.where(allowed, jnp.exp(jnp.where(allowed, scores - lse, 0.0)), 0.0)
    dscores = (weights * (grads - delta)).astype(BF16)
    weights = weights.astype(BF16)
    query_side = dot_nn(weights, v0) + dot_nn(dscores, k1)
    key_side = dot_tn(dscores, q0) + dot_tn(weights, g1)
    low = iota((1, 128), 1) < FEAT
    return query_side * jnp.where(low, 1.0, SCALE), key_side * jnp.where(low, SCALE, 1.0)


def far_order(index):
    return SEQ * OUTER - 1 - index


def owner_kernel(got_ref, stat_ref, far_got_ref, send_ref):
    place = (OUTER - 1 - lax.axis_index("outer")) * SEQ
    got = got_ref[...].astype(F32)
    near, far, copy = read_offsets(got)
    rows = SEQ * SLOTS
    lane = iota((rows, 128), 1)

    far_qk = far_got_ref[:, :SEQ].reshape(rows, 128).astype(F32)
    far_vg = far_got_ref[:, SEQ : 2 * SEQ].reshape(rows, 128).astype(F32)
    far_stats = far_got_ref[:, 2 * SEQ :].astype(F32)
    later = swap_halves(far_stats.reshape(rows // 2, 128)).reshape(far_stats.shape)
    far_stats = jnp.concatenate([far_stats, later], axis=1).reshape(rows, 128)
    far_halves = pair_halves(far_qk, far_vg)
    scores = dot_nt(far_halves[0], far_halves[1]) * SCALE
    grads = dot_nt(far_halves[3], far_halves[2])
    ask, key = far_order(iota((rows, rows), 0)), far_order(iota((rows, rows), 1))
    allowed = key <= ask
    top, total, grad_total = softmax_terms(scores, allowed, grads)
    lse, delta = merge_terms(*read_parts(far_stats, lane), top, total, grad_total)
    query_side, key_side = level_grads(far_halves, scores, allowed, grads, lse, delta)
    own_stats = part_lanes(top + jnp.log(total), grad_total / total, lane).astype(BF16)

    row, column = iota((rows, rows), 0), iota((rows, rows), 1)
    own = column == place + row // SLOTS
    to_far = jnp.where(own & (row % SLOTS == FAR_SLOT), 1.0, 0.0).astype(BF16)
    to_all = jnp.where(own, 1.0, 0.0).astype(BF16)
    first = dot_nn(to_far, query_side.astype(BF16))
    second = dot_nn(to_far, key_side.astype(BF16))
    far_lse, far_d = read_parts(dot_nn(to_all, own_stats), lane)

    col, line, col_at, line_at = slot_positions(near, far)
    slot = col % SLOTS
    active = (slot == FAR_SLOT) | ((slot < FAR_SLOT) & (near + NEAR_RATE * slot == far))
    lse, d = read_parts(stat_ref[...], lane)
    merged_lse, merged_d = merge_terms(lse, d, far_lse, 1.0, far_d)
    lse, delta = jnp.where(active, merged_lse, lse), jnp.where(active, merged_d, d)

    halves = pair_halves(got[:, :SLOTS].reshape(rows, 128), got[:, SLOTS:].reshape(rows, 128))
    allowed = (slot < FAR_SLOT) & (line % SLOTS < FAR_SLOT) & (line_at <= col_at)
    query_side, key_side = level_grads(
        halves, dot_nt(halves[0], halves[1]) * SCALE, allowed, dot_nt(halves[3], halves[2]), lse, delta
    )
    first += query_side
    second += key_side
    used = slot <= FAR_SLOT
    stats = pack_stats(jnp.where(used, lse, 0.0), jnp.where(used, delta, 0.0))
    near_block = jnp.where(slot < FAR_SLOT, first, pltpu.roll(second, FAR_SLOT, 0))
    far_block = jnp.where(slot == 0, pltpu.roll(second, rows - FAR_SLOT, 0), stats)
    far_block = jnp.where(slot == FAR_SLOT, first, far_block)
    send_ref[...] = jnp.where(copy == 0, near_block, far_block).astype(BF16)


def owner_call(got, stats, far_got):
    vmem = pl.BlockSpec(memory_space=pltpu.VMEM)
    return pl.pallas_call(
        owner_kernel,
        in_specs=[vmem, vmem, vmem],
        out_specs=vmem,
        out_shape=pltpu.VMEM((SEQ * SLOTS, 128), BF16),
        compiler_params=pltpu.CompilerParams(vmem_limit_bytes=VMEM_BYTES),
        name="owner_level",
    )(got, stats, far_got)


def finish_kernel(got_ref, *refs):
    halves, outs, (results, out_sems) = (refs[:5], refs[5:10]), refs[10:14], refs[14:]
    mask = head_mask()
    low = iota((GSLOTS, 128), 1) < FEAT
    slot = iota((GSLOTS, 128), 0) % SLOTS
    zero = jnp.zeros((GSLOTS, GLANES), F32)
    sends = []

    def finished(i, b, value):
        results[i, :, b * GLANES : (b + 1) * GLANES] = value.astype(BF16)

    def send(arrays, first, count):
        here = slice(first * GLANES, (first + count) * GLANES)
        for i in arrays:
            copy = pltpu.make_async_copy(
                results.at[i, :, here], outs[i].at[:, here], out_sems.at[first, i]
            )
            copy.start()
            sends.append(copy)

    def spread(x):
        swapped = swap_halves(x)
        for half in (jnp.where(low, x, swapped), jnp.where(low, swapped, x)):
            yield jnp.where(mask, jnp.concatenate([half, half], axis=1), 0.0)

    for b in range(GROUPS):
        half, at = (0, b) if b < EARLY else (1, b - EARLY)
        there = slice(at * GLANES, (at + 1) * GLANES)
        query_part, key_part, stat_ref, slot_ref, left_ref = halves[half]
        near = got_ref[b * GSLOTS : (b + 1) * GSLOTS].astype(F32)
        far = got_ref[HEADS * SLOTS + b * GSLOTS : HEADS * SLOTS + (b + 1) * GSLOTS].astype(F32)
        lse, delta = unpack_stats(far.reshape(GROUP, SLOTS, 128), 2)
        query_side = tuple(spread(jnp.where(slot < FAR_SLOT, near, far)))
        key_side = tuple(spread(jnp.where(slot < FAR_SLOT, far, near)))
        qs, gs, out, dq, mean = (slot_ref[slot_part(i), there].astype(F32) for i in range(5))
        stats = stat_ref[:, there]
        factor = jnp.exp(stats[:, :1] - lse)
        shift = factor * (stats[:, 1:2] - delta)
        out = factor * out + query_side[0]
        dq = factor * dq + shift * mean + query_side[1]
        right = (
            (zero, zero, shift * qs, factor * gs),
            (zero, zero, factor * qs, zero),
            (out, dq, zero, zero),
            (zero, zero) + key_side,
        )
        right = jnp.concatenate([jnp.concatenate(x, axis=1) for x in right], axis=0)
        sums = dot_nn(left_ref[:, at * TERMS : (at + 1) * TERMS], right.astype(BF16))
        if b:
            send((0, 1, 2, 3), b - 1, 1)
        for i in range(4):
            bulk = (query_part if i < 2 else key_part)[i % 2, :, there].astype(F32)
            finished(i, b, bulk + sums[:, i * GLANES : (i + 1) * GLANES])
    send((0, 1, 2, 3), 3, 1)
    for copy in sends:
        copy.wait()


def finish_call(got, parts):
    hbm = pl.BlockSpec(memory_space=pltpu.HBM)
    vmem = pl.BlockSpec(memory_space=pltpu.VMEM)
    return pl.pallas_call(
        finish_kernel,
        in_specs=[vmem] * 11,
        out_specs=[hbm] * 4,
        out_shape=[jax.ShapeDtypeStruct((ROWS, WIDTH), BF16)] * 4,
        scratch_shapes=[
            pltpu.VMEM((4, ROWS, WIDTH), BF16),
            pltpu.SemaphoreType.DMA((GROUPS, 4)),
        ],
        compiler_params=pltpu.CompilerParams(vmem_limit_bytes=VMEM_BYTES),
        name="finish_rows",
    )(got, *parts)


def exchange(x, axis, groups=None):
    return lax.all_to_all(
        x, axis, split_axis=0, concat_axis=0, axis_index_groups=groups, tiled=True
    )


def on_device(queries, keys, values, out_grad, near_offsets, far_offsets):
    arrays = (queries, keys, values, out_grad)
    pay = select_call(near_offsets, far_offsets, *arrays)
    got = exchange(pay.reshape(SEQ, 2 * SLOTS, 128), "seq", BACKWARDS)
    (near_1, far_1), _ = lax.optimization_barrier(((near_offsets, far_offsets), pay))
    parts = local_call(0, EARLY, near_1, far_1, *arrays, BF16)
    got, parts = lax.optimization_barrier((got, parts))
    far_pay, stats = near_call(got)
    far_got = exchange(far_pay, "outer", [list(range(OUTER - 1, -1, -1))])
    back = owner_call(got, stats, far_got)
    (near_2, far_2), back = lax.optimization_barrier(((near_offsets, far_offsets), back))
    back_got = exchange(back, "seq", BACKWARDS)
    parts += local_call(EARLY, GROUPS - EARLY, near_2, far_2, *arrays, F32)
    return finish_call(back_got, parts)


def solution(mesh):
    split = P(("outer", "seq"), None)
    return jax.shard_map(
        on_device,
        mesh=mesh,
        in_specs=(split, split, split, split, P(), P()),
        out_specs=(split, split, split, split),
        check_vma=False,
    )
```

```python
import functools

import jax
import jax.numpy as jnp
from jax import lax
from jax.experimental import pallas as pl
from jax.experimental.pallas import tpu as pltpu
from jax.sharding import PartitionSpec as P

HEADS = 16
FEAT = 64
ROWS = 256
WIDTH = 1024
NEAR_RATE = 64
FAR_RATE = 256
SEQ = 32
OUTER = 8
SLOTS = 8
FAR_SLOT = 4
STAT_SLOT = 5
NEAR_LANE = 48
FAR_LANE = 49
COPY_LANE = 50
GROUP = 4
GROUPS = HEADS // GROUP
EARLY = 2
GLANES = GROUP * FEAT
GSLOTS = GROUP * SLOTS
SCALE = FEAT**-0.5
LOW = -1e30
BACKWARDS = [list(range(SEQ - 1, -1, -1))]
SLOT_PARTS = 5
TERMS = 4 * GSLOTS
F32 = jnp.float32
BF16 = jnp.bfloat16
VMEM_BYTES = 24 * 1024 * 1024


def pinned(space, *arrays):
    return tuple(pltpu.with_memory_space_constraint(x, space) for x in arrays)


def iota(shape, axis):
    return lax.broadcasted_iota(jnp.int32, shape, axis)


def dot_nn(a, b):
    return lax.dot_general(a, b, (((1,), (0,)), ((), ())), preferred_element_type=F32)


def dot_nt(a, b):
    return lax.dot_general(a, b, (((1,), (1,)), ((), ())), preferred_element_type=F32)


def dot_tn(a, b):
    return lax.dot_general(a, b, (((0,), (0,)), ((), ())), preferred_element_type=F32)


def parts_of(value):
    high = value.astype(BF16).astype(F32)
    rest = value - high
    middle = rest.astype(BF16).astype(F32)
    return high, middle, rest - middle


def part_lanes(lse, d, at):
    out = jnp.zeros((lse.shape[0], at.shape[1]), F32)
    for index, part in enumerate(parts_of(lse) + parts_of(d)):
        out = jnp.where(at == index, part, out)
    return out


def read_parts(lanes, at):
    lse = jnp.sum(jnp.where((at >= 0) & (at < 3), lanes, 0.0), axis=1, keepdims=True)
    d = jnp.sum(jnp.where((at >= 3) & (at < 6), lanes, 0.0), axis=1, keepdims=True)
    return lse, d


def read_wide(lanes, at):
    part = iota((128, 256), 0) % 8
    ones = jnp.where(part // 3 == iota((128, 256), 1) // 128, 1.0, 0.0).astype(BF16)
    both = dot_nn(jnp.where((at >= 0) & (at < 6), lanes, 0.0).astype(BF16), ones)
    return both[:, :128], both[:, 128:]


def pack_stats(lse, d):
    rows = lse.shape[0]
    row, lane = iota((rows, 128), 0), iota((rows, 128), 1)
    at = jnp.where(lane // 8 == row % SLOTS, lane % 8, -1)
    spread = part_lanes(lse, d, at).reshape(rows // SLOTS, SLOTS, 128)
    total = jnp.sum(spread, axis=1, keepdims=True)
    return jnp.broadcast_to(total, spread.shape).reshape(rows, 128)


def unpack_stats(block, at=STAT_SLOT, read=read_parts):
    lanes = jnp.broadcast_to(block[:, at : at + 1, :], (block.shape[0], SLOTS, 128))
    lanes = lanes.reshape(block.shape[0] * SLOTS, 128)
    row, lane = iota(lanes.shape, 0), iota(lanes.shape, 1)
    return read(lanes, jnp.where(lane // 8 == row % SLOTS, lane % 8, -1))


def swap_halves(x):
    return pltpu.roll(x, FEAT, 1)


def group_offsets(near_ref, far_ref, first):
    index = iota((GSLOTS, 1), 0)
    near = jnp.zeros((GSLOTS, 1), jnp.int32)
    far = jnp.zeros((GSLOTS, 1), jnp.int32)
    for h in range(GROUP):
        here = index // SLOTS == h
        near = jnp.where(here, near_ref[first + h], near)
        far = jnp.where(here, far_ref[first + h], far)
    return near, far


def slot_rows(near_ref, far_ref, first):
    near, far = group_offsets(near_ref, far_ref, first)
    slot = iota((GSLOTS, 1), 0) % SLOTS
    row = jnp.where(slot < FAR_SLOT, near + NEAR_RATE * slot, jnp.where(slot == FAR_SLOT, far, -1))
    repeat = (slot == FAR_SLOT) & (far % NEAR_RATE == near)
    return row, repeat, slot


def head_mask():
    return iota((GSLOTS, GLANES), 1) // FEAT == iota((GSLOTS, GLANES), 0) // SLOTS


def softmax_terms(scores, allowed, weight_grads):
    masked = jnp.where(allowed, scores, LOW)
    top = jnp.max(masked, axis=1, keepdims=True)
    weights = jnp.where(allowed, jnp.exp(masked - top), 0.0)
    total = jnp.sum(weights, axis=1, keepdims=True)
    return top, total, jnp.sum(weights * weight_grads, axis=1, keepdims=True)


def merge_terms(lse, d, top, total, grad_total):
    overall = jnp.maximum(lse, top)
    old, new = jnp.exp(lse - overall), jnp.exp(top - overall)
    mass = old + new * total
    return overall + jnp.log(mass), (old * d + new * grad_total) / mass


OFFSET_SCRATCH = [
    pltpu.SMEM((HEADS,), jnp.int32),
    pltpu.SMEM((HEADS,), jnp.int32),
    pltpu.SemaphoreType.DMA((2,)),
]


def start_offsets(near_in, far_in, near_ref, far_ref, sems):
    copies = [
        pltpu.make_async_copy(near_in, near_ref, sems.at[0]),
        pltpu.make_async_copy(far_in, far_ref, sems.at[1]),
    ]
    for copy in copies:
        copy.start()
    return copies


def pick_matrix(row):
    return jnp.where(iota((GSLOTS, ROWS), 1) == row, 1.0, 0.0).astype(BF16)


def slot_stats(scores, row, grads, live):
    allowed = iota((GSLOTS, ROWS), 1) <= row
    masked = jnp.where(allowed, scores, LOW)
    top = jnp.max(masked, axis=1, keepdims=True)
    weights = jnp.where(allowed & live, jnp.exp(masked - top), 0.0)
    total = jnp.where(live, jnp.sum(weights, axis=1, keepdims=True), 1.0)
    scale = 1.0 / total
    d = jnp.sum(weights * grads, axis=1, keepdims=True) * scale
    return jnp.where(live, top + jnp.log(total), 0.0), d, weights * scale, grads - d


def start_copies(sources, base, count, buffer, sems):
    copies = []
    for b in range(count):
        here = pl.ds(b * GLANES, GLANES)
        there = pl.ds((base + b) * GLANES, GLANES)
        copies.append(
            [
                pltpu.make_async_copy(source.at[:, there], buffer.at[i, :, here], sems.at[b, i])
                for i, source in enumerate(sources)
            ]
        )
    for group in copies:
        for copy in group:
            copy.start()
    return copies


def start_whole(sources, buffer, sems):
    copies = [
        pltpu.make_async_copy(source, buffer.at[i], sems.at[i]) for i, source in enumerate(sources)
    ]
    for copy in copies:
        copy.start()
    return copies


def select_kernel(
    near_in, far_in, q_ref, k_ref, v_ref, g_ref, pay_ref, near_ref, far_ref, offset_sems, buffer, sems
):
    offset_copies = start_offsets(near_in, far_in, near_ref, far_ref, offset_sems)
    copies = start_whole((q_ref, g_ref, k_ref, v_ref), buffer, sems)
    for copy in offset_copies:
        copy.wait()
    groups = range(GROUPS)
    rows = [slot_rows(near_ref, far_ref, b * GROUP)[0] for b in groups]
    picks = [pick_matrix(row) for row in rows]
    mask = head_mask()
    lane = iota((GSLOTS, 128), 1)
    slot = iota((GSLOTS, 1), 0) % SLOTS

    def columns(i, b):
        return buffer[i, :, b * GLANES : (b + 1) * GLANES]

    def selected(i):
        copies[i].wait()
        return [jnp.where(mask, dot_nn(picks[b], columns(i, b)), 0.0) for b in groups]

    def folded(x):
        x = x[:, :128] + x[:, 128:]
        return x + swap_halves(x)

    qs, gs, ks = selected(0), selected(1), selected(2)
    scores = [dot_nt(qs[b].astype(BF16), columns(2, b)) * SCALE for b in groups]
    vs = selected(3)
    grads = [dot_nt(gs[b].astype(BF16), columns(3, b)) for b in groups]
    for b in groups:
        lse, d, _, _ = slot_stats(scores[b], rows[b], grads[b], slot <= FAR_SLOT)
        stats = pack_stats(lse, d)
        near, far = group_offsets(near_ref, far_ref, b * GROUP)
        stats = jnp.where(lane == NEAR_LANE, near, jnp.where(lane == FAR_LANE, far, stats))
        qk = jnp.where(lane < FEAT, folded(qs[b]), folded(ks[b]))
        vg = jnp.where(lane < FEAT, folded(vs[b]), folded(gs[b]))
        qk = jnp.where(slot == STAT_SLOT, stats, qk)
        block = jnp.concatenate(
            [qk.reshape(GROUP, SLOTS, 128), vg.reshape(GROUP, SLOTS, 128)], axis=1
        ).astype(BF16)
        pay_ref[0, b * GROUP : (b + 1) * GROUP] = block
        mark = (iota(block.shape, 1) == STAT_SLOT) & (iota(block.shape, 2) == COPY_LANE)
        pay_ref[1, b * GROUP : (b + 1) * GROUP] = jnp.where(mark, jnp.ones((), BF16), block)


def select_call(near, far, q, k, v, g):
    hbm = pl.BlockSpec(memory_space=pltpu.HBM)
    vmem = pl.BlockSpec(memory_space=pltpu.VMEM)
    return pl.pallas_call(
        select_kernel,
        in_specs=[hbm] * 6,
        out_specs=vmem,
        out_shape=pltpu.VMEM((2, HEADS, 2 * SLOTS, 128), BF16),
        scratch_shapes=OFFSET_SCRATCH
        + [pltpu.VMEM((4, ROWS, WIDTH), BF16), pltpu.SemaphoreType.DMA((4,))],
        compiler_params=pltpu.CompilerParams(vmem_limit_bytes=VMEM_BYTES),
        name="select_rows",
    )(*pinned(pltpu.HBM, near, far, q, k, v, g))


def local_head(head, here, near_ref, far_ref, q, k, v, g):
    half = ROWS // 2
    query = iota((1, ROWS), 1)
    zero = jnp.zeros((), BF16)
    special = (query % NEAR_RATE == near_ref[head]) | (query == far_ref[head])
    kh, vh, qh, gh = (jnp.where(here, x, zero) for x in (k, v, q, g))
    triangle = iota((half, half), 0) <= iota((half, half), 1)
    top, bottom = dot_nt(kh[:half], q), dot_nt(kh[half:], q[half:])
    early, late = jnp.where(triangle, top[:, :half], LOW), top[:, half:]
    bottom = jnp.where(triangle, bottom, LOW)
    early_top = jnp.max(early, axis=0, keepdims=True)
    late_top = jnp.maximum(jnp.max(late, axis=0, keepdims=True), jnp.max(bottom, axis=0, keepdims=True))
    early, late, bottom = jnp.exp(early - early_top), jnp.exp(late - late_top), jnp.exp(bottom - late_top)
    early_total = jnp.sum(early, axis=0, keepdims=True)
    late_total = jnp.sum(late, axis=0, keepdims=True) + jnp.sum(bottom, axis=0, keepdims=True)
    scale = jnp.where(special, 0.0, 1.0 / jnp.concatenate([early_total, late_total], axis=1))
    grads, grads_b = dot_nt(vh[:half], g), dot_nt(vh[half:], g[half:])
    top = jnp.concatenate([early, late], axis=1) * scale
    bottom = bottom * scale[:, half:]
    delta = jnp.sum(top * grads, axis=0, keepdims=True)
    late_delta = delta[:, half:] + jnp.sum(bottom * grads_b, axis=0, keepdims=True)
    delta = jnp.concatenate([delta[:, :half], late_delta], axis=1)
    blank = jnp.zeros((half, half), BF16)

    def square(top, bottom):
        bottom = jnp.concatenate([blank, bottom.astype(BF16)], axis=1)
        return jnp.concatenate([top.astype(BF16), bottom], axis=0)

    dscores = square(top * (grads - delta), bottom * (grads_b - late_delta))
    return square(top, bottom), dscores, qh, kh, vh, gh


def joined(heads):
    weights, dscores, q, k, v, g = zip(*heads)
    over_keys = jnp.concatenate(weights, axis=0), jnp.concatenate(dscores, axis=0)
    over_queries = jnp.concatenate(weights, axis=1), jnp.concatenate(dscores, axis=1)
    out = dot_tn(over_keys[0], jnp.concatenate(v, axis=0))
    dq = dot_tn(over_keys[1], jnp.concatenate(k, axis=0)) * SCALE
    dk = dot_nn(over_queries[1], jnp.concatenate(q, axis=0))
    return out, dq, dk, dot_nn(over_queries[0], jnp.concatenate(g, axis=0))


def local_group(near_ref, far_ref, first, q, k, v, g):
    half = ROWS // 2
    query = iota((1, ROWS), 1)
    q = (q.astype(F32) * SCALE).astype(BF16)
    zero = jnp.zeros((), BF16)
    triangle = iota((half, half), 0) <= iota((half, half), 1)
    blank = jnp.zeros((half, half), BF16)
    lane = iota((1, GLANES), 1) // FEAT
    heads = [local_head(first + h, lane == h, near_ref, far_ref, q, k, v, g) for h in range(GROUP)]
    return joined(heads)


def slot_part(i, count=1):
    return slice(i * GSLOTS, (i + count) * GSLOTS)


def local_kernel(
    base, count, near_in, far_in, q_ref, k_ref, v_ref, g_ref, query_ref, key_ref, stat_ref, slot_ref,
    left_ref, near_ref, far_ref, offset_sems, buffer, sems
):
    offset_copies = start_offsets(near_in, far_in, near_ref, far_ref, offset_sems)
    start_copies((q_ref, k_ref, v_ref, g_ref), base, count, buffer, sems)
    for copy in offset_copies:
        copy.wait()
    mask = head_mask()

    def one_group(b, carry):
        here = pl.ds(pl.multiple_of(b * GLANES, GLANES), GLANES)
        for i, source in enumerate((q_ref, k_ref, v_ref, g_ref)):
            there = pl.ds(pl.multiple_of((base + b) * GLANES, GLANES), GLANES)
            pltpu.make_async_copy(source.at[:, there], buffer.at[i, :, here], sems.at[b, i]).wait()
        q, k, v, g = (buffer[i, :, here] for i in range(4))
        first = (base + b) * GROUP
        row, repeat, slot = slot_rows(near_ref, far_ref, first)
        pick = pick_matrix(row)
        qs = jnp.where(mask, dot_nn(pick, q), 0.0)
        gs = jnp.where(mask, dot_nn(pick, g), 0.0)
        live = (slot <= FAR_SLOT) & ~repeat
        scores = dot_nt(qs.astype(BF16), k) * SCALE
        grads = dot_nt(gs.astype(BF16), v)
        lse, d, weights, grads = slot_stats(scores, row, grads, live)
        dscores = (weights * grads).astype(BF16)
        weights = weights.astype(BF16)
        lane = iota((GSLOTS, GLANES), 1)
        near, far = group_offsets(near_ref, far_ref, first)
        key_row = jnp.where(slot >= FAR_SLOT, near + NEAR_RATE * (slot - FAR_SLOT), -1)
        key_pick = pick_matrix(jnp.where(slot == 0, far, key_row))
        left = jnp.concatenate([weights, dscores, pick, key_pick], axis=0)
        left_ref[:, pl.ds(pl.multiple_of(b * TERMS, TERMS), TERMS)] = jnp.transpose(left)
        parts = (
            (qs * SCALE).astype(BF16),
            gs.astype(BF16),
            jnp.where(mask, dot_nn(weights, v), 0.0).astype(BF16),
            (jnp.where(mask, dot_nn(dscores, k), 0.0) * SCALE).astype(BF16),
            (jnp.where(mask, dot_nn(weights, k), 0.0) * SCALE).astype(BF16),
        )
        for i, part in enumerate(parts):
            slot_ref[slot_part(i), here] = part
        stat_ref[:, here] = jnp.where(lane == 0, jnp.where(live, lse, LOW), d)
        out, dq, dk, dv = local_group(near_ref, far_ref, first, q, k, v, g)
        query_ref[0, :, here] = out.astype(BF16)
        query_ref[1, :, here] = dq.astype(BF16)
        key_ref[0, :, here] = dk.astype(key_ref.dtype)
        key_ref[1, :, here] = dv.astype(key_ref.dtype)
        return carry

    lax.fori_loop(0, count, one_group, 0)


def local_call(base, count, near, far, q, k, v, g, key_type):
    hbm = pl.BlockSpec(memory_space=pltpu.HBM)
    vmem = pl.BlockSpec(memory_space=pltpu.VMEM)
    shape = (ROWS, count * GLANES)
    return pl.pallas_call(
        functools.partial(local_kernel, base, count),
        in_specs=[hbm] * 6,
        out_specs=[vmem] * 5,
        out_shape=[
            pltpu.VMEM((2,) + shape, BF16),
            pltpu.VMEM((2,) + shape, key_type),
            pltpu.VMEM((GSLOTS, count * GLANES), F32),
            pltpu.VMEM((SLOT_PARTS * GSLOTS, count * GLANES), BF16),
            pltpu.VMEM((ROWS, count * TERMS), BF16),
        ],
        scratch_shapes=OFFSET_SCRATCH
        + [pltpu.VMEM((4,) + shape, BF16), pltpu.SemaphoreType.DMA((count, 4))],
        compiler_params=pltpu.CompilerParams(vmem_limit_bytes=VMEM_BYTES),
        cost_estimate=pl.CostEstimate(
            flops=count * GROUP * 14 * ROWS * ROWS * FEAT,
            bytes_accessed=count * 7 * ROWS * GLANES * 2,
            transcendentals=count * GROUP * ROWS * ROWS,
        ),
        name="local_level",
    )(*pinned(pltpu.HBM, near, far, q, k, v, g))


def slot_positions(near, far):
    col = iota((SEQ * SLOTS, 1), 0)
    line = iota((1, SEQ * SLOTS), 1)

    def position(index):
        slot = index % SLOTS
        return (SEQ - 1 - index // SLOTS) * ROWS + jnp.where(slot < FAR_SLOT, near + NEAR_RATE * slot, far)

    return col, line, position(col), position(line)


def pair_halves(qk, vg):
    low = iota(qk.shape, 1) < FEAT
    q0 = jnp.where(low, qk, 0.0)
    k0 = jnp.where(low, swap_halves(qk), 0.0)
    g0 = jnp.where(low, swap_halves(vg), 0.0)
    v0 = jnp.where(low, vg, 0.0)
    k1 = jnp.where(low, 0.0, qk)
    g1 = jnp.where(low, 0.0, vg)
    return tuple(x.astype(BF16) for x in (q0, k0, v0, g0, k1, g1))


def read_offsets(got):
    line = got[0, STAT_SLOT : STAT_SLOT + 1, :].astype(jnp.int32)
    return tuple(line[:, at : at + 1] for at in (NEAR_LANE, FAR_LANE, COPY_LANE))


def near_kernel(got_ref, send_ref, stat_ref):
    got = got_ref[...].astype(F32)
    near, far, _ = read_offsets(got)
    qk, vg = got[:, :SLOTS].reshape(SEQ * SLOTS, 128), got[:, SLOTS:].reshape(SEQ * SLOTS, 128)
    lse, d = unpack_stats(got, read=read_wide)
    q0, k0, v0, g0, _, _ = pair_halves(qk, vg)
    col, line, col_at, line_at = slot_positions(near, far)
    asks = (col % SLOTS < FAR_SLOT) | ((col % SLOTS == FAR_SLOT) & (far % NEAR_RATE == near))
    allowed = asks & (line % SLOTS < FAR_SLOT) & (line_at <= col_at)
    terms = softmax_terms(dot_nt(q0, k0) * SCALE, allowed, dot_nt(g0, v0))
    lse, d = merge_terms(lse, d, *terms)
    lane = iota((SEQ * SLOTS, 128), 1)
    stats = part_lanes(lse, d, lane)
    stat_ref[...] = stats
    rows = SEQ * SLOTS
    pick = iota((SEQ, rows), 1) == iota((SEQ, rows), 0) * SLOTS + FAR_SLOT
    pick = jnp.where(pick, 1.0, 0.0).astype(BF16)
    qk, vg, stats = (dot_nn(pick, x.astype(BF16)) for x in (qk, vg, stats))
    stats = stats[: SEQ // 2] + swap_halves(stats[SEQ // 2 :])
    block = jnp.concatenate([qk, vg, stats], axis=0).astype(BF16)
    for o in range(OUTER):
        send_ref[o] = block


def near_call(got):
    return pl.pallas_call(
        near_kernel,
        in_specs=[pl.BlockSpec(memory_space=pltpu.VMEM)],
        out_specs=[pl.BlockSpec(memory_space=pltpu.VMEM)] * 2,
        out_shape=[
            pltpu.VMEM((OUTER, 5 * SEQ // 2, 128), BF16),
            pltpu.VMEM((SEQ * SLOTS, 128), F32),
        ],
        compiler_params=pltpu.CompilerParams(vmem_limit_bytes=VMEM_BYTES),
        name="near_forward",
    )(got)


def level_grads(halves, scores, allowed, grads, lse, delta):
    q0, k0, v0, g0, k1, g1 = halves
    weights = jnp.where(allowed, jnp.exp(jnp.where(allowed, scores - lse, 0.0)), 0.0)
    dscores = (weights * (grads - delta)).astype(BF16)
    weights = weights.astype(BF16)
    query_side = dot_nn(weights, v0) + dot_nn(dscores, k1)
    key_side = dot_tn(dscores, q0) + dot_tn(weights, g1)
    low = iota((1, 128), 1) < FEAT
    return query_side * jnp.where(low, 1.0, SCALE), key_side * jnp.where(low, SCALE, 1.0)


def far_order(index):
    return SEQ * OUTER - 1 - index


def owner_kernel(got_ref, stat_ref, far_got_ref, send_ref):
    place = (OUTER - 1 - lax.axis_index("outer")) * SEQ
    got = got_ref[...].astype(F32)
    near, far, copy = read_offsets(got)
    rows = SEQ * SLOTS
    lane = iota((rows, 128), 1)

    far_qk = far_got_ref[:, :SEQ].reshape(rows, 128).astype(F32)
    far_vg = far_got_ref[:, SEQ : 2 * SEQ].reshape(rows, 128).astype(F32)
    far_stats = far_got_ref[:, 2 * SEQ :].astype(F32)
    later = swap_halves(far_stats.reshape(rows // 2, 128)).reshape(far_stats.shape)
    far_stats = jnp.concatenate([far_stats, later], axis=1).reshape(rows, 128)
    far_halves = pair_halves(far_qk, far_vg)
    scores = dot_nt(far_halves[0], far_halves[1]) * SCALE
    grads = dot_nt(far_halves[3], far_halves[2])
    ask, key = far_order(iota((rows, rows), 0)), far_order(iota((rows, rows), 1))
    allowed = key <= ask
    top, total, grad_total = softmax_terms(scores, allowed, grads)
    lse, delta = merge_terms(*read_parts(far_stats, lane), top, total, grad_total)
    query_side, key_side = level_grads(far_halves, scores, allowed, grads, lse, delta)
    own_stats = part_lanes(top + jnp.log(total), grad_total / total, lane).astype(BF16)

    row, column = iota((rows, rows), 0), iota((rows, rows), 1)
    own = column == place + row // SLOTS
    to_far = jnp.where(own & (row % SLOTS == FAR_SLOT), 1.0, 0.0).astype(BF16)
    to_all = jnp.where(own, 1.0, 0.0).astype(BF16)
    first = dot_nn(to_far, query_side.astype(BF16))
    second = dot_nn(to_far, key_side.astype(BF16))
    far_lse, far_d = read_parts(dot_nn(to_all, own_stats), lane)

    col, line, col_at, line_at = slot_positions(near, far)
    slot = col % SLOTS
    active = (slot == FAR_SLOT) | ((slot < FAR_SLOT) & (near + NEAR_RATE * slot == far))
    lse, d = read_parts(stat_ref[...], lane)
    merged_lse, merged_d = merge_terms(lse, d, far_lse, 1.0, far_d)
    lse, delta = jnp.where(active, merged_lse, lse), jnp.where(active, merged_d, d)

    halves = pair_halves(got[:, :SLOTS].reshape(rows, 128), got[:, SLOTS:].reshape(rows, 128))
    allowed = (slot < FAR_SLOT) & (line % SLOTS < FAR_SLOT) & (line_at <= col_at)
    query_side, key_side = level_grads(
        halves, dot_nt(halves[0], halves[1]) * SCALE, allowed, dot_nt(halves[3], halves[2]), lse, delta
    )
    first += query_side
    second += key_side
    used = slot <= FAR_SLOT
    stats = pack_stats(jnp.where(used, lse, 0.0), jnp.where(used, delta, 0.0))
    near_block = jnp.where(slot < FAR_SLOT, first, pltpu.roll(second, FAR_SLOT, 0))
    far_block = jnp.where(slot == 0, pltpu.roll(second, rows - FAR_SLOT, 0), stats)
    far_block = jnp.where(slot == FAR_SLOT, first, far_block)
    send_ref[...] = jnp.where(copy == 0, near_block, far_block).astype(BF16)


def owner_call(got, stats, far_got):
    vmem = pl.BlockSpec(memory_space=pltpu.VMEM)
    return pl.pallas_call(
        owner_kernel,
        in_specs=[vmem, vmem, vmem],
        out_specs=vmem,
        out_shape=pltpu.VMEM((SEQ * SLOTS, 128), BF16),
        compiler_params=pltpu.CompilerParams(vmem_limit_bytes=VMEM_BYTES),
        name="owner_level",
    )(got, stats, far_got)


def finish_kernel(got_ref, *refs):
    halves, outs, (results, out_sems) = (refs[:5], refs[5:10]), refs[10:14], refs[14:]
    mask = head_mask()
    low = iota((GSLOTS, 128), 1) < FEAT
    slot = iota((GSLOTS, 128), 0) % SLOTS
    zero = jnp.zeros((GSLOTS, GLANES), F32)
    sends = []

    def finished(i, b, value):
        results[i, :, b * GLANES : (b + 1) * GLANES] = value.astype(BF16)

    def send(arrays, first, count):
        here = slice(first * GLANES, (first + count) * GLANES)
        for i in arrays:
            copy = pltpu.make_async_copy(
                results.at[i, :, here], outs[i].at[:, here], out_sems.at[first, i]
            )
            copy.start()
            sends.append(copy)

    def spread(x):
        swapped = swap_halves(x)
        for half in (jnp.where(low, x, swapped), jnp.where(low, swapped, x)):
            yield jnp.where(mask, jnp.concatenate([half, half], axis=1), 0.0)

    for b in range(GROUPS):
        half, at = (0, b) if b < EARLY else (1, b - EARLY)
        there = slice(at * GLANES, (at + 1) * GLANES)
        query_part, key_part, stat_ref, slot_ref, left_ref = halves[half]
        near = got_ref[b * GSLOTS : (b + 1) * GSLOTS].astype(F32)
        far = got_ref[HEADS * SLOTS + b * GSLOTS : HEADS * SLOTS + (b + 1) * GSLOTS].astype(F32)
        lse, delta = unpack_stats(far.reshape(GROUP, SLOTS, 128), 2)
        query_side = tuple(spread(jnp.where(slot < FAR_SLOT, near, far)))
        key_side = tuple(spread(jnp.where(slot < FAR_SLOT, far, near)))
        qs, gs, out, dq, mean = (slot_ref[slot_part(i), there].astype(F32) for i in range(5))
        stats = stat_ref[:, there]
        factor = jnp.exp(stats[:, :1] - lse)
        shift = factor * (stats[:, 1:2] - delta)
        out = factor * out + query_side[0]
        dq = factor * dq + shift * mean + query_side[1]
        right = (
            (zero, zero, shift * qs, factor * gs),
            (zero, zero, factor * qs, zero),
            (out, dq, zero, zero),
            (zero, zero) + key_side,
        )
        right = jnp.concatenate([jnp.concatenate(x, axis=1) for x in right], axis=0)
        sums = dot_nn(left_ref[:, at * TERMS : (at + 1) * TERMS], right.astype(BF16))
        if b:
            send((0, 1, 2, 3), b - 1, 1)
        for i in range(4):
            bulk = (query_part if i < 2 else key_part)[i % 2, :, there].astype(F32)
            finished(i, b, bulk + sums[:, i * GLANES : (i + 1) * GLANES])
    send((0, 1, 2, 3), 3, 1)
    for copy in sends:
        copy.wait()


def finish_call(got, parts):
    hbm = pl.BlockSpec(memory_space=pltpu.HBM)
    vmem = pl.BlockSpec(memory_space=pltpu.VMEM)
    return pl.pallas_call(
        finish_kernel,
        in_specs=[vmem] * 11,
        out_specs=[hbm] * 4,
        out_shape=[jax.ShapeDtypeStruct((ROWS, WIDTH), BF16)] * 4,
        scratch_shapes=[
            pltpu.VMEM((4, ROWS, WIDTH), BF16),
            pltpu.SemaphoreType.DMA((GROUPS, 4)),
        ],
        compiler_params=pltpu.CompilerParams(vmem_limit_bytes=VMEM_BYTES),
        name="finish_rows",
    )(got, *parts)


def exchange(x, axis, groups=None):
    return lax.all_to_all(
        x, axis, split_axis=0, concat_axis=0, axis_index_groups=groups, tiled=True
    )


def on_device(queries, keys, values, out_grad, near_offsets, far_offsets):
    arrays = (queries, keys, values, out_grad)
    pay = select_call(near_offsets, far_offsets, *arrays)
    got = exchange(pay.reshape(SEQ, 2 * SLOTS, 128), "seq", BACKWARDS)
    (near_1, far_1), _ = lax.optimization_barrier(((near_offsets, far_offsets), pay))
    parts = local_call(0, EARLY, near_1, far_1, *arrays, BF16)
    got, parts = lax.optimization_barrier((got, parts))
    far_pay, stats = near_call(got)
    far_got = exchange(far_pay, "outer", [list(range(OUTER - 1, -1, -1))])
    back = owner_call(got, stats, far_got)
    (near_2, far_2), back = lax.optimization_barrier(((near_offsets, far_offsets), back))
    back_got = exchange(back, "seq", BACKWARDS)
    parts += local_call(EARLY, GROUPS - EARLY, near_2, far_2, *arrays, F32)
    return finish_call(back_got, parts)


def solution(mesh):
    split = P(("outer", "seq"), None)
    return jax.shard_map(
        on_device,
        mesh=mesh,
        in_specs=(split, split, split, split, P(), P()),
        out_specs=(split, split, split, split),
        check_vma=False,
    )
```
